512 devices in a mesh: ens: 4 (over y_hi), lat: 8 (over y_lo, x), lon: 16 (over z, core).
Axes of the slice: x: 4, y: 8 (y_hi: 4, y_lo: 2; y = y_hi * 2 + y_lo), z: 8, core: 2. Of those that a mesh axis runs over, the one named last changes fastest.
Arguments:
- initial_state: float32 [24, 128, 2048], P('ens', 'lat', 'lon'), parts along dimension 0, may hold values from -6 to 6
- diffusion: float32 [128, 2048], P('lat', 'lon'), may hold values from 0.05 to 0.2
- mixing: float32 [6, 6], replicated, may hold values from -0.3 to 0.3
- land_mask: int32 [128, 2048], P('lat', 'lon'), may hold values 0 or 1
- first_layer: bfloat16 [128, 54], replicated, may hold values from -0.875 to 0.875
- second_layer: bfloat16 [128, 128], replicated, may hold values from -0.5 to 0.5
- output_layer: bfloat16 [6, 128], replicated, may hold values from -0.5 to 0.5
- cotangent: float32 [24, 128, 2048], P('ens', 'lat', 'lon'), parts along dimension 0, may hold values from -20 to 20
- update_noise: float32 [96256], P('ens'), parts along dimension 0, may hold values from -0.15 to 0.15
Outputs:
- final_state: float32 [24, 128, 2048], P('ens', 'lat', 'lon'), parts along dimension 0
- initial_adjoint: float32 [24, 128, 2048], P('ens', 'lat', 'lon'), parts along dimension 0
- new_params: float32 [96256], P('ens'), parts along dimension 0
- noise_ratio: float32 [4], P('ens'), parts along dimension 0
The draws below stay inside these ranges and needn't reach their ends.
There are 4 independent parts, one for each index of `ens`. The reference program is written for one: setup_inputs(seed, part) draws one part's arguments, and reference() takes and returns one part's arrays. A program takes and returns all parts, laid end to end along the dimension named above; an argument that names none is the same for every part. Nothing has to cross between parts.
All inputs are finite; a program needn't handle non-finite values. No bound on the sum of `land_mask` on one device may be relied on, other than what follows from the above.
Results may differ from the reference program's by a relative error of at most 0.0033.
Values sent between devices are 32-bit elements; how exact they have to be, the bound alone decides.
A program may use at most 64 MiB of HBM per device.

```python
import math
import jax
import jax.numpy as jnp
from jax import lax

CLAT = 16
HID = 128
FIELDS = 6
STEPS = 2
PATCH = 54
PARAMS = 24064
NLAT = 128
NLON = 2048
N_LAT = 8


def draw_cotangent(key, part):
    rows = jnp.arange(NLAT, dtype=jnp.float32)
    ramp = 1.0 + 2.0 * rows / max(NLAT - 1, 1)
    base = jax.random.truncated_normal(key, -4.0, 4.0, (FIELDS, NLAT, NLON), jnp.float32)
    return base * ramp[None, :, None]


def place_ends(values, own_key, smallest, top_value):
    place = [jax.random.randint(jax.random.fold_in(own_key, axis), (), 0, length) for axis, length in enumerate(values.shape)]
    longest = values.shape.index(max(values.shape))
    neighbour = place[:longest] + [(place[longest] + 1) % values.shape[longest]] + place[longest + 1:]
    return values.at[tuple(place)].set(smallest).at[tuple(neighbour)].set(top_value)


def block_levels(stream_key, extent, cuts, smallest, largest):
    loudness = 1.0
    for dim, shards_of in cuts:
        steps = jax.random.uniform(jax.random.fold_in(jax.random.fold_in(stream_key, 6), dim), (shards_of,), jnp.float32, smallest / len(cuts), largest / len(cuts))
        loudness = loudness * jnp.repeat(jnp.exp(steps), extent[dim] // shards_of).reshape((-1,) + (1,) * (len(extent) - 1 - dim))
    return loudness


def scatter_about(stream_key, dims, scale, most, split=(), held_as=jnp.bfloat16):
    gain = block_levels(stream_key, dims, split, -0.22, 0.18) if split else 1.0
    values = jax.random.normal(stream_key, dims, jnp.float32) * scale * gain
    return jnp.minimum(jnp.maximum(values, -most), most).astype(held_as)


def setup_inputs(seed: int = 0, part: int = 0) -> dict:
    splits = jax.random.split(jax.random.key(seed), 10)
    part_splits = jax.random.split(jax.random.fold_in(splits[9], part), 10)
    return {
        "initial_state": scatter_about(part_splits[0], (FIELDS, NLAT, NLON), 1.0, 6.0, ((1, 8), (2, 16)), jnp.float32),
        "diffusion": jnp.clip(jnp.exp(math.log(0.2) - 1.3862944 * jax.random.uniform(splits[1], (NLAT, NLON), jnp.float32) ** block_levels(splits[1], (NLAT, NLON), ((0, 8), (1, 16)), -0.2, 0.2)), 0.05, 0.2),
        "mixing": scatter_about(splits[2], (FIELDS, FIELDS), 0.1, 0.3, (), jnp.float32),
        "land_mask": place_ends((jax.random.randint(splits[3], (NLAT, NLON), 0, 5) < 4).astype(jnp.int32), jax.random.fold_in(splits[3], 1), 0, 1),
        "first_layer": scatter_about(splits[4], (HID, PATCH), PATCH ** -0.5, 0.875),
        "second_layer": scatter_about(splits[5], (HID, HID), HID ** -0.5, 0.5),
        "output_layer": scatter_about(splits[6], (FIELDS, HID), HID ** -0.5, 0.5),
        "cotangent": draw_cotangent(jax.random.fold_in(jax.random.fold_in(splits[9], part), 71), part),
        "update_noise": scatter_about(part_splits[8], (PARAMS,), 0.03, 0.15, (), jnp.float32),
    }


closure_dt = 0.1
learn_rate = 0.1
epsilon = 1e-06
offsets = [(row_shift, col_shift) for row_shift in (-1, 0, 1) for col_shift in (-1, 0, 1)]

def contract_last(left, right):
    return lax.dot_general(left, right, (((1,), (1,)), ((), ())), preferred_element_type=jnp.float32)

def contract_first(left, right):
    return lax.dot_general(left, right, (((0,), (0,)), ((), ())), preferred_element_type=jnp.float32)

def build_patch(slab, rows, cols):
    return jnp.concatenate([slab[:, 1 + row_shift:1 + row_shift + rows, 1 + col_shift:1 + col_shift + cols] for row_shift, col_shift in offsets], axis=0)

def hidden_layers(flat, first_layer, second_layer):
    hidden_one = jnp.tanh(jnp.dot(first_layer, flat, preferred_element_type=jnp.float32)).astype(jnp.bfloat16)
    hidden_two = jnp.tanh(jnp.dot(second_layer, hidden_one, preferred_element_type=jnp.float32)).astype(jnp.bfloat16)
    return (hidden_one, hidden_two)

def forward_block(slab, mask_rows, diff_rows, mixing, first_layer, second_layer, output_layer):
    fields = slab.shape[0]
    rows = slab.shape[1] - 2
    cols = slab.shape[2] - 2
    count = rows * cols
    patch = build_patch(slab, rows, cols)
    centre = patch[4 * fields:5 * fields]
    laplace = patch[fields:2 * fields] + patch[3 * fields:4 * fields] + patch[5 * fields:6 * fields] + patch[7 * fields:8 * fields] - 4.0 * centre
    flat = patch.reshape(9 * fields, count).astype(jnp.bfloat16)
    hidden_one, hidden_two = hidden_layers(flat, first_layer, second_layer)
    tendency = jnp.dot(output_layer, hidden_two, preferred_element_type=jnp.float32)
    mixed = jnp.dot(mixing, centre.reshape(fields, count), precision=lax.Precision.HIGHEST)
    update = centre + diff_rows[None] * laplace + (mixed + closure_dt * tendency).reshape(fields, rows, cols)
    return mask_rows[None] * update

def backward_block(slab, adjoint_rows, mask_rows, diff_rows, mixing, first_layer, second_layer, output_layer):
    fields = slab.shape[0]
    rows = slab.shape[1] - 2
    cols = slab.shape[2] - 2
    count = rows * cols
    patch = build_patch(slab, rows, cols)
    flat = patch.reshape(9 * fields, count).astype(jnp.bfloat16)
    hidden_one, hidden_two = hidden_layers(flat, first_layer, second_layer)
    masked = (mask_rows[None] * adjoint_rows).reshape(fields, count)
    out_grad = (closure_dt * masked).astype(jnp.bfloat16)
    back_two = (contract_first(output_layer, out_grad) * (1.0 - jnp.square(hidden_two.astype(jnp.float32)))).astype(jnp.bfloat16)
    back_one = (contract_first(second_layer, back_two) * (1.0 - jnp.square(hidden_one.astype(jnp.float32)))).astype(jnp.bfloat16)
    patch_grad = contract_first(first_layer, back_one)
    direct = masked + lax.dot_general(mixing, masked, (((0,), (0,)), ((), ())), precision=lax.Precision.HIGHEST, preferred_element_type=jnp.float32)
    spread = diff_rows.reshape(1, count) * masked
    blank = jnp.zeros_like(masked)
    extra = jnp.concatenate([blank, spread, blank, spread, direct - 4.0 * spread, spread, blank, spread, blank], axis=0)
    patch_grad = (patch_grad + extra).reshape(9 * fields, rows, cols)
    grads = jnp.concatenate([contract_last(back_one, flat).ravel(), contract_last(back_two, hidden_one).ravel(), contract_last(out_grad, hidden_two).ravel()])
    return (patch_grad, grads)

def pad_grid(field):
    wide = jnp.concatenate([field[:, :, -1:], field, field[:, :, :1]], axis=2)
    return jnp.pad(wide, ((0, 0), (1, 1), (0, 0)))

def reference(initial_state, diffusion, mixing, land_mask, first_layer, second_layer, output_layer, cotangent, update_noise):
    fields = initial_state.shape[0]
    mask = land_mask.astype(jnp.float32)
    band_ids = jnp.arange(N_LAT, dtype=jnp.int32)

    def rows_of(field, index, axis):
        return lax.dynamic_slice_in_dim(field, index * CLAT, CLAT, axis)

    def restack(pieces):
        return jnp.moveaxis(pieces, 0, 1).reshape(pieces.shape[1], NLAT, NLON)
    states = [initial_state]
    for step in range(STEPS):
        padded = pad_grid(states[-1])

        def advance(index, padded=padded):
            slab = lax.dynamic_slice_in_dim(padded, index * CLAT, CLAT + 2, 1)
            return forward_block(slab, rows_of(mask, index, 0), rows_of(diffusion, index, 0), mixing, first_layer, second_layer, output_layer)
        states.append(restack(lax.map(advance, band_ids)))
    adjoint = cotangent
    band_grad = jnp.zeros((N_LAT, PARAMS), jnp.float32)
    for step in reversed(range(STEPS)):
        padded = pad_grid(states[step])

        def retreat(index, padded=padded, adjoint=adjoint):
            slab = lax.dynamic_slice_in_dim(padded, index * CLAT, CLAT + 2, 1)
            return backward_block(slab, rows_of(adjoint, index, 1), rows_of(mask, index, 0), rows_of(diffusion, index, 0), mixing, first_layer, second_layer, output_layer)
        pieces, grads = lax.map(retreat, band_ids)
        band_grad = band_grad + grads
        grad_pad = pad_grid(restack(pieces))
        total = jnp.zeros((fields, NLAT, NLON), jnp.float32)
        for number, (row_shift, col_shift) in enumerate(offsets):
            total = total + grad_pad[number * fields:(number + 1) * fields, 1 - row_shift:1 - row_shift + NLAT, 1 - col_shift:1 - col_shift + NLON]
        adjoint = total
    total_grad = lax.optimization_barrier(jnp.sum(band_grad, axis=0))
    grad_square = jnp.sum(total_grad * total_grad)
    noise_ratio = (jnp.sum(band_grad * band_grad) / (grad_square + epsilon)).reshape(1)
    params = jnp.concatenate([first_layer.astype(jnp.float32).ravel(), second_layer.astype(jnp.float32).ravel(), output_layer.astype(jnp.float32).ravel()])
    new_params = params - learn_rate * total_grad / jnp.sqrt(grad_square / PARAMS + epsilon) + update_noise
    return (states[-1], adjoint, new_params, noise_ratio)
```

```python
import functools
import math
from types import SimpleNamespace

import jax
import jax.numpy as jnp
from jax import lax
from jax.experimental import pallas as pl
from jax.experimental.pallas import tpu as pltpu
from jax.sharding import PartitionSpec as P

MESH = pl.DeviceIdType.MESH
F32 = jnp.float32
BF16 = jnp.bfloat16

closure_dt = 0.1
learn_rate = 0.1
epsilon = 1e-06
offsets = [(p, q) for p in (-1, 0, 1) for q in (-1, 0, 1)]

FIELDS, ROWS, COLS = 6, 16, 128
HALO = 4
PITCH = COLS + 2 * HALO
EXT = ROWS + 2 * HALO
LANES = 128
TILES = -(-EXT * PITCH // LANES)
FLAT = TILES * LANES
HID = 128
PATCH = 54
DEEP = 80
PARAMS = 24064
NLON, NLAT = 16, 8
CHUNK = 12


def ring(index, step, size):
    return lax.rem(index + step + size, size)


def tile_range(distance):
    low = (HALO - distance) * PITCH // LANES
    high = -(-(HALO + ROWS + distance) * PITCH // LANES)
    if (high - low) % 2:
        low, high = (low, high + 1) if high < TILES else (low - 1, high)
    return low * LANES, high * LANES


def chunks(low, high, size=512):
    return [(start, min(size, high - start)) for start in range(low, high, size)]


def spread_lanes(tile, length):
    return jnp.concatenate([tile] * (length // LANES), axis=1)


def segments(tile):
    found = []
    base = tile * LANES
    for row in range(EXT):
        start = row * PITCH
        for part, low, high in (
            ("left", start, start + HALO),
            ("main", start + HALO, start + HALO + COLS),
            ("right", start + HALO + COLS, start + PITCH),
        ):
            first, end = max(low, base), min(high, base + LANES)
            if first < end:
                found.append((first - base, end - base, row, part))
    return found


def kernel(
    state_hbm,
    diff_hbm,
    mix_ref,
    mask_hbm,
    first_ref,
    second_ref,
    output_ref,
    cot_hbm,
    noise_hbm,
    final_ref,
    adjoint_ref,
    params_ref,
    ratio_ref,
    state_in,
    diff_in,
    mask_in,
    cot_in,
    noise_in,
    load_sem,
    own_a,
    own_b,
    send_north,
    send_south,
    edge,
    from_north,
    from_south,
    edges_in,
    halo_send,
    halo_recv,
    flat_a,
    flat_b,
    own_ref,
    wide_mask,
    wide_diff,
    state_one,
    state_two,
    lap_ref,
    patch_zero,
    patch_one,
    hid_one_zero,
    hid_two_zero,
    hid_one_one,
    hid_two_one,
    back_one,
    back_two,
    out_grad,
    patch_grad,
    adj_one,
    weights_one,
    weights_three,
    base_params,
    grads,
    recv_one,
    recv_two,
    gathered,
    total_ref,
    send_one_sem,
    recv_one_sem,
    send_two_sem,
    recv_two_sem,
    send_three_sem,
    recv_three_sem,
):
    lat = lax.axis_index("lat")
    lon = lax.axis_index("lon")
    north, south = ring(lat, -1, NLAT), ring(lat, 1, NLAT)
    west, east = ring(lon, -1, NLON), ring(lon, 1, NLON)

    barrier = pltpu.get_barrier_semaphore()
    greet = [{"lon": ring(lon, d, NLON)} for d in range(1, NLON)]
    greet += [{"lat": ring(lat, d, NLAT)} for d in range(1, NLAT)]
    greet += [{"lat": a, "lon": b} for a in (north, south) for b in (west, east)]
    for device in greet:
        pl.semaphore_signal(barrier, inc=1, device_id=device, device_id_type=MESH)

    loads = [
        pltpu.make_async_copy(src, dst, load_sem.at[n])
        for n, (src, dst) in enumerate(
            (
                (state_hbm, state_in),
                (mask_hbm, mask_in),
                (diff_hbm, diff_in),
                (cot_hbm, cot_in),
                (noise_hbm, noise_in),
            )
        )
    ]
    for load in loads:
        load.start()

    lane = lax.broadcasted_iota(jnp.int32, (8, LANES), 1)
    sub = lax.broadcasted_iota(jnp.int32, (8, LANES), 0)
    for load in loads[:4]:
        load.wait()

    own_b[...] = jnp.zeros_like(own_b)
    for r in range(ROWS):
        own_a[r, 0:FIELDS, :] = state_in[:, r, :]
        own_a[r, 6:7, :] = mask_in[r : r + 1, :].astype(F32)
        own_a[r, 7:8, :] = diff_in[r : r + 1, :]
        own_b[r, 0:FIELDS, :] = cot_in[:, r, :]
    edge_a = jnp.zeros((8, LANES), F32)
    edge_b = jnp.zeros((8, LANES), F32)
    for r in range(ROWS):
        j = r + HALO
        turn = (j * PITCH + HALO) % LANES
        tile_a = pltpu.roll(own_a[r], turn, 1)
        tile_b = pltpu.roll(own_b[r], turn, 1)
        own_a[r] = tile_a
        own_b[r] = tile_b
        place = (j * PITCH) % LANES
        pick = (lane >= place) & (lane < place + 2 * HALO)
        edge_a = jnp.where(pick, tile_a, edge_a)
        edge_b = jnp.where(pick, tile_b, edge_b)
        if r < HALO:
            send_north[r] = tile_a
        if r < 2:
            send_north[HALO + r] = tile_b
        if r >= ROWS - HALO:
            send_south[r - (ROWS - HALO)] = tile_a
        if r >= ROWS - 2:
            send_south[HALO + r - (ROWS - 2)] = tile_b
    edge[0] = edge_a
    edge[1] = edge_b

    pl.semaphore_wait(barrier, len(greet))

    def halo_copy(n, source, target, device):
        return pltpu.make_async_remote_copy(
            src_ref=source,
            dst_ref=target,
            send_sem=halo_send.at[n],
            recv_sem=halo_recv.at[n],
            device_id=device,
            device_id_type=MESH,
        )

    halos = [
        halo_copy(0, send_north, from_south, {"lat": north}),
        halo_copy(1, send_south, from_north, {"lat": south}),
        halo_copy(2, edge, edges_in.at[0], {"lat": south, "lon": east}),
        halo_copy(3, edge, edges_in.at[1], {"lon": east}),
        halo_copy(4, edge, edges_in.at[2], {"lat": north, "lon": east}),
        halo_copy(5, edge, edges_in.at[3], {"lat": south, "lon": west}),
        halo_copy(6, edge, edges_in.at[4], {"lon": west}),
        halo_copy(7, edge, edges_in.at[5], {"lat": north, "lon": west}),
    ]
    for copy in halos:
        copy.start()

    weights_one[...] = jnp.zeros_like(weights_one)
    weights_one[:, 0:PATCH] = first_ref[...].astype(F32)
    weights_three[...] = jnp.zeros_like(weights_three)
    weights_three[0:FIELDS, :] = output_ref[...].astype(F32)

    def nt(left, right, precision=None):
        return lax.dot_general(
            left, right, (((1,), (1,)), ((), ())), preferred_element_type=F32, precision=precision
        )

    deep_i = lax.broadcasted_iota(jnp.int32, (DEEP, HID), 0)
    deep_j = lax.broadcasted_iota(jnp.int32, (DEEP, HID), 1)
    deep_f = lax.bitwise_and(deep_i, 7)
    picked = (deep_j == 6 * lax.shift_right_logical(deep_i, 3) + deep_f) & (deep_f < 6) & (deep_i < 72)
    select_f = jnp.where(picked, 1.0, 0.0).astype(F32)
    select = select_f.astype(BF16)
    row = lax.broadcasted_iota(jnp.int32, (HID, HID), 0)
    column = lax.broadcasted_iota(jnp.int32, (HID, HID), 1)
    eye = jnp.where(row == column, 1.0, 0.0).astype(BF16)
    plain_one = weights_one[...].astype(BF16)
    w1 = nt(plain_one, select).astype(BF16)
    w1_t = nt(select, plain_one).astype(BF16)
    w2 = second_ref[...]
    w2_t = nt(eye, w2).astype(BF16)
    w3 = weights_three[...].astype(BF16)
    w3_t = nt(eye, w3).astype(BF16)

    turn_of = lax.bitwise_and(row * PATCH, LANES - 1)
    deep_r = lax.broadcasted_iota(jnp.int32, (56, 2 * HID), 0)
    deep_h = lax.broadcasted_iota(jnp.int32, (56, 2 * HID), 1)
    hid_h = lax.bitwise_and(deep_h, HID - 1)
    lands = lax.shift_right_logical(hid_h * PATCH, 7) + lax.shift_right_logical(deep_h, 7)
    gather_rows = jnp.where(lands == deep_r, 1.0, 0.0).astype(F32)

    def flatten_rows(value, exact):
        for bit in range(1, 7):
            moved = pltpu.roll(value, 1 << bit, 1)
            chosen = lax.bitwise_and(lax.shift_right_logical(turn_of, bit), 1) == 1
            value = jnp.where(chosen, moved, value)
        ahead = jnp.where(column >= turn_of, value, 0.0)
        behind = jnp.where(column < turn_of, value, 0.0)
        both = jnp.concatenate([ahead, behind], axis=0)
        if exact:
            return jnp.dot(
                gather_rows, both, preferred_element_type=F32, precision=lax.Precision.HIGHEST
            )
        return jnp.dot(gather_rows.astype(BF16), both.astype(BF16), preferred_element_type=F32)

    base_params[0:56, :] = flatten_rows(weights_one[...], False)
    base_params[54:182, :] = w2.astype(F32)
    base_params[182:188, :] = output_ref[...].astype(F32)

    for t in range(TILES):
        own = jnp.zeros((8, LANES), F32)
        for first, end, j, part in segments(t):
            if part == "main" and HALO <= j < HALO + ROWS:
                own = jnp.where((lane >= first) & (lane < end), 1.0, own)
        own_ref[:, t * LANES : (t + 1) * LANES] = jnp.concatenate([own] * (HID // 8), axis=0).astype(BF16)

    mix_to = []
    mix_from = []
    for g in range(FIELDS):
        to_tile = jnp.zeros((8, LANES), F32)
        from_tile = jnp.zeros((8, LANES), F32)
        for f in range(FIELDS):
            to_tile = jnp.where(sub == f, mix_ref[f, g], to_tile)
            from_tile = jnp.where(sub == f, mix_ref[g, f], from_tile)
        mix_to.append(to_tile)
        mix_from.append(from_tile)

    def mixed(tiles, value):
        length = value.shape[1]
        total = None
        for g in range(FIELDS):
            term = spread_lanes(tiles[g], length) * jnp.broadcast_to(value[g : g + 1, :], (8, length))
            total = term if total is None else total + term
        return total

    for copy in halos:
        copy.wait_recv()

    def top(value):
        return jnp.where(lat > 0, value, 0.0)

    def bottom(value):
        return jnp.where(lat < NLAT - 1, value, 0.0)

    blank = jnp.zeros((8, LANES), F32)
    sides = []
    for which in range(2):
        sides.append(
            {
                "left": (top(edges_in[0, which]), edges_in[1, which], bottom(edges_in[2, which])),
                "right": (top(edges_in[3, which]), edges_in[4, which], bottom(edges_in[5, which])),
            }
        )

    def source(which, j, part):
        if which == 1 and (j < 2 or j >= EXT - 2):
            return blank
        if part != "main":
            return sides[which][part][0 if j < HALO else 1 if j < HALO + ROWS else 2]
        if j < HALO:
            return top(from_north[j if which == 0 else HALO + j - 2])
        if j < HALO + ROWS:
            return (own_a if which == 0 else own_b)[j - HALO]
        return bottom(from_south[(j - HALO - ROWS) if which == 0 else HALO + j - HALO - ROWS])

    for t in range(TILES):
        here = slice(t * LANES, (t + 1) * LANES)
        for which, target in ((0, flat_a), (1, flat_b)):
            value = blank
            for first, end, j, part in segments(t):
                piece = source(which, j, part)
                value = jnp.where((lane >= first) & (lane < end), piece, value)
            target[:, here] = value
            if which == 0:
                wide_mask[:, here] = jnp.broadcast_to(value[6:7, :], (8, LANES))
                wide_diff[:, here] = jnp.broadcast_to(value[7:8, :], (8, LANES))

    def shift(value, amount):
        return pltpu.roll(value, (-amount) % FLAT, 1)

    def make_patch(value, patch_ref):
        blocks = [value if (p, q) == (0, 0) else shift(value, p * PITCH + q) for p, q in offsets]
        for m in range(5):
            after = blocks[2 * m + 1] if m < 4 else jnp.zeros_like(value)
            patch_ref[16 * m : 16 * m + 16, :] = jnp.concatenate([blocks[2 * m], after], axis=0).astype(BF16)
        lap_ref[...] = blocks[1] + blocks[7] + blocks[3] + blocks[5] - 4.0 * value

    def forward(state_ref, patch_ref, one_ref, two_ref, next_ref, low, high, write_low, write_high):
        for start, size in chunks(low, high):
            here = slice(start, start + size)
            one = jnp.tanh(jnp.dot(w1, patch_ref[:, here], preferred_element_type=F32)).astype(BF16)
            one_ref[:, here] = one
            two = jnp.tanh(jnp.dot(w2, one, preferred_element_type=F32)).astype(BF16)
            two_ref[:, here] = two
            tendency = jnp.dot(w3, two, preferred_element_type=F32)[0:8]
            centre = state_ref[:, here]
            update = (
                centre
                + wide_diff[:, here] * lap_ref[:, here]
                + (mixed(mix_to, centre) + closure_dt * tendency)
            )
            next_ref[:, here] = wide_mask[:, here] * update

    state_one[...] = jnp.zeros_like(state_one)
    make_patch(flat_a[...], patch_zero)
    low, high = tile_range(3)
    forward(flat_a, patch_zero, hid_one_zero, hid_two_zero, state_one, low, high, low, high)
    make_patch(state_one[...], patch_one)
    low, high = tile_range(2)
    forward(state_one, patch_one, hid_one_one, hid_two_one, state_two, low, high, low, high)

    def write_rows(source_ref, target_ref):
        for r in range(ROWS):
            start = (r + HALO) * PITCH + HALO
            t, turn = start // LANES, start % LANES
            before = source_ref[:, t * LANES : (t + 1) * LANES]
            after = source_ref[:, (t + 1) * LANES : (t + 2) * LANES]
            value = pltpu.roll(jnp.where(lane >= turn, before, after), (LANES - turn) % LANES, 1)
            target_ref[:, r, :] = value[0:FIELDS]

    grad_low, grad_high = tile_range(0)
    grad_here = slice(grad_low, grad_high)

    def backward(adj_ref, patch_ref, one_ref, two_ref, low, high):
        for start, size in chunks(low, high):
            here = slice(start, start + size)
            masked = wide_mask[:, here] * adj_ref[:, here]
            low_grad = jnp.concatenate([closure_dt * masked, jnp.zeros_like(masked)], axis=0).astype(BF16)
            out_grad[:, here] = low_grad
            two = two_ref[:, here].astype(F32)
            grad_two = (
                jnp.dot(w3_t, low_grad, preferred_element_type=F32) * (1.0 - two * two)
            ).astype(BF16)
            back_two[:, here] = grad_two
            one = one_ref[:, here].astype(F32)
            grad_one = (
                jnp.dot(w2_t, grad_two, preferred_element_type=F32) * (1.0 - one * one)
            ).astype(BF16)
            back_one[:, here] = grad_one
            grad_zero = jnp.dot(w1_t, grad_one, preferred_element_type=F32)
            spread = wide_diff[:, here] * masked
            direct = masked + mixed(mix_from, masked) - 4.0 * spread
            for k in range(9):
                block = grad_zero[8 * k : 8 * k + 8]
                if k == 4:
                    block = block + direct
                elif k % 2:
                    block = block + spread
                patch_grad[8 * k : 8 * k + 8, here] = block
        own = own_ref[:, grad_here]
        grad_first = nt(back_one[:, grad_here], patch_ref[:, grad_here] * own[0:DEEP])
        grad_second = nt(back_two[:, grad_here], one_ref[:, grad_here] * own)
        grad_output = nt(out_grad[:, grad_here] * own[0:16], two_ref[:, grad_here])
        return grad_first, grad_second, grad_output

    def scatter():
        total = None
        for k, (p, q) in enumerate(offsets):
            block = patch_grad[8 * k : 8 * k + 8, :]
            if (p, q) != (0, 0):
                block = shift(block, -(p * PITCH + q))
            total = block if total is None else total + block
        return total

    patch_grad[...] = jnp.zeros_like(patch_grad)
    low, high = tile_range(2)
    late_first, late_second, late_output = backward(flat_b, patch_one, hid_one_one, hid_two_one, low, high)
    adj_one[...] = scatter()
    low, high = tile_range(1)
    first, second, output = backward(adj_one, patch_zero, hid_one_zero, hid_two_zero, low, high)
    first = first + late_first
    second = second + late_second
    output = output + late_output

    narrow = jnp.dot(first, select_f, preferred_element_type=F32, precision=lax.Precision.HIGHEST)
    others = jnp.concatenate([flatten_rows(narrow, True), output[0:8]], axis=0)
    for i in range(NLON):
        grads[i, 0:8, :] = second[8 * i : 8 * i + 8]
        grads[i, 8:12, :] = others[4 * i : 4 * i + 4]

    scatters = []
    for d in range(1, NLON):
        peer = ring(lon, d, NLON)
        copy = pltpu.make_async_remote_copy(
            src_ref=grads.at[peer],
            dst_ref=recv_one.at[d - 1],
            send_sem=send_one_sem.at[d - 1],
            recv_sem=recv_one_sem.at[d - 1],
            device_id={"lon": peer},
            device_id_type=MESH,
        )
        copy.start()
        scatters.append(copy)

    write_rows(state_two, final_ref)
    adj_one[...] = scatter()
    write_rows(adj_one, adjoint_ref)

    band = grads[lon]
    for d in range(1, NLON):
        scatters[d - 1].wait_recv()
        band = band + recv_one[d - 1]
    recv_two[lat] = band

    exchanges = []
    for d in range(1, NLAT):
        peer = ring(lat, d, NLAT)
        copy = pltpu.make_async_remote_copy(
            src_ref=recv_two.at[lat],
            dst_ref=recv_two.at[lat],
            send_sem=send_two_sem.at[d - 1],
            recv_sem=recv_two_sem.at[d - 1],
            device_id={"lat": peer},
            device_id_type=MESH,
        )
        copy.start()
        exchanges.append(copy)
    for copy in exchanges:
        copy.wait_recv()
    total = recv_two[0]
    squares = total * total
    for b in range(1, NLAT):
        value = recv_two[b]
        total = total + value
        squares = squares + value * value
    gathered[lon, 0:CHUNK, :] = total
    gathered[lon, CHUNK:16, :] = jnp.broadcast_to(jnp.sum(squares, axis=0, keepdims=True), (16 - CHUNK, LANES))

    collects = []
    for d in range(1, NLON):
        peer = ring(lon, d, NLON)
        copy = pltpu.make_async_remote_copy(
            src_ref=gathered.at[lon],
            dst_ref=gathered.at[lon],
            send_sem=send_three_sem.at[d - 1],
            recv_sem=recv_three_sem.at[d - 1],
            device_id={"lon": peer},
            device_id_type=MESH,
        )
        copy.start()
        collects.append(copy)
    loads[4].wait()
    for copy in collects:
        copy.wait_recv()

    square_sum = jnp.zeros((CHUNK, LANES), F32)
    band_sum = jnp.zeros((1, LANES), F32)
    for i in range(NLON):
        value = gathered[i, 0:CHUNK, :]
        square_sum = square_sum + value * value
        band_sum = band_sum + gathered[i, CHUNK : CHUNK + 1, :]
        total_ref[54 + 8 * i : 62 + 8 * i, :] = value[0:8]
        if i < 13:
            total_ref[4 * i : 4 * i + 4, :] = value[8:12]
        elif i == 13:
            total_ref[52:54, :] = value[8:10]
        elif i == 14:
            total_ref[182:186, :] = value[8:12]
        else:
            total_ref[186:188, :] = value[8:10]
    grad_square = jnp.sum(square_sum)
    ratio_ref[0] = jnp.sum(band_sum) / (grad_square + epsilon)
    spread_square = jnp.full((1, LANES), grad_square / PARAMS + epsilon, F32)
    scale = learn_rate / jnp.sqrt(spread_square)
    params_ref[...] = base_params[0:188, :] - scale * total_ref[0:188, :] + noise_in[...]

    for copy in halos + scatters + exchanges + collects:
        copy.wait_send()


def on_device(
    initial_state,
    diffusion,
    mixing,
    land_mask,
    first_layer,
    second_layer,
    output_layer,
    cotangent,
    update_noise,
):
    vmem = pltpu.VMEM
    flat8 = vmem((8, FLAT), F32)
    hidden = vmem((HID, FLAT), BF16)
    dma = pltpu.SemaphoreType.DMA
    scratch = [
        vmem((FIELDS, ROWS, COLS), F32),
        vmem((ROWS, COLS), F32),
        vmem((ROWS, COLS), jnp.int32),
        vmem((FIELDS, ROWS, COLS), F32),
        vmem((188, LANES), F32),
        dma((5,)),
        vmem((ROWS, 8, LANES), F32),
        vmem((ROWS, 8, LANES), F32),
        vmem((6, 8, LANES), F32),
        vmem((6, 8, LANES), F32),
        vmem((2, 8, LANES), F32),
        vmem((6, 8, LANES), F32),
        vmem((6, 8, LANES), F32),
        vmem((6, 2, 8, LANES), F32),
        dma((8,)),
        dma((8,)),
        flat8,
        flat8,
        hidden,
        flat8,
        flat8,
        flat8,
        flat8,
        flat8,
        vmem((DEEP, FLAT), BF16),
        vmem((DEEP, FLAT), BF16),
        hidden,
        hidden,
        hidden,
        hidden,
        hidden,
        hidden,
        vmem((16, FLAT), BF16),
        vmem((72, FLAT), F32),
        flat8,
        vmem((HID, LANES), F32),
        vmem((16, LANES), F32),
        vmem((192, LANES), F32),
        vmem((NLON, CHUNK, LANES), F32),
        vmem((NLON - 1, CHUNK, LANES), F32),
        vmem((NLAT, CHUNK, LANES), F32),
        vmem((NLON, 16, LANES), F32),
        vmem((192, LANES), F32),
        dma((NLON - 1,)),
        dma((NLON - 1,)),
        dma((NLAT - 1,)),
        dma((NLAT - 1,)),
        dma((NLON - 1,)),
        dma((NLON - 1,)),
    ]
    hbm = pl.BlockSpec(memory_space=pl.ANY)
    local = pl.BlockSpec(memory_space=pltpu.VMEM)
    scalars = pl.BlockSpec(memory_space=pltpu.SMEM)
    final, adjoint, params, ratio = pl.pallas_call(
        kernel,
        out_shape=(
            jax.ShapeDtypeStruct((FIELDS, ROWS, COLS), F32),
            jax.ShapeDtypeStruct((FIELDS, ROWS, COLS), F32),
            jax.ShapeDtypeStruct((188, LANES), F32),
            jax.ShapeDtypeStruct((1,), F32),
        ),
        in_specs=[hbm, hbm, scalars, hbm, local, local, local, hbm, hbm],
        out_specs=(local, local, local, scalars),
        scratch_shapes=scratch,
        compiler_params=pltpu.CompilerParams(
            collective_id=0, has_side_effects=True, vmem_limit_bytes=40 * 1024 * 1024
        ),
        name="ocean",
    )(
        initial_state,
        diffusion,
        mixing,
        land_mask,
        first_layer,
        second_layer,
        output_layer,
        cotangent,
        update_noise.reshape(188, LANES),
    )
    return final, adjoint, params.reshape(PARAMS), ratio


def solution(mesh):
    placed = (
        P("ens", "lat", "lon"),
        P("lat", "lon"),
        P(),
        P("lat", "lon"),
        P(),
        P(),
        P(),
        P("ens", "lat", "lon"),
        P("ens"),
    )
    return jax.shard_map(
        on_device,
        mesh=mesh,
        in_specs=placed,
        out_specs=(P("ens", "lat", "lon"), P("ens", "lat", "lon"), P("ens"), P("ens")),
        check_vma=False,
    )
```

```python
import functools
import math
from types import SimpleNamespace

import jax
import jax.numpy as jnp
from jax import lax
from jax.experimental import pallas as pl
from jax.experimental.pallas import tpu as pltpu
from jax.sharding import PartitionSpec as P

MESH = pl.DeviceIdType.MESH
F32 = jnp.float32
BF16 = jnp.bfloat16

closure_dt = 0.1
learn_rate = 0.1
epsilon = 1e-06
offsets = [(p, q) for p in (-1, 0, 1) for q in (-1, 0, 1)]

FIELDS, ROWS, COLS = 6, 16, 128
HALO = 4
PITCH = COLS + 2 * HALO
EXT = ROWS + 2 * HALO
LANES = 128
TILES = -(-EXT * PITCH // LANES)
FLAT = TILES * LANES
HID = 128
PATCH = 54
DEEP = 80
PARAMS = 24064
NLON, NLAT = 16, 8
CHUNK = 12


def ring(index, step, size):
    return lax.rem(index + step + size, size)


def tile_range(distance):
    low = (HALO - distance) * PITCH // LANES
    high = -(-(HALO + ROWS + distance) * PITCH // LANES)
    if (high - low) % 2:
        low, high = (low, high + 1) if high < TILES else (low - 1, high)
    return low * LANES, high * LANES


def chunks(low, high, size=512):
    return [(start, min(size, high - start)) for start in range(low, high, size)]


def spread_lanes(tile, length):
    return jnp.concatenate([tile] * (length // LANES), axis=1)


def segments(tile):
    found = []
    base = tile * LANES
    for row in range(EXT):
        start = row * PITCH
        for part, low, high in (
            ("left", start, start + HALO),
            ("main", start + HALO, start + HALO + COLS),
            ("right", start + HALO + COLS, start + PITCH),
        ):
            first, end = max(low, base), min(high, base + LANES)
            if first < end:
                found.append((first - base, end - base, row, part))
    return found


def kernel(
    state_hbm,
    diff_hbm,
    mix_hbm,
    mask_hbm,
    first_hbm,
    second_hbm,
    output_hbm,
    cot_hbm,
    noise_hbm,
    final_ref,
    adjoint_ref,
    params_ref,
    ratio_ref,
    state_in,
    diff_in,
    mask_in,
    cot_in,
    noise_in,
    mix_ref,
    first_ref,
    second_ref,
    output_ref,
    load_sem,
    own_a,
    own_b,
    send_north,
    send_south,
    edge,
    from_north,
    from_south,
    edges_in,
    halo_send,
    halo_recv,
    flat_a,
    flat_b,
    own_ref,
    wide_mask,
    wide_diff,
    state_one,
    state_two,
    lap_ref,
    patch_zero,
    patch_one,
    hid_one_zero,
    hid_two_zero,
    hid_one_one,
    hid_two_one,
    back_one,
    back_two,
    out_grad,
    patch_grad,
    adj_one,
    weights_one,
    weights_three,
    base_params,
    grads,
    recv_one,
    recv_two,
    gathered,
    total_ref,
    send_one_sem,
    recv_one_sem,
    send_two_sem,
    recv_two_sem,
    send_three_sem,
    recv_three_sem,
):
    lat = lax.axis_index("lat")
    lon = lax.axis_index("lon")
    north, south = ring(lat, -1, NLAT), ring(lat, 1, NLAT)
    west, east = ring(lon, -1, NLON), ring(lon, 1, NLON)

    barrier = pltpu.get_barrier_semaphore()
    greet = [{"lon": ring(lon, d, NLON)} for d in range(1, NLON)]
    greet += [{"lat": ring(lat, d, NLAT)} for d in range(1, NLAT)]
    greet += [{"lat": a, "lon": b} for a in (north, south) for b in (west, east)]
    for device in greet:
        pl.semaphore_signal(barrier, inc=1, device_id=device, device_id_type=MESH)

    loads = [
        pltpu.make_async_copy(src, dst, load_sem.at[n])
        for n, (src, dst) in enumerate(
            (
                (state_hbm, state_in),
                (mask_hbm, mask_in),
                (diff_hbm, diff_in),
                (cot_hbm, cot_in),
                (mix_hbm, mix_ref),
                (first_hbm, first_ref),
                (second_hbm, second_ref),
                (output_hbm, output_ref),
                (noise_hbm, noise_in),
            )
        )
    ]
    for load in loads:
        load.start()

    lane = lax.broadcasted_iota(jnp.int32, (8, LANES), 1)
    sub = lax.broadcasted_iota(jnp.int32, (8, LANES), 0)
    for load in loads[:4]:
        load.wait()

    own_b[...] = jnp.zeros_like(own_b)
    for r in range(ROWS):
        own_a[r, 0:FIELDS, :] = state_in[:, r, :]
        own_a[r, 6:7, :] = mask_in[r : r + 1, :].astype(F32)
        own_a[r, 7:8, :] = diff_in[r : r + 1, :]
        own_b[r, 0:FIELDS, :] = cot_in[:, r, :]
    edge_a = jnp.zeros((8, LANES), F32)
    edge_b = jnp.zeros((8, LANES), F32)
    for r in range(ROWS):
        j = r + HALO
        turn = (j * PITCH + HALO) % LANES
        tile_a = pltpu.roll(own_a[r], turn, 1)
        tile_b = pltpu.roll(own_b[r], turn, 1)
        own_a[r] = tile_a
        own_b[r] = tile_b
        place = (j * PITCH) % LANES
        pick = (lane >= place) & (lane < place + 2 * HALO)
        edge_a = jnp.where(pick, tile_a, edge_a)
        edge_b = jnp.where(pick, tile_b, edge_b)
        if r < HALO:
            send_north[r] = tile_a
        if r < 2:
            send_north[HALO + r] = tile_b
        if r >= ROWS - HALO:
            send_south[r - (ROWS - HALO)] = tile_a
        if r >= ROWS - 2:
            send_south[HALO + r - (ROWS - 2)] = tile_b
    edge[0] = edge_a
    edge[1] = edge_b

    pl.semaphore_wait(barrier, len(greet))

    def halo_copy(n, source, target, device):
        return pltpu.make_async_remote_copy(
            src_ref=source,
            dst_ref=target,
            send_sem=halo_send.at[n],
            recv_sem=halo_recv.at[n],
            device_id=device,
            device_id_type=MESH,
        )

    halos = [
        halo_copy(0, send_north, from_south, {"lat": north}),
        halo_copy(1, send_south, from_north, {"lat": south}),
        halo_copy(2, edge, edges_in.at[0], {"lat": south, "lon": east}),
        halo_copy(3, edge, edges_in.at[1], {"lon": east}),
        halo_copy(4, edge, edges_in.at[2], {"lat": north, "lon": east}),
        halo_copy(5, edge, edges_in.at[3], {"lat": south, "lon": west}),
        halo_copy(6, edge, edges_in.at[4], {"lon": west}),
        halo_copy(7, edge, edges_in.at[5], {"lat": north, "lon": west}),
    ]
    for copy in halos:
        copy.start()

    for load in loads[4:8]:
        load.wait()
    weights_one[...] = jnp.zeros_like(weights_one)
    weights_one[0:PATCH, :] = first_ref[...].astype(F32)
    weights_three[...] = jnp.zeros_like(weights_three)
    weights_three[0:FIELDS, :] = output_ref[...].astype(F32)

    def nt(left, right, precision=None):
        return lax.dot_general(
            left, right, (((1,), (1,)), ((), ())), preferred_element_type=F32, precision=precision
        )

    deep_i = lax.broadcasted_iota(jnp.int32, (DEEP, HID), 0)
    deep_j = lax.broadcasted_iota(jnp.int32, (DEEP, HID), 1)
    deep_f = lax.bitwise_and(deep_i, 7)
    picked = (deep_j == 6 * lax.shift_right_logical(deep_i, 3) + deep_f) & (deep_f < 6) & (deep_i < 72)
    select_f = jnp.where(picked, 1.0, 0.0).astype(F32)
    select = select_f.astype(BF16)
    row = lax.broadcasted_iota(jnp.int32, (HID, HID), 0)
    column = lax.broadcasted_iota(jnp.int32, (HID, HID), 1)
    eye = jnp.where(row == column, 1.0, 0.0).astype(BF16)
    turned_one = weights_one[...].astype(BF16)
    plain_one = nt(eye, turned_one).astype(BF16)
    w1 = nt(plain_one, select).astype(BF16)
    w1_t = jnp.dot(select, turned_one, preferred_element_type=F32).astype(BF16)
    w2 = second_ref[...]
    w2_t = nt(eye, w2).astype(BF16)
    w3 = weights_three[...].astype(BF16)
    w3_t = nt(eye, w3).astype(BF16)

    turn_of = lax.bitwise_and(row * PATCH, LANES - 1)
    deep_r = lax.broadcasted_iota(jnp.int32, (56, 2 * HID), 0)
    deep_h = lax.broadcasted_iota(jnp.int32, (56, 2 * HID), 1)
    hid_h = lax.bitwise_and(deep_h, HID - 1)
    lands = lax.shift_right_logical(hid_h * PATCH, 7) + lax.shift_right_logical(deep_h, 7)
    gather_rows = jnp.where(lands == deep_r, 1.0, 0.0).astype(F32)

    def flatten_rows(value, exact):
        for bit in range(1, 7):
            moved = pltpu.roll(value, 1 << bit, 1)
            chosen = lax.bitwise_and(lax.shift_right_logical(turn_of, bit), 1) == 1
            value = jnp.where(chosen, moved, value)
        ahead = jnp.where(column >= turn_of, value, 0.0)
        behind = jnp.where(column < turn_of, value, 0.0)
        both = jnp.concatenate([ahead, behind], axis=0)
        if exact:
            return jnp.dot(
                gather_rows, both, preferred_element_type=F32, precision=lax.Precision.HIGHEST
            )
        return jnp.dot(gather_rows.astype(BF16), both.astype(BF16), preferred_element_type=F32)

    base_params[0:56, :] = flatten_rows(plain_one.astype(F32), False)
    base_params[54:182, :] = w2.astype(F32)
    base_params[182:188, :] = output_ref[...].astype(F32)

    for t in range(TILES):
        own = jnp.zeros((8, LANES), F32)
        for first, end, j, part in segments(t):
            if part == "main" and HALO <= j < HALO + ROWS:
                own = jnp.where((lane >= first) & (lane < end), 1.0, own)
        own_ref[:, t * LANES : (t + 1) * LANES] = jnp.concatenate([own] * (HID // 8), axis=0).astype(BF16)

    mix_to = []
    mix_from = []
    for g in range(FIELDS):
        to_tile = jnp.zeros((8, LANES), F32)
        from_tile = jnp.zeros((8, LANES), F32)
        for f in range(FIELDS):
            to_tile = jnp.where(sub == f, mix_ref[f, g], to_tile)
            from_tile = jnp.where(sub == f, mix_ref[g, f], from_tile)
        mix_to.append(to_tile)
        mix_from.append(from_tile)

    def mixed(tiles, value):
        length = value.shape[1]
        total = None
        for g in range(FIELDS):
            term = spread_lanes(tiles[g], length) * jnp.broadcast_to(value[g : g + 1, :], (8, length))
            total = term if total is None else total + term
        return total

    for copy in halos:
        copy.wait_recv()

    def top(value):
        return jnp.where(lat > 0, value, 0.0)

    def bottom(value):
        return jnp.where(lat < NLAT - 1, value, 0.0)

    blank = jnp.zeros((8, LANES), F32)
    sides = []
    for which in range(2):
        sides.append(
            {
                "left": (top(edges_in[0, which]), edges_in[1, which], bottom(edges_in[2, which])),
                "right": (top(edges_in[3, which]), edges_in[4, which], bottom(edges_in[5, which])),
            }
        )

    def source(which, j, part):
        if which == 1 and (j < 2 or j >= EXT - 2):
            return blank
        if part != "main":
            return sides[which][part][0 if j < HALO else 1 if j < HALO + ROWS else 2]
        if j < HALO:
            return top(from_north[j if which == 0 else HALO + j - 2])
        if j < HALO + ROWS:
            return (own_a if which == 0 else own_b)[j - HALO]
        return bottom(from_south[(j - HALO - ROWS) if which == 0 else HALO + j - HALO - ROWS])

    for t in range(TILES):
        here = slice(t * LANES, (t + 1) * LANES)
        for which, target in ((0, flat_a), (1, flat_b)):
            value = blank
            for first, end, j, part in segments(t):
                piece = source(which, j, part)
                value = jnp.where((lane >= first) & (lane < end), piece, value)
            target[:, here] = value
            if which == 0:
                wide_mask[:, here] = jnp.broadcast_to(value[6:7, :], (8, LANES))
                wide_diff[:, here] = jnp.broadcast_to(value[7:8, :], (8, LANES))

    def shift(value, amount):
        return pltpu.roll(value, (-amount) % FLAT, 1)

    def make_patch(value, patch_ref):
        blocks = [value if (p, q) == (0, 0) else shift(value, p * PITCH + q) for p, q in offsets]
        for m in range(5):
            after = blocks[2 * m + 1] if m < 4 else jnp.zeros_like(value)
            patch_ref[16 * m : 16 * m + 16, :] = jnp.concatenate([blocks[2 * m], after], axis=0).astype(BF16)
        lap_ref[...] = blocks[1] + blocks[7] + blocks[3] + blocks[5] - 4.0 * value

    def forward(state_ref, patch_ref, one_ref, two_ref, next_ref, low, high, write_low, write_high):
        for start, size in chunks(low, high):
            here = slice(start, start + size)
            one = jnp.tanh(jnp.dot(w1, patch_ref[:, here], preferred_element_type=F32)).astype(BF16)
            one_ref[:, here] = one
            two = jnp.tanh(jnp.dot(w2, one, preferred_element_type=F32)).astype(BF16)
            two_ref[:, here] = two
            tendency = jnp.dot(w3, two, preferred_element_type=F32)[0:8]
            centre = state_ref[:, here]
            update = (
                centre
                + wide_diff[:, here] * lap_ref[:, here]
                + (mixed(mix_to, centre) + closure_dt * tendency)
            )
            next_ref[:, here] = wide_mask[:, here] * update

    state_one[...] = jnp.zeros_like(state_one)
    make_patch(flat_a[...], patch_zero)
    low, high = tile_range(3)
    forward(flat_a, patch_zero, hid_one_zero, hid_two_zero, state_one, low, high, low, high)
    make_patch(state_one[...], patch_one)
    low, high = tile_range(2)
    forward(state_one, patch_one, hid_one_one, hid_two_one, state_two, low, high, low, high)

    def write_rows(source_ref, target_ref):
        for r in range(ROWS):
            start = (r + HALO) * PITCH + HALO
            t, turn = start // LANES, start % LANES
            before = source_ref[:, t * LANES : (t + 1) * LANES]
            after = source_ref[:, (t + 1) * LANES : (t + 2) * LANES]
            value = pltpu.roll(jnp.where(lane >= turn, before, after), (LANES - turn) % LANES, 1)
            target_ref[:, r, :] = value[0:FIELDS]

    grad_low, grad_high = tile_range(0)
    grad_here = slice(grad_low, grad_high)

    def backward(adj_ref, patch_ref, one_ref, two_ref, low, high):
        for start, size in chunks(low, high):
            here = slice(start, start + size)
            masked = wide_mask[:, here] * adj_ref[:, here]
            low_grad = jnp.concatenate([closure_dt * masked, jnp.zeros_like(masked)], axis=0).astype(BF16)
            out_grad[:, here] = low_grad
            two = two_ref[:, here].astype(F32)
            grad_two = (
                jnp.dot(w3_t, low_grad, preferred_element_type=F32) * (1.0 - two * two)
            ).astype(BF16)
            back_two[:, here] = grad_two
            one = one_ref[:, here].astype(F32)
            grad_one = (
                jnp.dot(w2_t, grad_two, preferred_element_type=F32) * (1.0 - one * one)
            ).astype(BF16)
            back_one[:, here] = grad_one
            grad_zero = jnp.dot(w1_t, grad_one, preferred_element_type=F32)
            spread = wide_diff[:, here] * masked
            direct = masked + mixed(mix_from, masked) - 4.0 * spread
            for k in range(9):
                block = grad_zero[8 * k : 8 * k + 8]
                if k == 4:
                    block = block + direct
                elif k % 2:
                    block = block + spread
                patch_grad[8 * k : 8 * k + 8, here] = block
        own = own_ref[:, grad_here]
        grad_first = nt(back_one[:, grad_here], patch_ref[:, grad_here] * own[0:DEEP])
        grad_second = nt(back_two[:, grad_here], one_ref[:, grad_here] * own)
        grad_output = nt(out_grad[:, grad_here] * own[0:16], two_ref[:, grad_here])
        return grad_first, grad_second, grad_output

    def scatter():
        total = None
        for k, (p, q) in enumerate(offsets):
            block = patch_grad[8 * k : 8 * k + 8, :]
            if (p, q) != (0, 0):
                block = shift(block, -(p * PITCH + q))
            total = block if total is None else total + block
        return total

    patch_grad[...] = jnp.zeros_like(patch_grad)
    low, high = tile_range(2)
    late_first, late_second, late_output = backward(flat_b, patch_one, hid_one_one, hid_two_one, low, high)
    adj_one[...] = scatter()
    low, high = tile_range(1)
    first, second, output = backward(adj_one, patch_zero, hid_one_zero, hid_two_zero, low, high)
    first = first + late_first
    second = second + late_second
    output = output + late_output

    narrow = jnp.dot(first, select_f, preferred_element_type=F32, precision=lax.Precision.HIGHEST)
    others = jnp.concatenate([flatten_rows(narrow, True), output[0:8]], axis=0)
    for i in range(NLON):
        grads[i, 0:8, :] = second[8 * i : 8 * i + 8]
        grads[i, 8:12, :] = others[4 * i : 4 * i + 4]

    scatters = []
    for d in range(1, NLON):
        peer = ring(lon, d, NLON)
        copy = pltpu.make_async_remote_copy(
            src_ref=grads.at[peer],
            dst_ref=recv_one.at[d - 1],
            send_sem=send_one_sem.at[d - 1],
            recv_sem=recv_one_sem.at[d - 1],
            device_id={"lon": peer},
            device_id_type=MESH,
        )
        copy.start()
        scatters.append(copy)

    write_rows(state_two, final_ref)
    adj_one[...] = scatter()
    write_rows(adj_one, adjoint_ref)

    band = grads[lon]
    for d in range(1, NLON):
        scatters[d - 1].wait_recv()
        band = band + recv_one[d - 1]
    recv_two[lat] = band

    exchanges = []
    for d in range(1, NLAT):
        peer = ring(lat, d, NLAT)
        copy = pltpu.make_async_remote_copy(
            src_ref=recv_two.at[lat],
            dst_ref=recv_two.at[lat],
            send_sem=send_two_sem.at[d - 1],
            recv_sem=recv_two_sem.at[d - 1],
            device_id={"lat": peer},
            device_id_type=MESH,
        )
        copy.start()
        exchanges.append(copy)
    for copy in exchanges:
        copy.wait_recv()
    total = recv_two[0]
    squares = total * total
    for b in range(1, NLAT):
        value = recv_two[b]
        total = total + value
        squares = squares + value * value
    gathered[lon, 0:CHUNK, :] = total
    gathered[lon, CHUNK:16, :] = jnp.broadcast_to(jnp.sum(squares, axis=0, keepdims=True), (16 - CHUNK, LANES))

    collects = []
    for d in range(1, NLON):
        peer = ring(lon, d, NLON)
        copy = pltpu.make_async_remote_copy(
            src_ref=gathered.at[lon],
            dst_ref=gathered.at[lon],
            send_sem=send_three_sem.at[d - 1],
            recv_sem=recv_three_sem.at[d - 1],
            device_id={"lon": peer},
            device_id_type=MESH,
        )
        copy.start()
        collects.append(copy)
    loads[8].wait()
    for copy in collects:
        copy.wait_recv()

    square_sum = jnp.zeros((CHUNK, LANES), F32)
    band_sum = jnp.zeros((1, LANES), F32)
    for i in range(NLON):
        value = gathered[i, 0:CHUNK, :]
        square_sum = square_sum + value * value
        band_sum = band_sum + gathered[i, CHUNK : CHUNK + 1, :]
        total_ref[54 + 8 * i : 62 + 8 * i, :] = value[0:8]
        if i < 13:
            total_ref[4 * i : 4 * i + 4, :] = value[8:12]
        elif i == 13:
            total_ref[52:54, :] = value[8:10]
        elif i == 14:
            total_ref[182:186, :] = value[8:12]
        else:
            total_ref[186:188, :] = value[8:10]
    grad_square = jnp.sum(square_sum)
    ratio_ref[...] = jnp.full((1, LANES), jnp.sum(band_sum) / (grad_square + epsilon), F32)
    spread_square = jnp.full((1, LANES), grad_square / PARAMS + epsilon, F32)
    scale = learn_rate / jnp.sqrt(spread_square)
    params_ref[...] = base_params[0:188, :] - scale * total_ref[0:188, :] + noise_in[...]

    for copy in halos + scatters + exchanges + collects:
        copy.wait_send()


def emit(final_in, adjoint_in, params_in, ratio_in, final_out, adjoint_out, params_out, ratio_out, sem):
    pairs = ((final_in, final_out), (adjoint_in, adjoint_out), (params_in, params_out))
    copies = [pltpu.make_async_copy(src, dst, sem.at[n]) for n, (src, dst) in enumerate(pairs)]
    for copy in copies:
        copy.start()
    ratio_out[0] = ratio_in[0, 0]
    for copy in copies:
        copy.wait()


def on_device(
    initial_state,
    diffusion,
    mixing,
    land_mask,
    first_layer,
    second_layer,
    output_layer,
    cotangent,
    update_noise,
):
    vmem = pltpu.VMEM
    flat8 = vmem((8, FLAT), F32)
    hidden = vmem((HID, FLAT), BF16)
    dma = pltpu.SemaphoreType.DMA
    scratch = [
        vmem((FIELDS, ROWS, COLS), F32),
        vmem((ROWS, COLS), F32),
        vmem((ROWS, COLS), jnp.int32),
        vmem((FIELDS, ROWS, COLS), F32),
        vmem((188, LANES), F32),
        pltpu.SMEM((FIELDS, FIELDS), F32),
        vmem((PATCH, HID), BF16),
        vmem((HID, HID), BF16),
        vmem((FIELDS, HID), BF16),
        dma((9,)),
        vmem((ROWS, 8, LANES), F32),
        vmem((ROWS, 8, LANES), F32),
        vmem((6, 8, LANES), F32),
        vmem((6, 8, LANES), F32),
        vmem((2, 8, LANES), F32),
        vmem((6, 8, LANES), F32),
        vmem((6, 8, LANES), F32),
        vmem((6, 2, 8, LANES), F32),
        dma((8,)),
        dma((8,)),
        flat8,
        flat8,
        hidden,
        flat8,
        flat8,
        flat8,
        flat8,
        flat8,
        vmem((DEEP, FLAT), BF16),
        vmem((DEEP, FLAT), BF16),
        hidden,
        hidden,
        hidden,
        hidden,
        hidden,
        hidden,
        vmem((16, FLAT), BF16),
        vmem((72, FLAT), F32),
        flat8,
        vmem((HID, LANES), F32),
        vmem((16, LANES), F32),
        vmem((192, LANES), F32),
        vmem((NLON, CHUNK, LANES), F32),
        vmem((NLON - 1, CHUNK, LANES), F32),
        vmem((NLAT, CHUNK, LANES), F32),
        vmem((NLON, 16, LANES), F32),
        vmem((192, LANES), F32),
        dma((NLON - 1,)),
        dma((NLON - 1,)),
        dma((NLAT - 1,)),
        dma((NLAT - 1,)),
        dma((NLON - 1,)),
        dma((NLON - 1,)),
    ]
    hbm = pl.BlockSpec(memory_space=pltpu.HBM)
    local = pl.BlockSpec(memory_space=pltpu.VMEM)
    final, adjoint, params, ratio = pl.pallas_call(
        kernel,
        out_shape=(
            jax.ShapeDtypeStruct((FIELDS, ROWS, COLS), F32),
            jax.ShapeDtypeStruct((FIELDS, ROWS, COLS), F32),
            jax.ShapeDtypeStruct((188, LANES), F32),
            jax.ShapeDtypeStruct((1, LANES), F32),
        ),
        in_specs=[hbm] * 9,
        out_specs=(local,) * 4,
        scratch_shapes=scratch,
        compiler_params=pltpu.CompilerParams(
            collective_id=0, has_side_effects=True, vmem_limit_bytes=40 * 1024 * 1024
        ),
        name="ocean",
    )(
        *(
            pltpu.with_memory_space_constraint(value, pltpu.HBM)
            for value in (
                initial_state,
                diffusion,
                mixing,
                land_mask,
                first_layer.T,
                second_layer,
                output_layer,
                cotangent,
                update_noise.reshape(188, LANES),
            )
        )
    )
    final, adjoint, params, ratio = pl.pallas_call(
        emit,
        out_shape=(
            jax.ShapeDtypeStruct((FIELDS, ROWS, COLS), F32),
            jax.ShapeDtypeStruct((FIELDS, ROWS, COLS), F32),
            jax.ShapeDtypeStruct((188, LANES), F32),
            jax.ShapeDtypeStruct((1,), F32),
        ),
        in_specs=[local] * 4,
        out_specs=(hbm, hbm, hbm, pl.BlockSpec(memory_space=pltpu.SMEM)),
        scratch_shapes=[dma((3,))],
        name="emit",
    )(*(pltpu.with_memory_space_constraint(value, pltpu.VMEM) for value in (final, adjoint, params, ratio)))
    return final, adjoint, params.reshape(PARAMS), ratio


def solution(mesh):
    placed = (
        P("ens", "lat", "lon"),
        P("lat", "lon"),
        P(),
        P("lat", "lon"),
        P(),
        P(),
        P(),
        P("ens", "lat", "lon"),
        P("ens"),
    )
    return jax.shard_map(
        on_device,
        mesh=mesh,
        in_specs=placed,
        out_specs=(P("ens", "lat", "lon"), P("ens", "lat", "lon"), P("ens"), P("ens")),
        check_vma=False,
    )
```

```python
import functools
import math
from types import SimpleNamespace

import jax
import jax.numpy as jnp
from jax import lax
from jax.experimental import pallas as pl
from jax.experimental.pallas import tpu as pltpu
from jax.sharding import PartitionSpec as P

MESH = pl.DeviceIdType.MESH
F32 = jnp.float32
BF16 = jnp.bfloat16

closure_dt = 0.1
learn_rate = 0.1
epsilon = 1e-06
offsets = [(p, q) for p in (-1, 0, 1) for q in (-1, 0, 1)]

FIELDS, ROWS, COLS = 6, 16, 128
HALO = 4
PITCH = COLS + 2 * HALO
EXT = ROWS + 2 * HALO
LANES = 128
TILES = -(-EXT * PITCH // LANES)
FLAT = TILES * LANES
HID = 128
PATCH = 54
DEEP = 80
PARAMS = 24064
NLON, NLAT = 16, 8
CHUNK = 12


def ring(index, step, size):
    return lax.rem(index + step + size, size)


def tile_range(distance):
    low = (HALO - distance) * PITCH // LANES
    high = -(-(HALO + ROWS + distance) * PITCH // LANES)
    if (high - low) % 2:
        low, high = (low, high + 1) if high < TILES else (low - 1, high)
    return low * LANES, high * LANES


def chunks(low, high, size=4096):
    return [(start, min(size, high - start)) for start in range(low, high, size)]


def spread_lanes(tile, length):
    return jnp.concatenate([tile] * (length // LANES), axis=1)


def segments(tile):
    found = []
    base = tile * LANES
    for row in range(EXT):
        start = row * PITCH
        for part, low, high in (
            ("left", start, start + HALO),
            ("main", start + HALO, start + HALO + COLS),
            ("right", start + HALO + COLS, start + PITCH),
        ):
            first, end = max(low, base), min(high, base + LANES)
            if first < end:
                found.append((first - base, end - base, row, part))
    return found


def kernel(
    state_hbm,
    diff_hbm,
    mix_hbm,
    mask_hbm,
    first_hbm,
    second_hbm,
    output_hbm,
    cot_hbm,
    noise_hbm,
    final_ref,
    adjoint_ref,
    params_ref,
    ratio_ref,
    state_in,
    diff_in,
    mask_in,
    cot_in,
    noise_in,
    mix_ref,
    first_ref,
    second_ref,
    output_ref,
    load_sem,
    own_a,
    own_b,
    send_north,
    send_south,
    edge,
    from_north,
    from_south,
    edges_in,
    halo_send,
    halo_recv,
    flat_a,
    flat_b,
    own_ref,
    wide_mask,
    wide_diff,
    state_one,
    state_two,
    lap_ref,
    patch_zero,
    patch_one,
    hid_one_zero,
    hid_two_zero,
    hid_one_one,
    hid_two_one,
    back_one,
    back_two,
    out_grad,
    patch_grad,
    adj_one,
    weights_one,
    weights_three,
    base_params,
    grads,
    recv_one,
    recv_two,
    gathered,
    total_ref,
    send_one_sem,
    recv_one_sem,
    send_two_sem,
    recv_two_sem,
    send_three_sem,
    recv_three_sem,
):
    lat = lax.axis_index("lat")
    lon = lax.axis_index("lon")
    north, south = ring(lat, -1, NLAT), ring(lat, 1, NLAT)
    west, east = ring(lon, -1, NLON), ring(lon, 1, NLON)

    barrier = pltpu.get_barrier_semaphore()
    greet = [{"lon": ring(lon, d, NLON)} for d in range(1, NLON)]
    greet += [{"lat": ring(lat, d, NLAT)} for d in range(1, NLAT)]
    greet += [{"lat": a, "lon": b} for a in (north, south) for b in (west, east)]
    for device in greet:
        pl.semaphore_signal(barrier, inc=1, device_id=device, device_id_type=MESH)

    loads = [
        pltpu.make_async_copy(src, dst, load_sem.at[n])
        for n, (src, dst) in enumerate(
            (
                (state_hbm, state_in),
                (mask_hbm, mask_in),
                (diff_hbm, diff_in),
                (cot_hbm, cot_in),
                (mix_hbm, mix_ref),
                (first_hbm, first_ref),
                (second_hbm, second_ref),
                (output_hbm, output_ref),
                (noise_hbm, noise_in),
            )
        )
    ]
    for load in loads:
        load.start()

    lane = lax.broadcasted_iota(jnp.int32, (8, LANES), 1)
    sub = lax.broadcasted_iota(jnp.int32, (8, LANES), 0)
    for load in loads[:4]:
        load.wait()

    own_b[...] = jnp.zeros_like(own_b)
    for r in range(ROWS):
        own_a[r, 0:FIELDS, :] = state_in[:, r, :]
        own_a[r, 6:7, :] = mask_in[r : r + 1, :].astype(F32)
        own_a[r, 7:8, :] = diff_in[r : r + 1, :]
        own_b[r, 0:FIELDS, :] = cot_in[:, r, :]
    edge_a = jnp.zeros((8, LANES), F32)
    edge_b = jnp.zeros((8, LANES), F32)
    for r in range(ROWS):
        j = r + HALO
        turn = (j * PITCH + HALO) % LANES
        tile_a = pltpu.roll(own_a[r], turn, 1)
        tile_b = pltpu.roll(own_b[r], turn, 1)
        own_a[r] = tile_a
        own_b[r] = tile_b
        place = (j * PITCH) % LANES
        pick = (lane >= place) & (lane < place + 2 * HALO)
        edge_a = jnp.where(pick, tile_a, edge_a)
        edge_b = jnp.where(pick, tile_b, edge_b)
        if r < HALO:
            send_north[r] = tile_a
        if r < 2:
            send_north[HALO + r] = tile_b
        if r >= ROWS - HALO:
            send_south[r - (ROWS - HALO)] = tile_a
        if r >= ROWS - 2:
            send_south[HALO + r - (ROWS - 2)] = tile_b
    edge[0] = edge_a
    edge[1] = edge_b

    pl.semaphore_wait(barrier, len(greet))

    def halo_copy(n, source, target, device):
        return pltpu.make_async_remote_copy(
            src_ref=source,
            dst_ref=target,
            send_sem=halo_send.at[n],
            recv_sem=halo_recv.at[n],
            device_id=device,
            device_id_type=MESH,
        )

    halos = [
        halo_copy(0, send_north, from_south, {"lat": north}),
        halo_copy(1, send_south, from_north, {"lat": south}),
        halo_copy(2, edge, edges_in.at[0], {"lat": south, "lon": east}),
        halo_copy(3, edge, edges_in.at[1], {"lon": east}),
        halo_copy(4, edge, edges_in.at[2], {"lat": north, "lon": east}),
        halo_copy(5, edge, edges_in.at[3], {"lat": south, "lon": west}),
        halo_copy(6, edge, edges_in.at[4], {"lon": west}),
        halo_copy(7, edge, edges_in.at[5], {"lat": north, "lon": west}),
    ]
    for copy in halos:
        copy.start()

    for load in loads[4:8]:
        load.wait()
    weights_one[...] = jnp.zeros_like(weights_one)
    weights_one[0:PATCH, :] = first_ref[...].astype(F32)
    weights_three[...] = jnp.zeros_like(weights_three)
    weights_three[0:FIELDS, :] = output_ref[...].astype(F32)

    def nt(left, right, precision=None):
        return lax.dot_general(
            left, right, (((1,), (1,)), ((), ())), preferred_element_type=F32, precision=precision
        )

    deep_i = lax.broadcasted_iota(jnp.int32, (DEEP, HID), 0)
    deep_j = lax.broadcasted_iota(jnp.int32, (DEEP, HID), 1)
    deep_f = lax.bitwise_and(deep_i, 7)
    picked = (deep_j == 6 * lax.shift_right_logical(deep_i, 3) + deep_f) & (deep_f < 6) & (deep_i < 72)
    select_f = jnp.where(picked, 1.0, 0.0).astype(F32)
    select = select_f.astype(BF16)
    row = lax.broadcasted_iota(jnp.int32, (HID, HID), 0)
    column = lax.broadcasted_iota(jnp.int32, (HID, HID), 1)
    eye = jnp.where(row == column, 1.0, 0.0).astype(BF16)
    turned_one = weights_one[...].astype(BF16)
    plain_one = nt(eye, turned_one).astype(BF16)
    w1 = nt(plain_one, select).astype(BF16)
    w1_t = jnp.dot(select, turned_one, preferred_element_type=F32).astype(BF16)
    w2 = second_ref[...]
    w2_t = nt(eye, w2).astype(BF16)
    w3 = weights_three[...].astype(BF16)
    w3_t = nt(eye, w3).astype(BF16)

    turn_of = lax.bitwise_and(row * PATCH, LANES - 1)
    deep_r = lax.broadcasted_iota(jnp.int32, (56, 2 * HID), 0)
    deep_h = lax.broadcasted_iota(jnp.int32, (56, 2 * HID), 1)
    hid_h = lax.bitwise_and(deep_h, HID - 1)
    lands = lax.shift_right_logical(hid_h * PATCH, 7) + lax.shift_right_logical(deep_h, 7)
    gather_rows = jnp.where(lands == deep_r, 1.0, 0.0).astype(F32)

    def flatten_rows(value, exact):
        for bit in range(1, 7):
            moved = pltpu.roll(value, 1 << bit, 1)
            chosen = lax.bitwise_and(lax.shift_right_logical(turn_of, bit), 1) == 1
            value = jnp.where(chosen, moved, value)
        ahead = jnp.where(column >= turn_of, value, 0.0)
        behind = jnp.where(column < turn_of, value, 0.0)
        both = jnp.concatenate([ahead, behind], axis=0)
        if exact:
            return jnp.dot(
                gather_rows, both, preferred_element_type=F32, precision=lax.Precision.HIGHEST
            )
        return jnp.dot(gather_rows.astype(BF16), both.astype(BF16), preferred_element_type=F32)

    base_params[0:56, :] = flatten_rows(plain_one.astype(F32), False)
    base_params[54:182, :] = w2.astype(F32)
    base_params[182:188, :] = output_ref[...].astype(F32)

    for t in range(TILES):
        own = jnp.zeros((8, LANES), F32)
        for first, end, j, part in segments(t):
            if part == "main" and HALO <= j < HALO + ROWS:
                own = jnp.where((lane >= first) & (lane < end), 1.0, own)
        own_ref[:, t * LANES : (t + 1) * LANES] = jnp.concatenate([own] * (HID // 8), axis=0).astype(BF16)

    mix_to = []
    mix_from = []
    for g in range(FIELDS):
        to_tile = jnp.zeros((8, LANES), F32)
        from_tile = jnp.zeros((8, LANES), F32)
        for f in range(FIELDS):
            to_tile = jnp.where(sub == f, mix_ref[f, g], to_tile)
            from_tile = jnp.where(sub == f, mix_ref[g, f], from_tile)
        mix_to.append(to_tile)
        mix_from.append(from_tile)

    def mixed(tiles, value):
        length = value.shape[1]
        total = None
        for g in range(FIELDS):
            term = spread_lanes(tiles[g], length) * jnp.broadcast_to(value[g : g + 1, :], (8, length))
            total = term if total is None else total + term
        return total

    for copy in halos:
        copy.wait_recv()

    def top(value):
        return jnp.where(lat > 0, value, 0.0)

    def bottom(value):
        return jnp.where(lat < NLAT - 1, value, 0.0)

    blank = jnp.zeros((8, LANES), F32)
    sides = []
    for which in range(2):
        sides.append(
            {
                "left": (top(edges_in[0, which]), edges_in[1, which], bottom(edges_in[2, which])),
                "right": (top(edges_in[3, which]), edges_in[4, which], bottom(edges_in[5, which])),
            }
        )

    def source(which, j, part):
        if which == 1 and (j < 2 or j >= EXT - 2):
            return blank
        if part != "main":
            return sides[which][part][0 if j < HALO else 1 if j < HALO + ROWS else 2]
        if j < HALO:
            return top(from_north[j if which == 0 else HALO + j - 2])
        if j < HALO + ROWS:
            return (own_a if which == 0 else own_b)[j - HALO]
        return bottom(from_south[(j - HALO - ROWS) if which == 0 else HALO + j - HALO - ROWS])

    for t in range(TILES):
        here = slice(t * LANES, (t + 1) * LANES)
        for which, target in ((0, flat_a), (1, flat_b)):
            value = blank
            for first, end, j, part in segments(t):
                piece = source(which, j, part)
                value = jnp.where((lane >= first) & (lane < end), piece, value)
            target[:, here] = value
            if which == 0:
                wide_mask[:, here] = jnp.broadcast_to(value[6:7, :], (8, LANES))
                wide_diff[:, here] = jnp.broadcast_to(value[7:8, :], (8, LANES))

    def shift(value, amount):
        return pltpu.roll(value, (-amount) % FLAT, 1)

    def make_patch(value, patch_ref):
        blocks = [value if (p, q) == (0, 0) else shift(value, p * PITCH + q) for p, q in offsets]
        for m in range(5):
            after = blocks[2 * m + 1] if m < 4 else jnp.zeros_like(value)
            patch_ref[16 * m : 16 * m + 16, :] = jnp.concatenate([blocks[2 * m], after], axis=0).astype(BF16)
        lap_ref[...] = blocks[1] + blocks[7] + blocks[3] + blocks[5] - 4.0 * value

    def forward(state_ref, patch_ref, one_ref, two_ref, next_ref, low, high, write_low, write_high):
        for start, size in chunks(low, high):
            here = slice(start, start + size)
            one = jnp.tanh(jnp.dot(w1, patch_ref[:, here], preferred_element_type=F32)).astype(BF16)
            one_ref[:, here] = one
            two = jnp.tanh(jnp.dot(w2, one, preferred_element_type=F32)).astype(BF16)
            two_ref[:, here] = two
            tendency = jnp.dot(w3, two, preferred_element_type=F32)[0:8]
            centre = state_ref[:, here]
            update = (
                centre
                + wide_diff[:, here] * lap_ref[:, here]
                + (mixed(mix_to, centre) + closure_dt * tendency)
            )
            next_ref[:, here] = wide_mask[:, here] * update

    state_one[...] = jnp.zeros_like(state_one)
    make_patch(flat_a[...], patch_zero)
    low, high = tile_range(3)
    forward(flat_a, patch_zero, hid_one_zero, hid_two_zero, state_one, low, high, low, high)
    make_patch(state_one[...], patch_one)
    low, high = tile_range(2)
    forward(state_one, patch_one, hid_one_one, hid_two_one, state_two, low, high, low, high)

    def write_rows(source_ref, target_ref):
        for r in range(ROWS):
            start = (r + HALO) * PITCH + HALO
            t, turn = start // LANES, start % LANES
            before = source_ref[:, t * LANES : (t + 1) * LANES]
            after = source_ref[:, (t + 1) * LANES : (t + 2) * LANES]
            value = pltpu.roll(jnp.where(lane >= turn, before, after), (LANES - turn) % LANES, 1)
            target_ref[:, r, :] = value[0:FIELDS]

    grad_low, grad_high = tile_range(0)
    grad_here = slice(grad_low, grad_high)

    def backward(adj_ref, patch_ref, one_ref, two_ref, low, high):
        for start, size in chunks(low, high):
            here = slice(start, start + size)
            masked = wide_mask[:, here] * adj_ref[:, here]
            low_grad = jnp.concatenate([closure_dt * masked, jnp.zeros_like(masked)], axis=0).astype(BF16)
            out_grad[:, here] = low_grad
            two = two_ref[:, here].astype(F32)
            grad_two = (
                jnp.dot(w3_t, low_grad, preferred_element_type=F32) * (1.0 - two * two)
            ).astype(BF16)
            back_two[:, here] = grad_two
            one = one_ref[:, here].astype(F32)
            grad_one = (
                jnp.dot(w2_t, grad_two, preferred_element_type=F32) * (1.0 - one * one)
            ).astype(BF16)
            back_one[:, here] = grad_one
            grad_zero = jnp.dot(w1_t, grad_one, preferred_element_type=F32)
            spread = wide_diff[:, here] * masked
            direct = masked + mixed(mix_from, masked) - 4.0 * spread
            for k in range(9):
                block = grad_zero[8 * k : 8 * k + 8]
                if k == 4:
                    block = block + direct
                elif k % 2:
                    block = block + spread
                patch_grad[8 * k : 8 * k + 8, here] = block
        own = own_ref[:, grad_here]
        grad_first = nt(back_one[:, grad_here], patch_ref[:, grad_here] * own[0:DEEP])
        grad_second = nt(back_two[:, grad_here], one_ref[:, grad_here] * own)
        grad_output = nt(out_grad[:, grad_here] * own[0:16], two_ref[:, grad_here])
        return grad_first, grad_second, grad_output

    def scatter():
        total = None
        for k, (p, q) in enumerate(offsets):
            block = patch_grad[8 * k : 8 * k + 8, :]
            if (p, q) != (0, 0):
                block = shift(block, -(p * PITCH + q))
            total = block if total is None else total + block
        return total

    patch_grad[...] = jnp.zeros_like(patch_grad)
    low, high = tile_range(2)
    late_first, late_second, late_output = backward(flat_b, patch_one, hid_one_one, hid_two_one, low, high)
    adj_one[...] = scatter()
    low, high = tile_range(1)
    first, second, output = backward(adj_one, patch_zero, hid_one_zero, hid_two_zero, low, high)
    first = first + late_first
    second = second + late_second
    output = output + late_output

    narrow = jnp.dot(first, select_f, preferred_element_type=F32, precision=lax.Precision.HIGHEST)
    others = jnp.concatenate([flatten_rows(narrow, True), output[0:8]], axis=0)
    for i in range(NLON):
        grads[i, 0:8, :] = second[8 * i : 8 * i + 8]
        grads[i, 8:12, :] = others[4 * i : 4 * i + 4]

    scatters = []
    for d in range(1, NLON):
        peer = ring(lon, d, NLON)
        copy = pltpu.make_async_remote_copy(
            src_ref=grads.at[peer],
            dst_ref=recv_one.at[d - 1],
            send_sem=send_one_sem.at[d - 1],
            recv_sem=recv_one_sem.at[d - 1],
            device_id={"lon": peer},
            device_id_type=MESH,
        )
        copy.start()
        scatters.append(copy)

    write_rows(state_two, final_ref)
    adj_one[...] = scatter()
    write_rows(adj_one, adjoint_ref)

    band = grads[lon]
    for d in range(1, NLON):
        scatters[d - 1].wait_recv()
        band = band + recv_one[d - 1]
    recv_two[lat] = band

    exchanges = []
    for d in range(1, NLAT):
        peer = ring(lat, d, NLAT)
        copy = pltpu.make_async_remote_copy(
            src_ref=recv_two.at[lat],
            dst_ref=recv_two.at[lat],
            send_sem=send_two_sem.at[d - 1],
            recv_sem=recv_two_sem.at[d - 1],
            device_id={"lat": peer},
            device_id_type=MESH,
        )
        copy.start()
        exchanges.append(copy)
    for copy in exchanges:
        copy.wait_recv()
    total = recv_two[0]
    squares = total * total
    for b in range(1, NLAT):
        value = recv_two[b]
        total = total + value
        squares = squares + value * value
    gathered[lon, 0:CHUNK, :] = total
    gathered[lon, CHUNK:16, :] = jnp.broadcast_to(jnp.sum(squares, axis=0, keepdims=True), (16 - CHUNK, LANES))

    collects = []
    for d in range(1, NLON):
        peer = ring(lon, d, NLON)
        copy = pltpu.make_async_remote_copy(
            src_ref=gathered.at[lon],
            dst_ref=gathered.at[lon],
            send_sem=send_three_sem.at[d - 1],
            recv_sem=recv_three_sem.at[d - 1],
            device_id={"lon": peer},
            device_id_type=MESH,
        )
        copy.start()
        collects.append(copy)
    loads[8].wait()
    for copy in collects:
        copy.wait_recv()

    square_sum = jnp.zeros((CHUNK, LANES), F32)
    band_sum = jnp.zeros((1, LANES), F32)
    for i in range(NLON):
        value = gathered[i, 0:CHUNK, :]
        square_sum = square_sum + value * value
        band_sum = band_sum + gathered[i, CHUNK : CHUNK + 1, :]
        total_ref[54 + 8 * i : 62 + 8 * i, :] = value[0:8]
        if i < 13:
            total_ref[4 * i : 4 * i + 4, :] = value[8:12]
        elif i == 13:
            total_ref[52:54, :] = value[8:10]
        elif i == 14:
            total_ref[182:186, :] = value[8:12]
        else:
            total_ref[186:188, :] = value[8:10]
    grad_square = jnp.sum(square_sum)
    ratio_ref[...] = jnp.full((1, LANES), jnp.sum(band_sum) / (grad_square + epsilon), F32)
    spread_square = jnp.full((1, LANES), grad_square / PARAMS + epsilon, F32)
    scale = learn_rate / jnp.sqrt(spread_square)
    params_ref[...] = base_params[0:188, :] - scale * total_ref[0:188, :] + noise_in[...]

    for copy in halos + scatters + exchanges + collects:
        copy.wait_send()


def emit(final_in, adjoint_in, params_in, ratio_in, final_out, adjoint_out, params_out, ratio_out, sem):
    pairs = ((final_in, final_out), (adjoint_in, adjoint_out), (params_in, params_out))
    copies = [pltpu.make_async_copy(src, dst, sem.at[n]) for n, (src, dst) in enumerate(pairs)]
    for copy in copies:
        copy.start()
    ratio_out[0] = ratio_in[0, 0]
    for copy in copies:
        copy.wait()


def on_device(
    initial_state,
    diffusion,
    mixing,
    land_mask,
    first_layer,
    second_layer,
    output_layer,
    cotangent,
    update_noise,
):
    vmem = pltpu.VMEM
    flat8 = vmem((8, FLAT), F32)
    hidden = vmem((HID, FLAT), BF16)
    dma = pltpu.SemaphoreType.DMA
    scratch = [
        vmem((FIELDS, ROWS, COLS), F32),
        vmem((ROWS, COLS), F32),
        vmem((ROWS, COLS), jnp.int32),
        vmem((FIELDS, ROWS, COLS), F32),
        vmem((188, LANES), F32),
        pltpu.SMEM((FIELDS, FIELDS), F32),
        vmem((PATCH, HID), BF16),
        vmem((HID, HID), BF16),
        vmem((FIELDS, HID), BF16),
        dma((9,)),
        vmem((ROWS, 8, LANES), F32),
        vmem((ROWS, 8, LANES), F32),
        vmem((6, 8, LANES), F32),
        vmem((6, 8, LANES), F32),
        vmem((2, 8, LANES), F32),
        vmem((6, 8, LANES), F32),
        vmem((6, 8, LANES), F32),
        vmem((6, 2, 8, LANES), F32),
        dma((8,)),
        dma((8,)),
        flat8,
        flat8,
        hidden,
        flat8,
        flat8,
        flat8,
        flat8,
        flat8,
        vmem((DEEP, FLAT), BF16),
        vmem((DEEP, FLAT), BF16),
        hidden,
        hidden,
        hidden,
        hidden,
        hidden,
        hidden,
        vmem((16, FLAT), BF16),
        vmem((72, FLAT), F32),
        flat8,
        vmem((HID, LANES), F32),
        vmem((16, LANES), F32),
        vmem((192, LANES), F32),
        vmem((NLON, CHUNK, LANES), F32),
        vmem((NLON - 1, CHUNK, LANES), F32),
        vmem((NLAT, CHUNK, LANES), F32),
        vmem((NLON, 16, LANES), F32),
        vmem((192, LANES), F32),
        dma((NLON - 1,)),
        dma((NLON - 1,)),
        dma((NLAT - 1,)),
        dma((NLAT - 1,)),
        dma((NLON - 1,)),
        dma((NLON - 1,)),
    ]
    hbm = pl.BlockSpec(memory_space=pltpu.HBM)
    local = pl.BlockSpec(memory_space=pltpu.VMEM)
    final, adjoint, params, ratio = pl.pallas_call(
        kernel,
        out_shape=(
            jax.ShapeDtypeStruct((FIELDS, ROWS, COLS), F32),
            jax.ShapeDtypeStruct((FIELDS, ROWS, COLS), F32),
            jax.ShapeDtypeStruct((188, LANES), F32),
            jax.ShapeDtypeStruct((1, LANES), F32),
        ),
        in_specs=[hbm] * 9,
        out_specs=(local,) * 4,
        scratch_shapes=scratch,
        compiler_params=pltpu.CompilerParams(
            collective_id=0, has_side_effects=True, vmem_limit_bytes=40 * 1024 * 1024
        ),
        name="ocean",
    )(
        *(
            pltpu.with_memory_space_constraint(value, pltpu.HBM)
            for value in (
                initial_state,
                diffusion,
                mixing,
                land_mask,
                first_layer.T,
                second_layer,
                output_layer,
                cotangent,
                update_noise.reshape(188, LANES),
            )
        )
    )
    final, adjoint, params, ratio = pl.pallas_call(
        emit,
        out_shape=(
            jax.ShapeDtypeStruct((FIELDS, ROWS, COLS), F32),
            jax.ShapeDtypeStruct((FIELDS, ROWS, COLS), F32),
            jax.ShapeDtypeStruct((188, LANES), F32),
            jax.ShapeDtypeStruct((1,), F32),
        ),
        in_specs=[local] * 4,
        out_specs=(hbm, hbm, hbm, pl.BlockSpec(memory_space=pltpu.SMEM)),
        scratch_shapes=[dma((3,))],
        name="emit",
    )(*(pltpu.with_memory_space_constraint(value, pltpu.VMEM) for value in (final, adjoint, params, ratio)))
    return final, adjoint, params.reshape(PARAMS), ratio


def solution(mesh):
    placed = (
        P("ens", "lat", "lon"),
        P("lat", "lon"),
        P(),
        P("lat", "lon"),
        P(),
        P(),
        P(),
        P("ens", "lat", "lon"),
        P("ens"),
    )
    return jax.shard_map(
        on_device,
        mesh=mesh,
        in_specs=placed,
        out_specs=(P("ens", "lat", "lon"), P("ens", "lat", "lon"), P("ens"), P("ens")),
        check_vma=False,
    )
```

```python
import functools
import math
from types import SimpleNamespace

import jax
import jax.numpy as jnp
from jax import lax
from jax.experimental import pallas as pl
from jax.experimental.pallas import tpu as pltpu
from jax.sharding import PartitionSpec as P

MESH = pl.DeviceIdType.MESH
F32 = jnp.float32
BF16 = jnp.bfloat16

closure_dt = 0.1
learn_rate = 0.1
epsilon = 1e-06
offsets = [(p, q) for p in (-1, 0, 1) for q in (-1, 0, 1)]

FIELDS, ROWS, COLS = 6, 16, 128
HALO = 4
PITCH = COLS + 2 * HALO
EXT = ROWS + 2 * HALO
LANES = 128
TILES = -(-EXT * PITCH // LANES)
FLAT = TILES * LANES
HID = 128
PATCH = 54
DEEP = 80
PARAMS = 24064
NLON, NLAT = 16, 8
CHUNK = 12
SENT = CHUNK + 1
LON_STEPS = (8, 7, 9, 6, 10, 5, 11, 4, 12, 3, 13, 2, 14, 1, 15)
LAT_STEPS = (2, 6, 1, 3, 5, 7, 4)


def ring(index, step, size):
    return lax.rem(index + step + size, size)


def tile_range(distance):
    low = (HALO - distance) * PITCH // LANES
    high = -(-(HALO + ROWS + distance) * PITCH // LANES)
    if (high - low) % 2:
        low, high = (low, high + 1) if high < TILES else (low - 1, high)
    return low * LANES, high * LANES


def chunks(low, high, size=4096):
    return [(start, min(size, high - start)) for start in range(low, high, size)]


def spread_lanes(tile, length):
    return jnp.concatenate([tile] * (length // LANES), axis=1)


def segments(tile):
    found = []
    base = tile * LANES
    for row in range(EXT):
        start = row * PITCH
        for part, low, high in (
            ("left", start, start + HALO),
            ("main", start + HALO, start + HALO + COLS),
            ("right", start + HALO + COLS, start + PITCH),
        ):
            first, end = max(low, base), min(high, base + LANES)
            if first < end:
                found.append((first - base, end - base, row, part))
    return found


def kernel(
    state_hbm,
    diff_hbm,
    mix_hbm,
    mask_hbm,
    first_hbm,
    second_hbm,
    output_hbm,
    cot_hbm,
    noise_hbm,
    final_ref,
    adjoint_ref,
    params_ref,
    ratio_ref,
    state_in,
    diff_in,
    mask_in,
    cot_in,
    noise_in,
    mix_ref,
    first_ref,
    second_ref,
    output_ref,
    load_sem,
    own_a,
    own_b,
    send_north,
    send_south,
    edge,
    halo_in,
    send_sem,
    recv_sem,
    flat_a,
    flat_b,
    own_ref,
    wide_mask,
    wide_diff,
    state_one,
    state_two,
    lap_ref,
    patch_zero,
    patch_one,
    hid_one_zero,
    hid_two_zero,
    hid_one_one,
    hid_two_one,
    back_one,
    back_two,
    out_grad,
    patch_grad,
    adj_one,
    weights_one,
    weights_three,
    base_params,
    grads,
    recv_one,
    recv_two,
    gathered,
    total_ref,
):
    lat = lax.axis_index("lat")
    lon = lax.axis_index("lon")
    north, south = ring(lat, -1, NLAT), ring(lat, 1, NLAT)
    west, east = ring(lon, -1, NLON), ring(lon, 1, NLON)

    barrier = pltpu.get_barrier_semaphore()
    corners = [{"lat": a, "lon": b} for a in (north, south) for b in (west, east)]
    greet = [{"lon": ring(lon, d, NLON)} for d in LON_STEPS[:5]] + corners
    greet += [{"lat": ring(lat, d, NLAT)} for d in LAT_STEPS]
    greet += [{"lon": ring(lon, d, NLON)} for d in LON_STEPS[5:]]
    for device in greet:
        pl.semaphore_signal(barrier, inc=1, device_id=device, device_id_type=MESH)

    loads = [
        pltpu.make_async_copy(src, dst, load_sem.at[n])
        for n, (src, dst) in enumerate(
            (
                (state_hbm, state_in),
                (mask_hbm, mask_in),
                (diff_hbm, diff_in),
                (cot_hbm, cot_in),
                (mix_hbm, mix_ref),
                (first_hbm, first_ref),
                (second_hbm, second_ref),
                (output_hbm, output_ref),
                (noise_hbm, noise_in),
            )
        )
    ]
    for load in loads:
        load.start()

    lane = lax.broadcasted_iota(jnp.int32, (8, LANES), 1)
    sub = lax.broadcasted_iota(jnp.int32, (8, LANES), 0)
    for load in loads[:4]:
        load.wait()

    own_b[...] = jnp.zeros_like(own_b)
    for r in range(ROWS):
        own_a[r, 0:FIELDS, :] = state_in[:, r, :]
        own_a[r, 6:7, :] = mask_in[r : r + 1, :].astype(F32)
        own_a[r, 7:8, :] = diff_in[r : r + 1, :]
        own_b[r, 0:FIELDS, :] = cot_in[:, r, :]
    edge_a = jnp.zeros((8, LANES), F32)
    edge_b = jnp.zeros((8, LANES), F32)
    for r in range(ROWS):
        j = r + HALO
        turn = (j * PITCH + HALO) % LANES
        tile_a = pltpu.roll(own_a[r], turn, 1)
        tile_b = pltpu.roll(own_b[r], turn, 1)
        own_a[r] = tile_a
        own_b[r] = tile_b
        place = (j * PITCH) % LANES
        pick = (lane >= place) & (lane < place + 2 * HALO)
        edge_a = jnp.where(pick, tile_a, edge_a)
        edge_b = jnp.where(pick, tile_b, edge_b)
        if r < HALO:
            send_north[r] = tile_a
        if r < 2:
            send_north[HALO + r] = tile_b
        if r >= ROWS - HALO:
            send_south[r - (ROWS - HALO)] = tile_a
        if r >= ROWS - 2:
            send_south[HALO + r - (ROWS - 2)] = tile_b
    edge[0] = edge_a
    edge[1] = edge_b

    pl.semaphore_wait(barrier, len(greet))

    def halo_copy(source, target, device):
        return pltpu.make_async_remote_copy(
            src_ref=source,
            dst_ref=target,
            send_sem=send_sem.at[0],
            recv_sem=recv_sem.at[0],
            device_id=device,
            device_id_type=MESH,
        )

    from_north, from_south = halo_in.at[0:6], halo_in.at[6:12]
    edges_in = [halo_in.at[12 + 2 * n : 14 + 2 * n] for n in range(6)]
    halos = [
        halo_copy(edge, edges_in[0], {"lat": south, "lon": east}),
        halo_copy(edge, edges_in[2], {"lat": north, "lon": east}),
        halo_copy(edge, edges_in[3], {"lat": south, "lon": west}),
        halo_copy(edge, edges_in[5], {"lat": north, "lon": west}),
        halo_copy(send_north, from_south, {"lat": north}),
        halo_copy(send_south, from_north, {"lat": south}),
        halo_copy(edge, edges_in[1], {"lon": east}),
        halo_copy(edge, edges_in[4], {"lon": west}),
    ]
    for copy in halos:
        copy.start()

    for load in loads[4:8]:
        load.wait()
    weights_one[...] = jnp.zeros_like(weights_one)
    weights_one[0:PATCH, :] = first_ref[...].astype(F32)
    weights_three[...] = jnp.zeros_like(weights_three)
    weights_three[0:FIELDS, :] = output_ref[...].astype(F32)

    def nt(left, right, precision=None):
        return lax.dot_general(
            left, right, (((1,), (1,)), ((), ())), preferred_element_type=F32, precision=precision
        )

    deep_i = lax.broadcasted_iota(jnp.int32, (DEEP, HID), 0)
    deep_j = lax.broadcasted_iota(jnp.int32, (DEEP, HID), 1)
    deep_f = lax.bitwise_and(deep_i, 7)
    picked = (deep_j == 6 * lax.shift_right_logical(deep_i, 3) + deep_f) & (deep_f < 6) & (deep_i < 72)
    select = jnp.where(picked, 1.0, 0.0).astype(BF16)
    row = lax.broadcasted_iota(jnp.int32, (HID, HID), 0)
    column = lax.broadcasted_iota(jnp.int32, (HID, HID), 1)
    eye = jnp.where(row == column, 1.0, 0.0).astype(BF16)
    turned_one = weights_one[...].astype(BF16)
    plain_one = nt(eye, turned_one).astype(BF16)
    w1 = nt(plain_one, select).astype(BF16)
    w1_t = jnp.dot(select, turned_one, preferred_element_type=F32).astype(BF16)
    w2 = second_ref[...]
    w2_t = nt(eye, w2).astype(BF16)
    w3 = weights_three[...].astype(BF16)
    w3_t = nt(eye, w3).astype(BF16)

    turn_of = lax.bitwise_and(row * PATCH, LANES - 1)
    deep_r = lax.broadcasted_iota(jnp.int32, (56, 2 * HID), 0)
    deep_h = lax.broadcasted_iota(jnp.int32, (56, 2 * HID), 1)
    hid_h = lax.bitwise_and(deep_h, HID - 1)
    lands = lax.shift_right_logical(hid_h * PATCH, 7) + lax.shift_right_logical(deep_h, 7)
    gather_rows = jnp.where(lands == deep_r, 1.0, 0.0).astype(BF16)

    def halves(value):
        high = value.astype(BF16)
        return high, (value - high.astype(F32)).astype(BF16)

    def flatten_rows(value, exact):
        turned = []
        for m in range(HID // 8):
            tile = value[8 * m : 8 * m + 8]
            if (8 * m * PATCH) % LANES:
                tile = pltpu.roll(tile, (8 * m * PATCH) % LANES, 1)
            for _ in range(3):
                tile = pltpu.roll(tile, 0, 1, stride=PATCH // 3, stride_axis=0)
            turned.append(tile)
        value = jnp.concatenate(turned, axis=0)
        ahead = jnp.where(column >= turn_of, value, 0.0)
        behind = jnp.where(column < turn_of, value, 0.0)
        both = jnp.concatenate([ahead, behind], axis=0)
        if not exact:
            return jnp.dot(gather_rows, both.astype(BF16), preferred_element_type=F32)
        high, low = halves(both)
        return jnp.dot(gather_rows, high, preferred_element_type=F32) + jnp.dot(
            gather_rows, low, preferred_element_type=F32
        )

    base_params[0:56, :] = flatten_rows(plain_one.astype(F32), False)
    base_params[54:182, :] = w2.astype(F32)
    base_params[182:188, :] = output_ref[...].astype(F32)

    for t in range(TILES):
        own = jnp.zeros((8, LANES), F32)
        for first, end, j, part in segments(t):
            if part == "main" and HALO <= j < HALO + ROWS:
                own = jnp.where((lane >= first) & (lane < end), 1.0, own)
        own_ref[:, t * LANES : (t + 1) * LANES] = jnp.concatenate([own] * (HID // 8), axis=0).astype(BF16)

    mix_to = []
    mix_from = []
    for g in range(FIELDS):
        to_tile = jnp.zeros((8, LANES), F32)
        from_tile = jnp.zeros((8, LANES), F32)
        for f in range(FIELDS):
            to_tile = jnp.where(sub == f, mix_ref[f, g], to_tile)
            from_tile = jnp.where(sub == f, mix_ref[g, f], from_tile)
        mix_to.append(to_tile)
        mix_from.append(from_tile)

    def mixed(tiles, value):
        length = value.shape[1]
        total = None
        for g in range(FIELDS):
            term = spread_lanes(tiles[g], length) * jnp.broadcast_to(value[g : g + 1, :], (8, length))
            total = term if total is None else total + term
        return total

    all_halos = halo_copy(halo_in, halo_in, {"lon": east})
    all_halos.wait_recv()

    def top(value):
        return jnp.where(lat > 0, value, 0.0)

    def bottom(value):
        return jnp.where(lat < NLAT - 1, value, 0.0)

    blank = jnp.zeros((8, LANES), F32)
    sides = []
    for which in range(2):
        sides.append(
            {
                "left": (top(halo_in[12 + which]), halo_in[14 + which], bottom(halo_in[16 + which])),
                "right": (top(halo_in[18 + which]), halo_in[20 + which], bottom(halo_in[22 + which])),
            }
        )

    def source(which, j, part):
        if which == 1 and (j < 2 or j >= EXT - 2):
            return blank
        if part != "main":
            return sides[which][part][0 if j < HALO else 1 if j < HALO + ROWS else 2]
        if j < HALO:
            return top(halo_in[j if which == 0 else HALO + j - 2])
        if j < HALO + ROWS:
            return (own_a if which == 0 else own_b)[j - HALO]
        return bottom(halo_in[6 + (j - HALO - ROWS if which == 0 else j - ROWS)])

    for t in range(TILES):
        here = slice(t * LANES, (t + 1) * LANES)
        for which, target in ((0, flat_a), (1, flat_b)):
            value = blank
            for first, end, j, part in segments(t):
                piece = source(which, j, part)
                value = jnp.where((lane >= first) & (lane < end), piece, value)
            target[:, here] = value
            if which == 0:
                wide_mask[:, here] = jnp.broadcast_to(value[6:7, :], (8, LANES))
                wide_diff[:, here] = jnp.broadcast_to(value[7:8, :], (8, LANES))

    def shift(value, amount):
        return pltpu.roll(value, (-amount) % FLAT, 1)

    def make_patch(value, patch_ref):
        blocks = [value if (p, q) == (0, 0) else shift(value, p * PITCH + q) for p, q in offsets]
        for m in range(5):
            after = blocks[2 * m + 1] if m < 4 else jnp.zeros_like(value)
            patch_ref[16 * m : 16 * m + 16, :] = jnp.concatenate([blocks[2 * m], after], axis=0).astype(BF16)
        lap_ref[...] = blocks[1] + blocks[7] + blocks[3] + blocks[5] - 4.0 * value

    def forward(state_ref, patch_ref, one_ref, two_ref, next_ref, low, high, write_low, write_high):
        for start, size in chunks(low, high):
            here = slice(start, start + size)
            one = jnp.tanh(jnp.dot(w1, patch_ref[:, here], preferred_element_type=F32)).astype(BF16)
            one_ref[:, here] = one
            two = jnp.tanh(jnp.dot(w2, one, preferred_element_type=F32)).astype(BF16)
            two_ref[:, here] = two
            tendency = jnp.dot(w3, two, preferred_element_type=F32)[0:8]
            centre = state_ref[:, here]
            update = (
                centre
                + wide_diff[:, here] * lap_ref[:, here]
                + (mixed(mix_to, centre) + closure_dt * tendency)
            )
            next_ref[:, here] = wide_mask[:, here] * update

    state_one[...] = jnp.zeros_like(state_one)
    make_patch(flat_a[...], patch_zero)
    low, high = tile_range(3)
    forward(flat_a, patch_zero, hid_one_zero, hid_two_zero, state_one, low, high, low, high)
    make_patch(state_one[...], patch_one)
    low, high = tile_range(2)
    forward(state_one, patch_one, hid_one_one, hid_two_one, state_two, low, high, low, high)

    def write_rows(source_ref, target_ref):
        for r in range(ROWS):
            start = (r + HALO) * PITCH + HALO
            t, turn = start // LANES, start % LANES
            before = source_ref[:, t * LANES : (t + 1) * LANES]
            after = source_ref[:, (t + 1) * LANES : (t + 2) * LANES]
            value = pltpu.roll(jnp.where(lane >= turn, before, after), (LANES - turn) % LANES, 1)
            target_ref[:, r, :] = value[0:FIELDS]

    grad_low, grad_high = tile_range(0)
    grad_here = slice(grad_low, grad_high)

    def backward(adj_ref, patch_ref, one_ref, two_ref, low, high):
        for start, size in chunks(low, high):
            here = slice(start, start + size)
            masked = wide_mask[:, here] * adj_ref[:, here]
            low_grad = jnp.concatenate([closure_dt * masked, jnp.zeros_like(masked)], axis=0).astype(BF16)
            out_grad[:, here] = low_grad
            two = two_ref[:, here].astype(F32)
            grad_two = (
                jnp.dot(w3_t, low_grad, preferred_element_type=F32) * (1.0 - two * two)
            ).astype(BF16)
            back_two[:, here] = grad_two
            one = one_ref[:, here].astype(F32)
            grad_one = (
                jnp.dot(w2_t, grad_two, preferred_element_type=F32) * (1.0 - one * one)
            ).astype(BF16)
            back_one[:, here] = grad_one
            grad_zero = jnp.dot(w1_t, grad_one, preferred_element_type=F32)
            spread = wide_diff[:, here] * masked
            direct = masked + mixed(mix_from, masked) - 4.0 * spread
            for k in range(9):
                block = grad_zero[8 * k : 8 * k + 8]
                if k == 4:
                    block = block + direct
                elif k % 2:
                    block = block + spread
                patch_grad[8 * k : 8 * k + 8, here] = block
        own = own_ref[:, grad_here]
        grad_first = nt(back_one[:, grad_here], patch_ref[:, grad_here] * own[0:DEEP])
        grad_second = nt(back_two[:, grad_here], one_ref[:, grad_here] * own)
        grad_output = nt(out_grad[:, grad_here] * own[0:16], two_ref[:, grad_here])
        return grad_first, grad_second, grad_output

    def scatter():
        total = None
        for k, (p, q) in enumerate(offsets):
            block = patch_grad[8 * k : 8 * k + 8, :]
            if (p, q) != (0, 0):
                block = shift(block, -(p * PITCH + q))
            total = block if total is None else total + block
        return total

    patch_grad[...] = jnp.zeros_like(patch_grad)
    low, high = tile_range(2)
    late_first, late_second, late_output = backward(flat_b, patch_one, hid_one_one, hid_two_one, low, high)
    adj_one[...] = scatter()
    low, high = tile_range(1)
    first, second, output = backward(adj_one, patch_zero, hid_one_zero, hid_two_zero, low, high)
    first = first + late_first
    second = second + late_second
    output = output + late_output

    high_part, low_part = halves(first)
    narrow = jnp.dot(high_part, select, preferred_element_type=F32) + jnp.dot(
        low_part, select, preferred_element_type=F32
    )
    others = jnp.concatenate([flatten_rows(narrow, True), output[0:8]], axis=0)
    for i in range(NLON):
        grads[i, 0:8, :] = second[8 * i : 8 * i + 8]
        grads[i, 8:12, :] = others[4 * i : 4 * i + 4]

    def copies_along(axis, here, steps, size, phase, source, target):
        made = []
        for place, d in enumerate(steps):
            peer = ring(here, d, size)
            made.append(
                pltpu.make_async_remote_copy(
                    src_ref=source(peer),
                    dst_ref=target(place),
                    send_sem=send_sem.at[phase],
                    recv_sem=recv_sem.at[phase],
                    device_id={axis: peer},
                    device_id_type=MESH,
                )
            )
        for copy in made:
            copy.start()

    def all_of(phase, buffer):
        return pltpu.make_async_remote_copy(
            src_ref=buffer,
            dst_ref=buffer,
            send_sem=send_sem.at[phase],
            recv_sem=recv_sem.at[phase],
            device_id={"lon": east},
            device_id_type=MESH,
        )

    copies_along("lon", lon, LON_STEPS, NLON, 1, lambda peer: grads.at[peer], lambda place: recv_one.at[place])

    write_rows(state_two, final_ref)
    adj_one[...] = scatter()
    write_rows(adj_one, adjoint_ref)

    scatters = all_of(1, recv_one)
    scatters.wait_recv()
    band = grads[lon]
    for n in range(NLON - 1):
        band = band + recv_one[n]
    recv_two[lat] = band

    copies_along("lat", lat, LAT_STEPS, NLAT, 2, lambda peer: recv_two.at[lat], lambda place: recv_two.at[lat])
    exchanges = all_of(2, recv_two.at[0 : NLAT - 1])
    exchanges.wait_recv()
    total = recv_two[0]
    squares = total * total
    for b in range(1, NLAT):
        value = recv_two[b]
        total = total + value
        squares = squares + value * value
    gathered[lon, 0:CHUNK, :] = total
    gathered[lon, CHUNK:SENT, :] = jnp.sum(squares, axis=0, keepdims=True)

    copies_along("lon", lon, LON_STEPS, NLON, 3, lambda peer: gathered.at[lon], lambda place: gathered.at[lon])
    loads[8].wait()
    collects = all_of(3, gathered.at[0 : NLON - 1])
    collects.wait_recv()

    square_sum = jnp.zeros((CHUNK, LANES), F32)
    band_sum = jnp.zeros((1, LANES), F32)
    for i in range(NLON):
        value = gathered[i, 0:CHUNK, :]
        square_sum = square_sum + value * value
        band_sum = band_sum + gathered[i, CHUNK : CHUNK + 1, :]
        total_ref[54 + 8 * i : 62 + 8 * i, :] = value[0:8]
        if i < 13:
            total_ref[4 * i : 4 * i + 4, :] = value[8:12]
        elif i == 13:
            total_ref[52:54, :] = value[8:10]
        elif i == 14:
            total_ref[182:186, :] = value[8:12]
        else:
            total_ref[186:188, :] = value[8:10]
    grad_square = jnp.sum(square_sum)
    ratio_ref[...] = jnp.full((1, LANES), jnp.sum(band_sum) / (grad_square + epsilon), F32)
    spread_square = jnp.full((1, LANES), grad_square / PARAMS + epsilon, F32)
    scale = learn_rate / jnp.sqrt(spread_square)
    params_ref[...] = base_params[0:188, :] - scale * total_ref[0:188, :] + noise_in[...]

    for copies in (all_halos, scatters, exchanges, collects):
        copies.wait_send()


def emit(final_in, adjoint_in, params_in, ratio_in, final_out, adjoint_out, params_out, ratio_out, held, sem):
    pairs = ((final_in, final_out), (adjoint_in, adjoint_out), (params_in, params_out))
    copies = [pltpu.make_async_copy(src, dst, sem.at[n]) for n, (src, dst) in enumerate(pairs)]
    for copy in copies:
        copy.start()
    held[0] = ratio_in[0, 0]
    copies.append(pltpu.make_async_copy(held, ratio_out, sem.at[3]))
    copies[3].start()
    for copy in copies:
        copy.wait()


def on_device(
    initial_state,
    diffusion,
    mixing,
    land_mask,
    first_layer,
    second_layer,
    output_layer,
    cotangent,
    update_noise,
):
    vmem = pltpu.VMEM
    flat8 = vmem((8, FLAT), F32)
    hidden = vmem((HID, FLAT), BF16)
    dma = pltpu.SemaphoreType.DMA
    scratch = [
        vmem((FIELDS, ROWS, COLS), F32),
        vmem((ROWS, COLS), F32),
        vmem((ROWS, COLS), jnp.int32),
        vmem((FIELDS, ROWS, COLS), F32),
        vmem((188, LANES), F32),
        pltpu.SMEM((FIELDS, FIELDS), F32),
        vmem((PATCH, HID), BF16),
        vmem((HID, HID), BF16),
        vmem((FIELDS, HID), BF16),
        dma((9,)),
        vmem((ROWS, 8, LANES), F32),
        vmem((ROWS, 8, LANES), F32),
        vmem((6, 8, LANES), F32),
        vmem((6, 8, LANES), F32),
        vmem((2, 8, LANES), F32),
        vmem((24, 8, LANES), F32),
        dma((4,)),
        dma((4,)),
        flat8,
        flat8,
        hidden,
        flat8,
        flat8,
        flat8,
        flat8,
        flat8,
        vmem((DEEP, FLAT), BF16),
        vmem((DEEP, FLAT), BF16),
        hidden,
        hidden,
        hidden,
        hidden,
        hidden,
        hidden,
        vmem((16, FLAT), BF16),
        vmem((72, FLAT), F32),
        flat8,
        vmem((HID, LANES), F32),
        vmem((16, LANES), F32),
        vmem((192, LANES), F32),
        vmem((NLON, CHUNK, LANES), F32),
        vmem((NLON - 1, CHUNK, LANES), F32),
        vmem((NLAT, CHUNK, LANES), F32),
        vmem((NLON, SENT, LANES), F32),
        vmem((192, LANES), F32),
    ]
    hbm = pl.BlockSpec(memory_space=pltpu.HBM)
    local = pl.BlockSpec(memory_space=pltpu.VMEM)
    final, adjoint, params, ratio = pl.pallas_call(
        kernel,
        out_shape=(
            jax.ShapeDtypeStruct((FIELDS, ROWS, COLS), F32),
            jax.ShapeDtypeStruct((FIELDS, ROWS, COLS), F32),
            jax.ShapeDtypeStruct((188, LANES), F32),
            jax.ShapeDtypeStruct((1, LANES), F32),
        ),
        in_specs=[hbm] * 9,
        out_specs=(local,) * 4,
        scratch_shapes=scratch,
        compiler_params=pltpu.CompilerParams(
            collective_id=0, has_side_effects=True, vmem_limit_bytes=40 * 1024 * 1024
        ),
        name="ocean",
    )(
        *(
            pltpu.with_memory_space_constraint(value, pltpu.HBM)
            for value in (
                initial_state,
                diffusion,
                mixing,
                land_mask,
                first_layer.T,
                second_layer,
                output_layer,
                cotangent,
                update_noise.reshape(188, LANES),
            )
        )
    )
    final, adjoint, params, ratio = pl.pallas_call(
        emit,
        out_shape=(
            jax.ShapeDtypeStruct((FIELDS, ROWS, COLS), F32),
            jax.ShapeDtypeStruct((FIELDS, ROWS, COLS), F32),
            jax.ShapeDtypeStruct((188, LANES), F32),
            jax.ShapeDtypeStruct((1,), F32),
        ),
        in_specs=[local] * 4,
        out_specs=(hbm,) * 4,
        scratch_shapes=[pltpu.SMEM((1,), F32), dma((4,))],
        name="emit",
    )(*(pltpu.with_memory_space_constraint(value, pltpu.VMEM) for value in (final, adjoint, params, ratio)))
    return final, adjoint, params.reshape(PARAMS), ratio


def solution(mesh):
    placed = (
        P("ens", "lat", "lon"),
        P("lat", "lon"),
        P(),
        P("lat", "lon"),
        P(),
        P(),
        P(),
        P("ens", "lat", "lon"),
        P("ens"),
    )
    return jax.shard_map(
        on_device,
        mesh=mesh,
        in_specs=placed,
        out_specs=(P("ens", "lat", "lon"), P("ens", "lat", "lon"), P("ens"), P("ens")),
        check_vma=False,
    )
```

```python
import functools
import math
from types import SimpleNamespace

import jax
import jax.numpy as jnp
from jax import lax
from jax.experimental import pallas as pl
from jax.experimental.pallas import tpu as pltpu
from jax.sharding import PartitionSpec as P

MESH = pl.DeviceIdType.MESH
F32 = jnp.float32
BF16 = jnp.bfloat16

closure_dt = 0.1
learn_rate = 0.1
epsilon = 1e-06
offsets = [(p, q) for p in (-1, 0, 1) for q in (-1, 0, 1)]

FIELDS, ROWS, COLS = 6, 16, 128
HALO = 4
PITCH = COLS + 2 * HALO
EXT = ROWS + 2 * HALO
LANES = 128
TILES = -(-EXT * PITCH // LANES)
FLAT = TILES * LANES
HID = 128
PATCH = 54
DEEP = 80
PARAMS = 24064
NLON, NLAT = 16, 8
CHUNK = 12
SENT = CHUNK + 1
LON_STEPS = (8, 7, 9, 6, 10, 5, 11, 4, 12, 3, 13, 2, 14, 1, 15)
LAT_STEPS = (2, 6, 1, 3, 5, 7, 4)


def ring(index, step, size):
    return lax.rem(index + step + size, size)


def tile_range(distance):
    low = (HALO - distance) * PITCH // LANES
    high = -(-(HALO + ROWS + distance) * PITCH // LANES)
    if (high - low) % 2:
        low, high = (low, high + 1) if high < TILES else (low - 1, high)
    return low * LANES, high * LANES


def chunks(low, high, size=4096):
    return [(start, min(size, high - start)) for start in range(low, high, size)]


def spread_lanes(tile, length):
    return jnp.concatenate([tile] * (length // LANES), axis=1)


def segments(tile):
    found = []
    base = tile * LANES
    for row in range(EXT):
        start = row * PITCH
        for part, low, high in (
            ("left", start, start + HALO),
            ("main", start + HALO, start + HALO + COLS),
            ("right", start + HALO + COLS, start + PITCH),
        ):
            first, end = max(low, base), min(high, base + LANES)
            if first < end:
                found.append((first - base, end - base, row, part))
    return found


def kernel(
    state_hbm,
    diff_hbm,
    mix_hbm,
    mask_hbm,
    first_hbm,
    second_hbm,
    output_hbm,
    cot_hbm,
    noise_hbm,
    final_ref,
    adjoint_ref,
    params_ref,
    ratio_ref,
    state_in,
    diff_in,
    mask_in,
    cot_in,
    noise_in,
    mix_ref,
    first_ref,
    second_ref,
    output_ref,
    load_sem,
    own_a,
    own_b,
    send_north,
    send_south,
    edge,
    halo_in,
    here_sem,
    send_sem,
    recv_sem,
    flat_a,
    flat_b,
    own_ref,
    wide_mask,
    wide_diff,
    state_one,
    state_two,
    lap_ref,
    patch_zero,
    patch_one,
    hid_one_zero,
    hid_two_zero,
    hid_one_one,
    hid_two_one,
    back_one,
    back_two,
    out_grad,
    patch_grad,
    adj_one,
    weights_one,
    weights_three,
    base_params,
    grads,
    others_ref,
    others,
    recv_one,
    recv_others,
    recv_two,
    gathered,
    total_ref,
):
    lat = lax.axis_index("lat")
    lon = lax.axis_index("lon")
    north, south = ring(lat, -1, NLAT), ring(lat, 1, NLAT)
    west, east = ring(lon, -1, NLON), ring(lon, 1, NLON)

    barrier = pltpu.get_barrier_semaphore()
    greet = [{"lat": a, "lon": b} for a in (north, south) for b in (west, east)]
    greet += [{"lat": north}, {"lat": south}, {"lon": west}, {"lon": east}]
    for device in greet:
        pl.semaphore_signal(barrier, inc=1, device_id=device, device_id_type=MESH)

    loads = [
        pltpu.make_async_copy(src, dst, load_sem.at[n])
        for n, (src, dst) in enumerate(
            (
                (state_hbm, state_in),
                (mask_hbm, mask_in),
                (diff_hbm, diff_in),
                (cot_hbm, cot_in),
                (mix_hbm, mix_ref),
                (first_hbm, first_ref),
                (second_hbm, second_ref),
                (output_hbm, output_ref),
                (noise_hbm, noise_in),
            )
        )
    ]
    for load in loads:
        load.start()

    lane = lax.broadcasted_iota(jnp.int32, (8, LANES), 1)
    sub = lax.broadcasted_iota(jnp.int32, (8, LANES), 0)
    for load in loads[:4]:
        load.wait()

    own_b[...] = jnp.zeros_like(own_b)
    for r in range(ROWS):
        own_a[r, 0:FIELDS, :] = state_in[:, r, :]
        own_a[r, 6:7, :] = mask_in[r : r + 1, :].astype(F32)
        own_a[r, 7:8, :] = diff_in[r : r + 1, :]
        own_b[r, 0:FIELDS, :] = cot_in[:, r, :]
    edge_a = jnp.zeros((8, LANES), F32)
    edge_b = jnp.zeros((8, LANES), F32)
    for r in range(ROWS):
        j = r + HALO
        turn = (j * PITCH + HALO) % LANES
        tile_a = pltpu.roll(own_a[r], turn, 1)
        tile_b = pltpu.roll(own_b[r], turn, 1)
        own_a[r] = tile_a
        own_b[r] = tile_b
        place = (j * PITCH) % LANES
        pick = (lane >= place) & (lane < place + 2 * HALO)
        edge_a = jnp.where(pick, tile_a, edge_a)
        edge_b = jnp.where(pick, tile_b, edge_b)
        if r < HALO:
            send_north[r] = tile_a
        if r < 2:
            send_north[HALO + r] = tile_b
        if r >= ROWS - HALO:
            send_south[r - (ROWS - HALO)] = tile_a
        if r >= ROWS - 2:
            send_south[HALO + r - (ROWS - 2)] = tile_b
    edge[0] = edge_a
    edge[1] = edge_b

    pl.semaphore_wait(barrier, len(greet))

    def halo_copy(source, target, device):
        return pltpu.make_async_remote_copy(
            src_ref=source,
            dst_ref=target,
            send_sem=send_sem.at[0],
            recv_sem=recv_sem.at[0],
            device_id=device,
            device_id_type=MESH,
        )

    from_north, from_south = halo_in.at[0:6], halo_in.at[6:12]
    edges_in = [halo_in.at[12 + 2 * n : 14 + 2 * n] for n in range(6)]
    halos = [
        halo_copy(edge, edges_in[0], {"lat": south, "lon": east}),
        halo_copy(edge, edges_in[2], {"lat": north, "lon": east}),
        halo_copy(edge, edges_in[3], {"lat": south, "lon": west}),
        halo_copy(edge, edges_in[5], {"lat": north, "lon": west}),
        halo_copy(send_north, from_south, {"lat": north}),
        halo_copy(send_south, from_north, {"lat": south}),
        halo_copy(edge, edges_in[1], {"lon": east}),
        halo_copy(edge, edges_in[4], {"lon": west}),
    ]
    for copy in halos:
        copy.start()

    def tell(stage, reach):
        devices = [{"lon": ring(lon, d, NLON)} for d in (reach, -reach)]
        if reach < NLAT // 2:
            devices += [{"lat": ring(lat, d, NLAT)} for d in (reach, -reach)]
        for device in devices:
            pl.semaphore_signal(here_sem.at[stage], inc=1, device_id=device, device_id_type=MESH)
        return len(devices)

    told = tell(0, 1)

    for load in loads[4:8]:
        load.wait()
    weights_one[...] = jnp.zeros_like(weights_one)
    weights_one[0:PATCH, :] = first_ref[...].astype(F32)
    others_ref[...] = jnp.zeros_like(others_ref)
    weights_three[...] = jnp.zeros_like(weights_three)
    weights_three[0:FIELDS, :] = output_ref[...].astype(F32)

    def nt(left, right, precision=None):
        return lax.dot_general(
            left, right, (((1,), (1,)), ((), ())), preferred_element_type=F32, precision=precision
        )

    def tn(left, right):
        return lax.dot_general(left, right, (((0,), (0,)), ((), ())), preferred_element_type=F32)

    deep_i = lax.broadcasted_iota(jnp.int32, (DEEP, HID), 0)
    deep_j = lax.broadcasted_iota(jnp.int32, (DEEP, HID), 1)
    deep_f = lax.bitwise_and(deep_i, 7)
    picked = (deep_j == 6 * lax.shift_right_logical(deep_i, 3) + deep_f) & (deep_f < 6) & (deep_i < 72)
    select = jnp.where(picked, 1.0, 0.0).astype(BF16)
    row = lax.broadcasted_iota(jnp.int32, (HID, HID), 0)
    column = lax.broadcasted_iota(jnp.int32, (HID, HID), 1)
    eye = jnp.where(row == column, 1.0, 0.0).astype(BF16)
    turned_one = weights_one[...].astype(BF16)
    plain_one = nt(eye, turned_one).astype(BF16)
    w1 = nt(plain_one, select).astype(BF16)
    w1_t = jnp.dot(select, turned_one, preferred_element_type=F32).astype(BF16)
    w2 = second_ref[...]
    w2_t = nt(eye, w2).astype(BF16)
    w3 = weights_three[...].astype(BF16)
    w3_t = nt(eye, w3).astype(BF16)

    turn_of = lax.bitwise_and(row * PATCH, LANES - 1)
    deep_r = lax.broadcasted_iota(jnp.int32, (56, 2 * HID), 0)
    deep_h = lax.broadcasted_iota(jnp.int32, (56, 2 * HID), 1)
    hid_h = lax.bitwise_and(deep_h, HID - 1)
    lands = lax.shift_right_logical(hid_h * PATCH, 7) + lax.shift_right_logical(deep_h, 7)
    gather_rows = jnp.where(lands == deep_r, 1.0, 0.0).astype(BF16)

    def halves(value):
        high = value.astype(BF16)
        return high, (value - high.astype(F32)).astype(BF16)

    def flatten_rows(value, exact):
        turned = []
        for m in range(HID // 8):
            tile = value[8 * m : 8 * m + 8]
            if (8 * m * PATCH) % LANES:
                tile = pltpu.roll(tile, (8 * m * PATCH) % LANES, 1)
            for _ in range(3):
                tile = pltpu.roll(tile, 0, 1, stride=PATCH // 3, stride_axis=0)
            turned.append(tile)
        value = jnp.concatenate(turned, axis=0)
        ahead = jnp.where(column >= turn_of, value, 0.0)
        behind = jnp.where(column < turn_of, value, 0.0)
        both = jnp.concatenate([ahead, behind], axis=0)
        if not exact:
            return jnp.dot(gather_rows, both.astype(BF16), preferred_element_type=F32)
        high, low = halves(both)
        return jnp.dot(gather_rows, high, preferred_element_type=F32) + jnp.dot(
            gather_rows, low, preferred_element_type=F32
        )

    base_params[0:56, :] = flatten_rows(plain_one.astype(F32), False)
    base_params[54:182, :] = w2.astype(F32)
    base_params[182:188, :] = output_ref[...].astype(F32)

    for t in range(TILES):
        own = jnp.zeros((8, LANES), F32)
        for first, end, j, part in segments(t):
            if part == "main" and HALO <= j < HALO + ROWS:
                own = jnp.where((lane >= first) & (lane < end), 1.0, own)
        own_ref[:, t * LANES : (t + 1) * LANES] = jnp.concatenate([own] * (HID // 8), axis=0).astype(BF16)

    mix_to = []
    mix_from = []
    for g in range(FIELDS):
        to_tile = jnp.zeros((8, LANES), F32)
        from_tile = jnp.zeros((8, LANES), F32)
        for f in range(FIELDS):
            to_tile = jnp.where(sub == f, mix_ref[f, g], to_tile)
            from_tile = jnp.where(sub == f, mix_ref[g, f], from_tile)
        mix_to.append(to_tile)
        mix_from.append(from_tile)

    pl.semaphore_wait(here_sem.at[0], told)
    told = tell(1, 2)

    def mixed(tiles, value):
        length = value.shape[1]
        total = None
        for g in range(FIELDS):
            term = spread_lanes(tiles[g], length) * jnp.broadcast_to(value[g : g + 1, :], (8, length))
            total = term if total is None else total + term
        return total

    pl.semaphore_wait(here_sem.at[1], told)
    told = tell(2, 4)
    all_halos = halo_copy(halo_in, halo_in, {"lon": east})
    all_halos.wait_recv()

    def top(value):
        return jnp.where(lat > 0, value, 0.0)

    def bottom(value):
        return jnp.where(lat < NLAT - 1, value, 0.0)

    blank = jnp.zeros((8, LANES), F32)
    sides = []
    for which in range(2):
        sides.append(
            {
                "left": (top(halo_in[12 + which]), halo_in[14 + which], bottom(halo_in[16 + which])),
                "right": (top(halo_in[18 + which]), halo_in[20 + which], bottom(halo_in[22 + which])),
            }
        )

    def source(which, j, part):
        if which == 1 and (j < 2 or j >= EXT - 2):
            return blank
        if part != "main":
            return sides[which][part][0 if j < HALO else 1 if j < HALO + ROWS else 2]
        if j < HALO:
            return top(halo_in[j if which == 0 else HALO + j - 2])
        if j < HALO + ROWS:
            return (own_a if which == 0 else own_b)[j - HALO]
        return bottom(halo_in[6 + (j - HALO - ROWS if which == 0 else j - ROWS)])

    for t in range(TILES):
        here = slice(t * LANES, (t + 1) * LANES)
        for which, target in ((0, flat_a), (1, flat_b)):
            value = blank
            for first, end, j, part in segments(t):
                piece = source(which, j, part)
                value = jnp.where((lane >= first) & (lane < end), piece, value)
            target[:, here] = value
            if which == 0:
                wide_mask[:, here] = jnp.broadcast_to(value[6:7, :], (8, LANES))
                wide_diff[:, here] = jnp.broadcast_to(value[7:8, :], (8, LANES))

    def shift(value, amount):
        return pltpu.roll(value, (-amount) % FLAT, 1)

    def make_patch(value, patch_ref):
        blocks = [value if (p, q) == (0, 0) else shift(value, p * PITCH + q) for p, q in offsets]
        for m in range(5):
            after = blocks[2 * m + 1] if m < 4 else jnp.zeros_like(value)
            patch_ref[16 * m : 16 * m + 16, :] = jnp.concatenate([blocks[2 * m], after], axis=0).astype(BF16)
        lap_ref[...] = blocks[1] + blocks[7] + blocks[3] + blocks[5] - 4.0 * value

    def forward(state_ref, patch_ref, one_ref, two_ref, next_ref, low, high, write_low, write_high):
        for start, size in chunks(low, high):
            here = slice(start, start + size)
            one = jnp.tanh(jnp.dot(w1, patch_ref[:, here], preferred_element_type=F32)).astype(BF16)
            one_ref[:, here] = one
            two = jnp.tanh(jnp.dot(w2, one, preferred_element_type=F32)).astype(BF16)
            two_ref[:, here] = two
            tendency = jnp.dot(w3, two, preferred_element_type=F32)[0:8]
            centre = state_ref[:, here]
            update = (
                centre
                + wide_diff[:, here] * lap_ref[:, here]
                + (mixed(mix_to, centre) + closure_dt * tendency)
            )
            next_ref[:, here] = wide_mask[:, here] * update

    state_one[...] = jnp.zeros_like(state_one)
    make_patch(flat_a[...], patch_zero)
    low, high = tile_range(3)
    forward(flat_a, patch_zero, hid_one_zero, hid_two_zero, state_one, low, high, low, high)
    make_patch(state_one[...], patch_one)
    low, high = tile_range(2)
    forward(state_one, patch_one, hid_one_one, hid_two_one, state_two, low, high, low, high)

    def write_rows(source_ref, target_ref):
        for r in range(ROWS):
            start = (r + HALO) * PITCH + HALO
            t, turn = start // LANES, start % LANES
            before = source_ref[:, t * LANES : (t + 1) * LANES]
            after = source_ref[:, (t + 1) * LANES : (t + 2) * LANES]
            value = pltpu.roll(jnp.where(lane >= turn, before, after), (LANES - turn) % LANES, 1)
            target_ref[:, r, :] = value[0:FIELDS]

    grad_low, grad_high = tile_range(0)
    grad_here = slice(grad_low, grad_high)

    def backward(adj_ref, patch_ref, one_ref, two_ref, low, high):
        for start, size in chunks(low, high):
            here = slice(start, start + size)
            masked = wide_mask[:, here] * adj_ref[:, here]
            low_grad = jnp.concatenate([closure_dt * masked, jnp.zeros_like(masked)], axis=0).astype(BF16)
            out_grad[:, here] = low_grad
            two = two_ref[:, here].astype(F32)
            grad_two = (
                jnp.dot(w3_t, low_grad, preferred_element_type=F32) * (1.0 - two * two)
            ).astype(BF16)
            back_two[:, here] = grad_two
            one = one_ref[:, here].astype(F32)
            grad_one = (
                jnp.dot(w2_t, grad_two, preferred_element_type=F32) * (1.0 - one * one)
            ).astype(BF16)
            back_one[:, here] = grad_one
            grad_zero = jnp.dot(w1_t, grad_one, preferred_element_type=F32)
            spread = wide_diff[:, here] * masked
            direct = masked + mixed(mix_from, masked) - 4.0 * spread
            for k in range(9):
                block = grad_zero[8 * k : 8 * k + 8]
                if k == 4:
                    block = block + direct
                elif k % 2:
                    block = block + spread
                patch_grad[8 * k : 8 * k + 8, here] = block
        own = own_ref[:, grad_here]
        grad_second = nt(back_two[:, grad_here], one_ref[:, grad_here] * own)
        grad_output = nt(out_grad[:, grad_here] * own[0:16], two_ref[:, grad_here])
        grad_first = nt(patch_ref[:, grad_here] * own[0:DEEP], back_one[:, grad_here])
        return grad_first, grad_second, grad_output

    def scatter():
        total = None
        for k, (p, q) in enumerate(offsets):
            block = patch_grad[8 * k : 8 * k + 8, :]
            if (p, q) != (0, 0):
                block = shift(block, -(p * PITCH + q))
            total = block if total is None else total + block
        return total

    patch_grad[...] = jnp.zeros_like(patch_grad)
    low, high = tile_range(2)
    late_first, late_second, late_output = backward(flat_b, patch_one, hid_one_one, hid_two_one, low, high)
    adj_one[...] = scatter()
    low, high = tile_range(1)
    first, second, output = backward(adj_one, patch_zero, hid_one_zero, hid_two_zero, low, high)
    first = first + late_first
    second = second + late_second
    output = output + late_output

    def copies_along(axis, here, steps, size, phase, source, target):
        made = []
        for place, d in enumerate(steps):
            peer = ring(here, d, size)
            made.append(
                pltpu.make_async_remote_copy(
                    src_ref=source(peer),
                    dst_ref=target(place),
                    send_sem=send_sem.at[phase],
                    recv_sem=recv_sem.at[phase],
                    device_id={axis: peer},
                    device_id_type=MESH,
                )
            )
        for copy in made:
            copy.start()

    def all_of(phase, buffer):
        return pltpu.make_async_remote_copy(
            src_ref=buffer,
            dst_ref=buffer,
            send_sem=send_sem.at[phase],
            recv_sem=recv_sem.at[phase],
            device_id={"lon": east},
            device_id_type=MESH,
        )

    for i in range(NLON):
        grads[i] = second[8 * i : 8 * i + 8]
    pl.semaphore_wait(here_sem.at[2], told)
    copies_along("lon", lon, LON_STEPS, NLON, 1, lambda peer: grads.at[peer], lambda place: recv_one.at[place])
    for k in range(9):
        others_ref[6 * k : 6 * k + 6, :] = first[8 * k : 8 * k + 6]
    others_ref[56:64, :] = output[0:8]
    for i in range(NLON):
        others[i] = others_ref[4 * i : 4 * i + 4, :]
    copies_along("lon", lon, LON_STEPS, NLON, 4, lambda peer: others.at[peer], lambda place: recv_others.at[place])

    write_rows(state_two, final_ref)
    adj_one[...] = scatter()
    write_rows(adj_one, adjoint_ref)

    scatters = all_of(1, recv_one)
    scatters.wait_recv()
    band = grads[lon]
    for n in range(NLON - 1):
        band = band + recv_one[n]
    recv_two[lat, 0:8, :] = band
    other_scatters = all_of(4, recv_others)
    other_scatters.wait_recv()
    band = others[lon]
    for n in range(NLON - 1):
        band = band + recv_others[n]
    recv_two[lat, 8:CHUNK, :] = band

    copies_along("lat", lat, LAT_STEPS, NLAT, 2, lambda peer: recv_two.at[lat], lambda place: recv_two.at[lat])
    exchanges = all_of(2, recv_two.at[0 : NLAT - 1])
    exchanges.wait_recv()
    total = recv_two[0]
    squares = total * total
    for b in range(1, NLAT):
        value = recv_two[b]
        total = total + value
        squares = squares + value * value
    gathered[lon, 0:CHUNK, :] = total
    gathered[lon, CHUNK:SENT, :] = jnp.sum(squares, axis=0, keepdims=True)

    copies_along("lon", lon, LON_STEPS, NLON, 3, lambda peer: gathered.at[lon], lambda place: gathered.at[lon])
    loads[8].wait()
    collects = all_of(3, gathered.at[0 : NLON - 1])
    collects.wait_recv()

    square_sum = jnp.zeros((CHUNK, LANES), F32)
    band_sum = jnp.zeros((1, LANES), F32)
    for i in range(NLON):
        value = gathered[i, 0:CHUNK, :]
        square_sum = square_sum + value * value
        band_sum = band_sum + gathered[i, CHUNK : CHUNK + 1, :]
        total_ref[54 + 8 * i : 62 + 8 * i, :] = value[0:8]
        if i < 14:
            others_ref[4 * i : 4 * i + 4, :] = value[8:12]
        elif i == 14:
            total_ref[182:186, :] = value[8:12]
        else:
            total_ref[186:188, :] = value[8:10]
    others_ref[56:64, :] = jnp.zeros((8, LANES), F32)
    high_part, low_part = halves(others_ref[...])
    turned_total = tn(high_part, eye[0:64]) + tn(low_part, eye[0:64])
    total_ref[0:PATCH, :] = flatten_rows(turned_total, True)[0:PATCH]
    grad_square = jnp.sum(square_sum)
    ratio_ref[...] = jnp.full((1, LANES), jnp.sum(band_sum) / (grad_square + epsilon), F32)
    spread_square = jnp.full((1, LANES), grad_square / PARAMS + epsilon, F32)
    scale = learn_rate / jnp.sqrt(spread_square)
    params_ref[...] = base_params[0:188, :] - scale * total_ref[0:188, :] + noise_in[...]

    for copies in (all_halos, scatters, other_scatters, exchanges, collects):
        copies.wait_send()


def emit(final_in, adjoint_in, params_in, ratio_in, final_out, adjoint_out, params_out, ratio_out, held, sem):
    pairs = ((final_in, final_out), (adjoint_in, adjoint_out), (params_in, params_out))
    copies = [pltpu.make_async_copy(src, dst, sem.at[n]) for n, (src, dst) in enumerate(pairs)]
    for copy in copies:
        copy.start()
    held[0] = ratio_in[0, 0]
    copies.append(pltpu.make_async_copy(held, ratio_out, sem.at[3]))
    copies[3].start()
    for copy in copies:
        copy.wait()


def on_device(
    initial_state,
    diffusion,
    mixing,
    land_mask,
    first_layer,
    second_layer,
    output_layer,
    cotangent,
    update_noise,
):
    vmem = pltpu.VMEM
    flat8 = vmem((8, FLAT), F32)
    hidden = vmem((HID, FLAT), BF16)
    dma = pltpu.SemaphoreType.DMA
    scratch = [
        vmem((FIELDS, ROWS, COLS), F32),
        vmem((ROWS, COLS), F32),
        vmem((ROWS, COLS), jnp.int32),
        vmem((FIELDS, ROWS, COLS), F32),
        vmem((188, LANES), F32),
        pltpu.SMEM((FIELDS, FIELDS), F32),
        vmem((PATCH, HID), BF16),
        vmem((HID, HID), BF16),
        vmem((FIELDS, HID), BF16),
        dma((9,)),
        vmem((ROWS, 8, LANES), F32),
        vmem((ROWS, 8, LANES), F32),
        vmem((6, 8, LANES), F32),
        vmem((6, 8, LANES), F32),
        vmem((2, 8, LANES), F32),
        vmem((24, 8, LANES), F32),
        pltpu.SemaphoreType.REGULAR((3,)),
        dma((5,)),
        dma((5,)),
        flat8,
        flat8,
        hidden,
        flat8,
        flat8,
        flat8,
        flat8,
        flat8,
        vmem((DEEP, FLAT), BF16),
        vmem((DEEP, FLAT), BF16),
        hidden,
        hidden,
        hidden,
        hidden,
        hidden,
        hidden,
        vmem((16, FLAT), BF16),
        vmem((72, FLAT), F32),
        flat8,
        vmem((HID, LANES), F32),
        vmem((16, LANES), F32),
        vmem((192, LANES), F32),
        vmem((NLON, 8, LANES), F32),
        vmem((64, LANES), F32),
        vmem((NLON, 4, LANES), F32),
        vmem((NLON - 1, 8, LANES), F32),
        vmem((NLON - 1, 4, LANES), F32),
        vmem((NLAT, CHUNK, LANES), F32),
        vmem((NLON, SENT, LANES), F32),
        vmem((192, LANES), F32),
    ]
    hbm = pl.BlockSpec(memory_space=pltpu.HBM)
    local = pl.BlockSpec(memory_space=pltpu.VMEM)
    final, adjoint, params, ratio = pl.pallas_call(
        kernel,
        out_shape=(
            jax.ShapeDtypeStruct((FIELDS, ROWS, COLS), F32),
            jax.ShapeDtypeStruct((FIELDS, ROWS, COLS), F32),
            jax.ShapeDtypeStruct((188, LANES), F32),
            jax.ShapeDtypeStruct((1, LANES), F32),
        ),
        in_specs=[hbm] * 9,
        out_specs=(local,) * 4,
        scratch_shapes=scratch,
        compiler_params=pltpu.CompilerParams(
            collective_id=0, has_side_effects=True, vmem_limit_bytes=40 * 1024 * 1024
        ),
        name="ocean",
    )(
        *(
            pltpu.with_memory_space_constraint(value, pltpu.HBM)
            for value in (
                initial_state,
                diffusion,
                mixing,
                land_mask,
                first_layer.T,
                second_layer,
                output_layer,
                cotangent,
                update_noise.reshape(188, LANES),
            )
        )
    )
    final, adjoint, params, ratio = pl.pallas_call(
        emit,
        out_shape=(
            jax.ShapeDtypeStruct((FIELDS, ROWS, COLS), F32),
            jax.ShapeDtypeStruct((FIELDS, ROWS, COLS), F32),
            jax.ShapeDtypeStruct((188, LANES), F32),
            jax.ShapeDtypeStruct((1,), F32),
        ),
        in_specs=[local] * 4,
        out_specs=(hbm,) * 4,
        scratch_shapes=[pltpu.SMEM((1,), F32), dma((4,))],
        name="emit",
    )(*(pltpu.with_memory_space_constraint(value, pltpu.VMEM) for value in (final, adjoint, params, ratio)))
    return final, adjoint, params.reshape(PARAMS), ratio


def solution(mesh):
    placed = (
        P("ens", "lat", "lon"),
        P("lat", "lon"),
        P(),
        P("lat", "lon"),
        P(),
        P(),
        P(),
        P("ens", "lat", "lon"),
        P("ens"),
    )
    return jax.shard_map(
        on_device,
        mesh=mesh,
        in_specs=placed,
        out_specs=(P("ens", "lat", "lon"), P("ens", "lat", "lon"), P("ens"), P("ens")),
        check_vma=False,
    )
```

```python
import functools
import math
from types import SimpleNamespace

import jax
import jax.numpy as jnp
from jax import lax
from jax.experimental import pallas as pl
from jax.experimental.pallas import tpu as pltpu
from jax.sharding import PartitionSpec as P

MESH = pl.DeviceIdType.MESH
F32 = jnp.float32
BF16 = jnp.bfloat16

closure_dt = 0.1
learn_rate = 0.1
epsilon = 1e-06
offsets = [(p, q) for p in (-1, 0, 1) for q in (-1, 0, 1)]

FIELDS, ROWS, COLS = 6, 16, 128
HALO = 4
PITCH = COLS + 2 * HALO
EXT = ROWS + 2 * HALO
LANES = 128
TILES = -(-EXT * PITCH // LANES)
FLAT = TILES * LANES
HID = 128
PATCH = 54
DEEP = 80
PARAMS = 24064
NLON, NLAT = 16, 8
CHUNKS = 8
CHUNK = 24
SENT = CHUNK + 1
CHIP_STEPS = (8, 6, 10, 4, 12, 2, 14)
NEAR_STEPS = (4, 13, 3, 14, 2, 15, 1)
LON_STEPS = (8, 6, 10, 4, 12, 3, 13, 2, 14, 1, 15)
LAT_STEPS = (2, 6, 1, 3, 5, 7, 4)


def ring(index, step, size):
    return lax.rem(index + step + size, size)


def tile_range(distance):
    low = (HALO - distance) * PITCH // LANES
    high = -(-(HALO + ROWS + distance) * PITCH // LANES)
    if (high - low) % 2:
        low, high = (low, high + 1) if high < TILES else (low - 1, high)
    return low * LANES, high * LANES


def chunks(low, high, size=4096):
    return [(start, min(size, high - start)) for start in range(low, high, size)]


def spread_lanes(tile, length):
    return jnp.concatenate([tile] * (length // LANES), axis=1)


def segments(tile):
    found = []
    base = tile * LANES
    for row in range(EXT):
        start = row * PITCH
        for part, low, high in (
            ("left", start, start + HALO),
            ("main", start + HALO, start + HALO + COLS),
            ("right", start + HALO + COLS, start + PITCH),
        ):
            first, end = max(low, base), min(high, base + LANES)
            if first < end:
                found.append((first - base, end - base, row, part))
    return found


def kernel(
    state_hbm,
    diff_hbm,
    mix_hbm,
    mask_hbm,
    first_hbm,
    second_hbm,
    output_hbm,
    cot_hbm,
    noise_hbm,
    final_ref,
    adjoint_ref,
    params_ref,
    ratio_ref,
    state_in,
    diff_in,
    mask_in,
    cot_in,
    noise_in,
    mix_ref,
    first_ref,
    second_ref,
    output_ref,
    load_sem,
    own_a,
    own_b,
    send_north,
    send_south,
    edge,
    halo_in,
    here_sem,
    send_sem,
    recv_sem,
    flat_a,
    flat_b,
    own_ref,
    wide_mask,
    wide_diff,
    state_one,
    state_two,
    lap_ref,
    patch_zero,
    patch_one,
    hid_one_zero,
    hid_two_zero,
    hid_one_one,
    hid_two_one,
    back_one,
    back_two,
    out_grad,
    patch_grad,
    adj_one,
    weights_one,
    weights_three,
    base_params,
    seconds,
    others,
    twin_seconds,
    twin_others,
    grads,
    recv_one,
    recv_two,
    gathered,
    total_ref,
):
    lat = lax.axis_index("lat")
    lon = lax.axis_index("lon")
    north, south = ring(lat, -1, NLAT), ring(lat, 1, NLAT)
    west, east = ring(lon, -1, NLON), ring(lon, 1, NLON)

    barrier = pltpu.get_barrier_semaphore()
    greet = [{"lat": a, "lon": b} for a in (north, south) for b in (west, east)]
    greet += [{"lat": north}, {"lat": south}, {"lon": west}, {"lon": east}]
    for device in greet:
        pl.semaphore_signal(barrier, inc=1, device_id=device, device_id_type=MESH)

    loads = [
        pltpu.make_async_copy(src, dst, load_sem.at[n])
        for n, (src, dst) in enumerate(
            (
                (state_hbm, state_in),
                (mask_hbm, mask_in),
                (diff_hbm, diff_in),
                (cot_hbm, cot_in),
                (mix_hbm, mix_ref),
                (first_hbm, first_ref),
                (second_hbm, second_ref),
                (output_hbm, output_ref),
                (noise_hbm, noise_in),
            )
        )
    ]
    for load in loads:
        load.start()

    lane = lax.broadcasted_iota(jnp.int32, (8, LANES), 1)
    sub = lax.broadcasted_iota(jnp.int32, (8, LANES), 0)
    for load in loads[:4]:
        load.wait()

    own_b[...] = jnp.zeros_like(own_b)
    for r in range(ROWS):
        own_a[r, 0:FIELDS, :] = state_in[:, r, :]
        own_a[r, 6:7, :] = mask_in[r : r + 1, :].astype(F32)
        own_a[r, 7:8, :] = diff_in[r : r + 1, :]
        own_b[r, 0:FIELDS, :] = cot_in[:, r, :]
    edge_a = jnp.zeros((8, LANES), F32)
    edge_b = jnp.zeros((8, LANES), F32)
    for r in range(ROWS):
        j = r + HALO
        turn = (j * PITCH + HALO) % LANES
        tile_a = pltpu.roll(own_a[r], turn, 1)
        tile_b = pltpu.roll(own_b[r], turn, 1)
        own_a[r] = tile_a
        own_b[r] = tile_b
        place = (j * PITCH) % LANES
        pick = (lane >= place) & (lane < place + 2 * HALO)
        edge_a = jnp.where(pick, tile_a, edge_a)
        edge_b = jnp.where(pick, tile_b, edge_b)
        if r < HALO:
            send_north[r] = tile_a
        if r < 2:
            send_north[HALO + r] = tile_b
        if r >= ROWS - HALO:
            send_south[r - (ROWS - HALO)] = tile_a
        if r >= ROWS - 2:
            send_south[HALO + r - (ROWS - 2)] = tile_b
    edge[0] = edge_a
    edge[1] = edge_b

    pl.semaphore_wait(barrier, len(greet))

    def halo_copy(source, target, device):
        return pltpu.make_async_remote_copy(
            src_ref=source,
            dst_ref=target,
            send_sem=send_sem.at[0],
            recv_sem=recv_sem.at[0],
            device_id=device,
            device_id_type=MESH,
        )

    from_north, from_south = halo_in.at[0:6], halo_in.at[6:12]
    edges_in = [halo_in.at[12 + 2 * n : 14 + 2 * n] for n in range(6)]
    halos = [
        halo_copy(edge, edges_in[0], {"lat": south, "lon": east}),
        halo_copy(edge, edges_in[2], {"lat": north, "lon": east}),
        halo_copy(edge, edges_in[3], {"lat": south, "lon": west}),
        halo_copy(edge, edges_in[5], {"lat": north, "lon": west}),
        halo_copy(send_north, from_south, {"lat": north}),
        halo_copy(send_south, from_north, {"lat": south}),
        halo_copy(edge, edges_in[1], {"lon": east}),
        halo_copy(edge, edges_in[4], {"lon": west}),
    ]
    for copy in halos:
        copy.start()

    def tell(stage, reach):
        devices = [{"lon": ring(lon, d, NLON)} for d in (reach, -reach)]
        if reach < NLAT // 2:
            devices += [{"lat": ring(lat, d, NLAT)} for d in (reach, -reach)]
        for device in devices:
            pl.semaphore_signal(here_sem.at[stage], inc=1, device_id=device, device_id_type=MESH)
        return len(devices)

    told = tell(0, 1)

    for load in loads[4:8]:
        load.wait()
    weights_one[...] = jnp.zeros_like(weights_one)
    weights_one[0:PATCH, :] = first_ref[...].astype(F32)
    weights_three[...] = jnp.zeros_like(weights_three)
    weights_three[0:FIELDS, :] = output_ref[...].astype(F32)

    def nt(left, right, precision=None):
        return lax.dot_general(
            left, right, (((1,), (1,)), ((), ())), preferred_element_type=F32, precision=precision
        )

    deep_i = lax.broadcasted_iota(jnp.int32, (DEEP, HID), 0)
    deep_j = lax.broadcasted_iota(jnp.int32, (DEEP, HID), 1)
    deep_f = lax.bitwise_and(deep_i, 7)
    picked = (deep_j == 6 * lax.shift_right_logical(deep_i, 3) + deep_f) & (deep_f < 6) & (deep_i < 72)
    select = jnp.where(picked, 1.0, 0.0).astype(BF16)
    row = lax.broadcasted_iota(jnp.int32, (HID, HID), 0)
    column = lax.broadcasted_iota(jnp.int32, (HID, HID), 1)
    eye = jnp.where(row == column, 1.0, 0.0).astype(BF16)
    turned_one = weights_one[...].astype(BF16)
    plain_one = nt(eye, turned_one).astype(BF16)
    w1 = nt(plain_one, select).astype(BF16)
    w1_t = jnp.dot(select, turned_one, preferred_element_type=F32).astype(BF16)
    w2 = second_ref[...]
    w2_t = nt(eye, w2).astype(BF16)
    w3 = weights_three[...].astype(BF16)
    w3_t = nt(eye, w3).astype(BF16)

    turn_of = lax.bitwise_and(row * PATCH, LANES - 1)
    deep_r = lax.broadcasted_iota(jnp.int32, (56, 2 * HID), 0)
    deep_h = lax.broadcasted_iota(jnp.int32, (56, 2 * HID), 1)
    hid_h = lax.bitwise_and(deep_h, HID - 1)
    lands = lax.shift_right_logical(hid_h * PATCH, 7) + lax.shift_right_logical(deep_h, 7)
    gather_rows = jnp.where(lands == deep_r, 1.0, 0.0).astype(BF16)

    def halves(value):
        high = value.astype(BF16)
        return high, (value - high.astype(F32)).astype(BF16)

    def flatten_rows(value, exact):
        turned = []
        for m in range(HID // 8):
            tile = value[8 * m : 8 * m + 8]
            if (8 * m * PATCH) % LANES:
                tile = pltpu.roll(tile, (8 * m * PATCH) % LANES, 1)
            for _ in range(3):
                tile = pltpu.roll(tile, 0, 1, stride=PATCH // 3, stride_axis=0)
            turned.append(tile)
        value = jnp.concatenate(turned, axis=0)
        ahead = jnp.where(column >= turn_of, value, 0.0)
        behind = jnp.where(column < turn_of, value, 0.0)
        both = jnp.concatenate([ahead, behind], axis=0)
        if not exact:
            return jnp.dot(gather_rows, both.astype(BF16), preferred_element_type=F32)
        high, low = halves(both)
        return jnp.dot(gather_rows, high, preferred_element_type=F32) + jnp.dot(
            gather_rows, low, preferred_element_type=F32
        )

    base_params[0:56, :] = flatten_rows(plain_one.astype(F32), False)
    base_params[54:182, :] = w2.astype(F32)
    base_params[182:188, :] = output_ref[...].astype(F32)

    for t in range(TILES):
        own = jnp.zeros((8, LANES), F32)
        for first, end, j, part in segments(t):
            if part == "main" and HALO <= j < HALO + ROWS:
                own = jnp.where((lane >= first) & (lane < end), 1.0, own)
        own_ref[:, t * LANES : (t + 1) * LANES] = jnp.concatenate([own] * (HID // 8), axis=0).astype(BF16)

    mix_to = []
    mix_from = []
    for g in range(FIELDS):
        to_tile = jnp.zeros((8, LANES), F32)
        from_tile = jnp.zeros((8, LANES), F32)
        for f in range(FIELDS):
            to_tile = jnp.where(sub == f, mix_ref[f, g], to_tile)
            from_tile = jnp.where(sub == f, mix_ref[g, f], from_tile)
        mix_to.append(to_tile)
        mix_from.append(from_tile)

    pl.semaphore_wait(here_sem.at[0], told)
    told = tell(1, 2)

    def mixed(tiles, value):
        length = value.shape[1]
        total = None
        for g in range(FIELDS):
            term = spread_lanes(tiles[g], length) * jnp.broadcast_to(value[g : g + 1, :], (8, length))
            total = term if total is None else total + term
        return total

    pl.semaphore_wait(here_sem.at[1], told)
    told = tell(2, 4)
    all_halos = halo_copy(halo_in, halo_in, {"lon": east})
    all_halos.wait_recv()

    def top(value):
        return jnp.where(lat > 0, value, 0.0)

    def bottom(value):
        return jnp.where(lat < NLAT - 1, value, 0.0)

    blank = jnp.zeros((8, LANES), F32)
    sides = []
    for which in range(2):
        sides.append(
            {
                "left": (top(halo_in[12 + which]), halo_in[14 + which], bottom(halo_in[16 + which])),
                "right": (top(halo_in[18 + which]), halo_in[20 + which], bottom(halo_in[22 + which])),
            }
        )

    def source(which, j, part):
        if which == 1 and (j < 2 or j >= EXT - 2):
            return blank
        if part != "main":
            return sides[which][part][0 if j < HALO else 1 if j < HALO + ROWS else 2]
        if j < HALO:
            return top(halo_in[j if which == 0 else HALO + j - 2])
        if j < HALO + ROWS:
            return (own_a if which == 0 else own_b)[j - HALO]
        return bottom(halo_in[6 + (j - HALO - ROWS if which == 0 else j - ROWS)])

    for t in range(TILES):
        here = slice(t * LANES, (t + 1) * LANES)
        for which, target in ((0, flat_a), (1, flat_b)):
            value = blank
            for first, end, j, part in segments(t):
                piece = source(which, j, part)
                value = jnp.where((lane >= first) & (lane < end), piece, value)
            target[:, here] = value
            if which == 0:
                wide_mask[:, here] = jnp.broadcast_to(value[6:7, :], (8, LANES))
                wide_diff[:, here] = jnp.broadcast_to(value[7:8, :], (8, LANES))

    def shift(value, amount):
        return pltpu.roll(value, (-amount) % FLAT, 1)

    def make_patch(value, patch_ref):
        blocks = [value if (p, q) == (0, 0) else shift(value, p * PITCH + q) for p, q in offsets]
        for m in range(5):
            after = blocks[2 * m + 1] if m < 4 else jnp.zeros_like(value)
            patch_ref[16 * m : 16 * m + 16, :] = jnp.concatenate([blocks[2 * m], after], axis=0).astype(BF16)
        lap_ref[...] = blocks[1] + blocks[7] + blocks[3] + blocks[5] - 4.0 * value

    def forward(state_ref, patch_ref, one_ref, two_ref, next_ref, low, high, write_low, write_high):
        for start, size in chunks(low, high):
            here = slice(start, start + size)
            one = jnp.tanh(jnp.dot(w1, patch_ref[:, here], preferred_element_type=F32)).astype(BF16)
            one_ref[:, here] = one
            two = jnp.tanh(jnp.dot(w2, one, preferred_element_type=F32)).astype(BF16)
            two_ref[:, here] = two
            tendency = jnp.dot(w3, two, preferred_element_type=F32)[0:8]
            centre = state_ref[:, here]
            update = (
                centre
                + wide_diff[:, here] * lap_ref[:, here]
                + (mixed(mix_to, centre) + closure_dt * tendency)
            )
            next_ref[:, here] = wide_mask[:, here] * update

    state_one[...] = jnp.zeros_like(state_one)
    make_patch(flat_a[...], patch_zero)
    low, high = tile_range(3)
    forward(flat_a, patch_zero, hid_one_zero, hid_two_zero, state_one, low, high, low, high)
    make_patch(state_one[...], patch_one)
    low, high = tile_range(2)
    forward(state_one, patch_one, hid_one_one, hid_two_one, state_two, low, high, low, high)

    def write_rows(source_ref, target_ref):
        for r in range(ROWS):
            start = (r + HALO) * PITCH + HALO
            t, turn = start // LANES, start % LANES
            before = source_ref[:, t * LANES : (t + 1) * LANES]
            after = source_ref[:, (t + 1) * LANES : (t + 2) * LANES]
            value = pltpu.roll(jnp.where(lane >= turn, before, after), (LANES - turn) % LANES, 1)
            target_ref[:, r, :] = value[0:FIELDS]

    grad_low, grad_high = tile_range(0)
    grad_here = slice(grad_low, grad_high)

    def backward(adj_ref, patch_ref, one_ref, two_ref, low, high):
        for start, size in chunks(low, high):
            here = slice(start, start + size)
            masked = wide_mask[:, here] * adj_ref[:, here]
            low_grad = jnp.concatenate([closure_dt * masked, jnp.zeros_like(masked)], axis=0).astype(BF16)
            out_grad[:, here] = low_grad
            two = two_ref[:, here].astype(F32)
            grad_two = (
                jnp.dot(w3_t, low_grad, preferred_element_type=F32) * (1.0 - two * two)
            ).astype(BF16)
            back_two[:, here] = grad_two
            one = one_ref[:, here].astype(F32)
            grad_one = (
                jnp.dot(w2_t, grad_two, preferred_element_type=F32) * (1.0 - one * one)
            ).astype(BF16)
            back_one[:, here] = grad_one
            grad_zero = jnp.dot(w1_t, grad_one, preferred_element_type=F32)
            spread = wide_diff[:, here] * masked
            direct = masked + mixed(mix_from, masked) - 4.0 * spread
            for k in range(9):
                block = grad_zero[8 * k : 8 * k + 8]
                if k == 4:
                    block = block + direct
                elif k % 2:
                    block = block + spread
                patch_grad[8 * k : 8 * k + 8, here] = block
        own = own_ref[:, grad_here]
        grad_second = nt(back_two[:, grad_here], one_ref[:, grad_here] * own)
        grad_output = nt(out_grad[:, grad_here] * own[0:16], two_ref[:, grad_here])
        grad_first = nt(back_one[:, grad_here], patch_ref[:, grad_here] * own[0:DEEP])
        return grad_first, grad_second, grad_output

    def scatter():
        total = None
        for k, (p, q) in enumerate(offsets):
            block = patch_grad[8 * k : 8 * k + 8, :]
            if (p, q) != (0, 0):
                block = shift(block, -(p * PITCH + q))
            total = block if total is None else total + block
        return total

    patch_grad[...] = jnp.zeros_like(patch_grad)
    low, high = tile_range(2)
    late_first, late_second, late_output = backward(flat_b, patch_one, hid_one_one, hid_two_one, low, high)
    adj_one[...] = scatter()
    low, high = tile_range(1)
    first, second, output = backward(adj_one, patch_zero, hid_one_zero, hid_two_zero, low, high)
    first = first + late_first
    second = second + late_second
    output = output + late_output

    def copies_along(axis, here, steps, size, phase, source, target):
        made = []
        for place, d in enumerate(steps):
            peer = ring(here, d, size)
            made.append(
                pltpu.make_async_remote_copy(
                    src_ref=source(peer),
                    dst_ref=target(place),
                    send_sem=send_sem.at[phase],
                    recv_sem=recv_sem.at[phase],
                    device_id={axis: peer},
                    device_id_type=MESH,
                )
            )
        for copy in made:
            copy.start()

    def all_of(phase, buffer):
        return pltpu.make_async_remote_copy(
            src_ref=buffer,
            dst_ref=buffer,
            send_sem=send_sem.at[phase],
            recv_sem=recv_sem.at[phase],
            device_id={"lon": east},
            device_id_type=MESH,
        )

    core = lax.rem(lon, 2)
    chip = lax.div(lon, 2)
    twin = lon + 1 - 2 * core

    def twin_copy(phase, source, target):
        return pltpu.make_async_remote_copy(
            src_ref=source.at[1 - core],
            dst_ref=target,
            send_sem=send_sem.at[phase],
            recv_sem=recv_sem.at[phase],
            device_id={"lon": twin},
            device_id_type=MESH,
        )

    for c in range(CHUNKS):
        seconds[c % 2, c // 2] = second[16 * c : 16 * c + 16]
    twin_second = twin_copy(4, seconds, twin_seconds)
    twin_second.start()
    high_part, low_part = halves(first)
    narrow = jnp.dot(high_part, select, preferred_element_type=F32) + jnp.dot(
        low_part, select, preferred_element_type=F32
    )
    flat_first = flatten_rows(narrow, True)
    for c in range(CHUNKS):
        others[c % 2, c // 2] = flat_first[8 * c : 8 * c + 8] if c < CHUNKS - 1 else output[0:8]
    twin_other = twin_copy(5, others, twin_others)
    twin_other.start()
    twin_second.wait_recv()
    for m in range(CHUNKS // 2):
        grads[m, 0:16, :] = seconds[core, m] + twin_seconds[m]
    twin_other.wait_recv()
    for m in range(CHUNKS // 2):
        grads[m, 16:CHUNK, :] = others[core, m] + twin_others[m]
    pl.semaphore_wait(here_sem.at[2], told)
    copies_along(
        "lon", lon, CHIP_STEPS, NLON, 1,
        lambda peer: grads.at[lax.rem(lax.div(peer, 2), 4)], lambda place: recv_one.at[chip],
    )
    recv_one[chip] = grads[lax.rem(chip, 4)]

    write_rows(state_two, final_ref)
    adj_one[...] = scatter()
    write_rows(adj_one, adjoint_ref)

    scatters = all_of(1, recv_one.at[0 : NLON // 2 - 1])
    scatters.wait_recv()
    band = recv_one[0]
    for n in range(1, NLON // 2):
        band = band + recv_one[n]
    recv_two[lat] = band

    copies_along("lat", lat, LAT_STEPS, NLAT, 2, lambda peer: recv_two.at[lat], lambda place: recv_two.at[lat])
    exchanges = all_of(2, recv_two.at[0 : NLAT - 1])
    exchanges.wait_recv()
    total = recv_two[0]
    squares = total * total
    for b in range(1, NLAT):
        value = recv_two[b]
        total = total + value
        squares = squares + value * value
    mine = lax.rem(lon, CHUNKS)
    gathered[mine, 0:CHUNK, :] = total
    gathered[mine, CHUNK:SENT, :] = jnp.sum(squares, axis=0, keepdims=True)

    copies_along("lon", lon, NEAR_STEPS, NLON, 3, lambda peer: gathered.at[mine], lambda place: gathered.at[mine])
    loads[8].wait()
    collects = all_of(3, gathered.at[0 : CHUNKS - 1])
    collects.wait_recv()

    square_sum = jnp.zeros((CHUNK, LANES), F32)
    band_sum = jnp.zeros((1, LANES), F32)
    for c in range(CHUNKS):
        value = gathered[c, 0:CHUNK, :]
        square_sum = square_sum + value * value
        band_sum = band_sum + gathered[c, CHUNK:SENT, :]
        total_ref[54 + 16 * c : 70 + 16 * c, :] = value[0:16]
        if c < 6:
            total_ref[8 * c : 8 * c + 8, :] = value[16:24]
        elif c == 6:
            total_ref[48:54, :] = value[16:22]
        else:
            total_ref[182:188, :] = value[16:22]
    grad_square = jnp.sum(jnp.sum(square_sum, axis=0, keepdims=True), axis=1, keepdims=True)
    band_square = jnp.sum(band_sum, axis=1, keepdims=True)
    ratio_ref[...] = jnp.broadcast_to(band_square / (grad_square + epsilon), (1, LANES))
    scale = learn_rate / jnp.sqrt(jnp.broadcast_to(grad_square, (1, LANES)) / PARAMS + epsilon)
    params_ref[...] = base_params[0:188, :] - scale * total_ref[0:188, :] + noise_in[...]

    for copies in (all_halos, twin_second, twin_other, scatters, exchanges, collects):
        copies.wait_send()


def emit(final_in, adjoint_in, params_in, ratio_in, final_out, adjoint_out, params_out, ratio_out, held, sem):
    pairs = ((final_in, final_out), (adjoint_in, adjoint_out), (params_in, params_out))
    copies = [pltpu.make_async_copy(src, dst, sem.at[n]) for n, (src, dst) in enumerate(pairs)]
    for copy in copies:
        copy.start()
    held[0] = ratio_in[0, 0]
    copies.append(pltpu.make_async_copy(held, ratio_out, sem.at[3]))
    copies[3].start()
    for copy in copies:
        copy.wait()


def on_device(
    initial_state,
    diffusion,
    mixing,
    land_mask,
    first_layer,
    second_layer,
    output_layer,
    cotangent,
    update_noise,
):
    vmem = pltpu.VMEM
    flat8 = vmem((8, FLAT), F32)
    hidden = vmem((HID, FLAT), BF16)
    dma = pltpu.SemaphoreType.DMA
    scratch = [
        vmem((FIELDS, ROWS, COLS), F32),
        vmem((ROWS, COLS), F32),
        vmem((ROWS, COLS), jnp.int32),
        vmem((FIELDS, ROWS, COLS), F32),
        vmem((188, LANES), F32),
        pltpu.SMEM((FIELDS, FIELDS), F32),
        vmem((PATCH, HID), BF16),
        vmem((HID, HID), BF16),
        vmem((FIELDS, HID), BF16),
        dma((9,)),
        vmem((ROWS, 8, LANES), F32),
        vmem((ROWS, 8, LANES), F32),
        vmem((6, 8, LANES), F32),
        vmem((6, 8, LANES), F32),
        vmem((2, 8, LANES), F32),
        vmem((24, 8, LANES), F32),
        pltpu.SemaphoreType.REGULAR((3,)),
        dma((6,)),
        dma((6,)),
        flat8,
        flat8,
        hidden,
        flat8,
        flat8,
        flat8,
        flat8,
        flat8,
        vmem((DEEP, FLAT), BF16),
        vmem((DEEP, FLAT), BF16),
        hidden,
        hidden,
        hidden,
        hidden,
        hidden,
        hidden,
        vmem((16, FLAT), BF16),
        vmem((72, FLAT), F32),
        flat8,
        vmem((HID, LANES), F32),
        vmem((16, LANES), F32),
        vmem((192, LANES), F32),
        vmem((2, CHUNKS // 2, 16, LANES), F32),
        vmem((2, CHUNKS // 2, 8, LANES), F32),
        vmem((CHUNKS // 2, 16, LANES), F32),
        vmem((CHUNKS // 2, 8, LANES), F32),
        vmem((CHUNKS // 2, CHUNK, LANES), F32),
        vmem((NLON // 2, CHUNK, LANES), F32),
        vmem((NLAT, CHUNK, LANES), F32),
        vmem((CHUNKS, SENT, LANES), F32),
        vmem((192, LANES), F32),
    ]
    hbm = pl.BlockSpec(memory_space=pltpu.HBM)
    local = pl.BlockSpec(memory_space=pltpu.VMEM)
    final, adjoint, params, ratio = pl.pallas_call(
        kernel,
        out_shape=(
            jax.ShapeDtypeStruct((FIELDS, ROWS, COLS), F32),
            jax.ShapeDtypeStruct((FIELDS, ROWS, COLS), F32),
            jax.ShapeDtypeStruct((188, LANES), F32),
            jax.ShapeDtypeStruct((1, LANES), F32),
        ),
        in_specs=[hbm] * 9,
        out_specs=(local,) * 4,
        scratch_shapes=scratch,
        compiler_params=pltpu.CompilerParams(
            collective_id=0, has_side_effects=True, vmem_limit_bytes=40 * 1024 * 1024
        ),
        name="ocean",
    )(
        *(
            pltpu.with_memory_space_constraint(value, pltpu.HBM)
            for value in (
                initial_state,
                diffusion,
                mixing,
                land_mask,
                first_layer.T,
                second_layer,
                output_layer,
                cotangent,
                update_noise.reshape(188, LANES),
            )
        )
    )
    final, adjoint, params, ratio = pl.pallas_call(
        emit,
        out_shape=(
            jax.ShapeDtypeStruct((FIELDS, ROWS, COLS), F32),
            jax.ShapeDtypeStruct((FIELDS, ROWS, COLS), F32),
            jax.ShapeDtypeStruct((188, LANES), F32),
            jax.ShapeDtypeStruct((1,), F32),
        ),
        in_specs=[local] * 4,
        out_specs=(hbm,) * 4,
        scratch_shapes=[pltpu.SMEM((1,), F32), dma((4,))],
        name="emit",
    )(*(pltpu.with_memory_space_constraint(value, pltpu.VMEM) for value in (final, adjoint, params, ratio)))
    return final, adjoint, params.reshape(PARAMS), ratio


def solution(mesh):
    placed = (
        P("ens", "lat", "lon"),
        P("lat", "lon"),
        P(),
        P("lat", "lon"),
        P(),
        P(),
        P(),
        P("ens", "lat", "lon"),
        P("ens"),
    )
    return jax.shard_map(
        on_device,
        mesh=mesh,
        in_specs=placed,
        out_specs=(P("ens", "lat", "lon"), P("ens", "lat", "lon"), P("ens"), P("ens")),
        check_vma=False,
    )
```

```python
import functools
import math
from types import SimpleNamespace

import jax
import jax.numpy as jnp
from jax import lax
from jax.experimental import pallas as pl
from jax.experimental.pallas import tpu as pltpu
from jax.sharding import PartitionSpec as P

MESH = pl.DeviceIdType.MESH
F32 = jnp.float32
BF16 = jnp.bfloat16

closure_dt = 0.1
learn_rate = 0.1
epsilon = 1e-06
offsets = [(p, q) for p in (-1, 0, 1) for q in (-1, 0, 1)]

FIELDS, ROWS, COLS = 6, 16, 128
HALO = 4
PITCH = COLS + 2 * HALO
EXT = ROWS + 2 * HALO
LANES = 128
TILES = -(-EXT * PITCH // LANES)
FLAT = TILES * LANES
HID = 128
PATCH = 54
DEEP = 80
PARAMS = 24064
NLON, NLAT = 16, 8
CHUNKS = 8
CHUNK = 24
SENT = CHUNK + 1
CHIP_STEPS = (8, 6, 10, 4, 12, 2, 14)
NEAR_STEPS = (4, 13, 3, 14, 2, 15, 1)
LON_STEPS = (8, 6, 10, 4, 12, 3, 13, 2, 14, 1, 15)
LAT_STEPS = (2, 6, 1, 3, 5, 7, 4)


def ring(index, step, size):
    return lax.rem(index + step + size, size)


def tile_range(distance):
    low = (HALO - distance) * PITCH // LANES
    high = -(-(HALO + ROWS + distance) * PITCH // LANES)
    if (high - low) % 2:
        low, high = (low, high + 1) if high < TILES else (low - 1, high)
    return low * LANES, high * LANES


def chunks(low, high, size=4096):
    return [(start, min(size, high - start)) for start in range(low, high, size)]


def spread_lanes(tile, length):
    return jnp.concatenate([tile] * (length // LANES), axis=1)


def segments(tile):
    found = []
    base = tile * LANES
    for row in range(EXT):
        start = row * PITCH
        for part, low, high in (
            ("left", start, start + HALO),
            ("main", start + HALO, start + HALO + COLS),
            ("right", start + HALO + COLS, start + PITCH),
        ):
            first, end = max(low, base), min(high, base + LANES)
            if first < end:
                found.append((first - base, end - base, row, part))
    return found


def kernel(
    state_hbm,
    diff_hbm,
    mix_hbm,
    mask_hbm,
    first_hbm,
    second_hbm,
    output_hbm,
    cot_hbm,
    noise_hbm,
    final_ref,
    adjoint_ref,
    params_ref,
    ratio_ref,
    state_in,
    diff_in,
    mask_in,
    cot_in,
    noise_in,
    mix_ref,
    first_ref,
    second_ref,
    output_ref,
    load_sem,
    own_a,
    own_b,
    send_north,
    send_south,
    edge,
    halo_in,
    here_sem,
    send_sem,
    recv_sem,
    flat_a,
    flat_b,
    own_ref,
    wide_mask,
    wide_diff,
    state_one,
    state_two,
    lap_ref,
    patch_zero,
    patch_one,
    hid_one_zero,
    hid_two_zero,
    hid_one_one,
    hid_two_one,
    back_one,
    back_two,
    out_grad,
    patch_grad,
    adj_one,
    weights_one,
    weights_three,
    base_params,
    seconds,
    others,
    twin_seconds,
    twin_others,
    grads,
    recv_one,
    recv_two,
    gathered,
    total_ref,
):
    lat = lax.axis_index("lat")
    lon = lax.axis_index("lon")
    north, south = ring(lat, -1, NLAT), ring(lat, 1, NLAT)
    west, east = ring(lon, -1, NLON), ring(lon, 1, NLON)

    barrier = pltpu.get_barrier_semaphore()
    greet = [{"lat": a, "lon": b} for a in (north, south) for b in (west, east)]
    greet += [{"lat": north}, {"lat": south}, {"lon": west}, {"lon": east}]
    for device in greet:
        pl.semaphore_signal(barrier, inc=1, device_id=device, device_id_type=MESH)

    loads = [
        pltpu.make_async_copy(src, dst, load_sem.at[n])
        for n, (src, dst) in enumerate(
            (
                (state_hbm, state_in),
                (mask_hbm, mask_in),
                (diff_hbm, diff_in),
                (cot_hbm, cot_in),
                (mix_hbm, mix_ref),
                (first_hbm, first_ref),
                (second_hbm, second_ref),
                (output_hbm, output_ref),
                (noise_hbm, noise_in),
            )
        )
    ]
    for load in loads:
        load.start()

    lane = lax.broadcasted_iota(jnp.int32, (8, LANES), 1)
    sub = lax.broadcasted_iota(jnp.int32, (8, LANES), 0)
    for load in loads[:4]:
        load.wait()

    own_b[...] = jnp.zeros_like(own_b)
    for r in range(ROWS):
        own_a[r, 0:FIELDS, :] = state_in[:, r, :]
        own_a[r, 6:7, :] = mask_in[r : r + 1, :].astype(F32)
        own_a[r, 7:8, :] = diff_in[r : r + 1, :]
        own_b[r, 0:FIELDS, :] = cot_in[:, r, :]
    edge_a = jnp.zeros((8, LANES), F32)
    edge_b = jnp.zeros((8, LANES), F32)
    for r in range(ROWS):
        j = r + HALO
        turn = (j * PITCH + HALO) % LANES
        tile_a = pltpu.roll(own_a[r], turn, 1)
        tile_b = pltpu.roll(own_b[r], turn, 1)
        own_a[r] = tile_a
        own_b[r] = tile_b
        place = (j * PITCH) % LANES
        pick = (lane >= place) & (lane < place + 2 * HALO)
        edge_a = jnp.where(pick, tile_a, edge_a)
        edge_b = jnp.where(pick, tile_b, edge_b)
        if r < HALO:
            send_north[r] = tile_a
        if r < 2:
            send_north[HALO + r] = tile_b
        if r >= ROWS - HALO:
            send_south[r - (ROWS - HALO)] = tile_a
        if r >= ROWS - 2:
            send_south[HALO + r - (ROWS - 2)] = tile_b
    edge[0] = edge_a
    edge[1] = edge_b

    pl.semaphore_wait(barrier, len(greet))

    def halo_copy(source, target, device):
        return pltpu.make_async_remote_copy(
            src_ref=source,
            dst_ref=target,
            send_sem=send_sem.at[0],
            recv_sem=recv_sem.at[0],
            device_id=device,
            device_id_type=MESH,
        )

    from_north, from_south = halo_in.at[0:6], halo_in.at[6:12]
    edges_in = [halo_in.at[12 + 2 * n : 14 + 2 * n] for n in range(6)]
    halos = [
        halo_copy(edge, edges_in[0], {"lat": south, "lon": east}),
        halo_copy(edge, edges_in[2], {"lat": north, "lon": east}),
        halo_copy(edge, edges_in[3], {"lat": south, "lon": west}),
        halo_copy(edge, edges_in[5], {"lat": north, "lon": west}),
        halo_copy(send_north, from_south, {"lat": north}),
        halo_copy(send_south, from_north, {"lat": south}),
        halo_copy(edge, edges_in[1], {"lon": east}),
        halo_copy(edge, edges_in[4], {"lon": west}),
    ]
    for copy in halos:
        copy.start()

    def tell(stage, reach):
        devices = [{"lon": ring(lon, d, NLON)} for d in (reach, -reach)]
        if reach < NLAT // 2:
            devices += [{"lat": ring(lat, d, NLAT)} for d in (reach, -reach)]
        for device in devices:
            pl.semaphore_signal(here_sem.at[stage], inc=1, device_id=device, device_id_type=MESH)
        return len(devices)

    told = tell(0, 1)

    for load in loads[4:8]:
        load.wait()
    weights_one[...] = jnp.zeros_like(weights_one)
    weights_one[0:PATCH, :] = first_ref[...].astype(F32)
    weights_three[...] = jnp.zeros_like(weights_three)
    state_one[...] = jnp.zeros_like(state_one)
    patch_grad[...] = jnp.zeros_like(patch_grad)
    weights_three[0:FIELDS, :] = output_ref[...].astype(F32)

    def nt(left, right, precision=None):
        return lax.dot_general(
            left, right, (((1,), (1,)), ((), ())), preferred_element_type=F32, precision=precision
        )

    deep_i = lax.broadcasted_iota(jnp.int32, (DEEP, HID), 0)
    deep_j = lax.broadcasted_iota(jnp.int32, (DEEP, HID), 1)
    deep_f = lax.bitwise_and(deep_i, 7)
    picked = (deep_j == 6 * lax.shift_right_logical(deep_i, 3) + deep_f) & (deep_f < 6) & (deep_i < 72)
    select = jnp.where(picked, 1.0, 0.0).astype(BF16)
    row = lax.broadcasted_iota(jnp.int32, (HID, HID), 0)
    column = lax.broadcasted_iota(jnp.int32, (HID, HID), 1)
    eye = jnp.where(row == column, 1.0, 0.0).astype(BF16)
    turned_one = weights_one[...].astype(BF16)
    plain_one = nt(eye, turned_one).astype(BF16)
    w1 = nt(plain_one, select).astype(BF16)
    w1_t = jnp.dot(select, turned_one, preferred_element_type=F32).astype(BF16)
    w2 = second_ref[...]
    w2_t = nt(eye, w2).astype(BF16)
    w3 = weights_three[...].astype(BF16)
    w3_t = nt(eye, w3).astype(BF16)

    turn_of = lax.bitwise_and(row * PATCH, LANES - 1)
    deep_r = lax.broadcasted_iota(jnp.int32, (56, 2 * HID), 0)
    deep_h = lax.broadcasted_iota(jnp.int32, (56, 2 * HID), 1)
    hid_h = lax.bitwise_and(deep_h, HID - 1)
    lands = lax.shift_right_logical(hid_h * PATCH, 7) + lax.shift_right_logical(deep_h, 7)
    gather_rows = jnp.where(lands == deep_r, 1.0, 0.0).astype(BF16)

    def halves(value):
        high = value.astype(BF16)
        return high, (value - high.astype(F32)).astype(BF16)

    def flatten_rows(value, exact):
        turned = []
        for m in range(HID // 8):
            tile = value[8 * m : 8 * m + 8]
            if (8 * m * PATCH) % LANES:
                tile = pltpu.roll(tile, (8 * m * PATCH) % LANES, 1)
            for _ in range(3):
                tile = pltpu.roll(tile, 0, 1, stride=PATCH // 3, stride_axis=0)
            turned.append(tile)
        value = jnp.concatenate(turned, axis=0)
        ahead = jnp.where(column >= turn_of, value, 0.0)
        behind = jnp.where(column < turn_of, value, 0.0)
        both = jnp.concatenate([ahead, behind], axis=0)
        if not exact:
            return jnp.dot(gather_rows, both.astype(BF16), preferred_element_type=F32)
        high, low = halves(both)
        return jnp.dot(gather_rows, high, preferred_element_type=F32) + jnp.dot(
            gather_rows, low, preferred_element_type=F32
        )

    base_params[0:56, :] = flatten_rows(plain_one.astype(F32), False)
    base_params[54:182, :] = w2.astype(F32)
    base_params[182:188, :] = output_ref[...].astype(F32)

    for t in range(TILES):
        own = jnp.zeros((8, LANES), F32)
        for first, end, j, part in segments(t):
            if part == "main" and HALO <= j < HALO + ROWS:
                own = jnp.where((lane >= first) & (lane < end), 1.0, own)
        own_ref[:, t * LANES : (t + 1) * LANES] = jnp.concatenate([own] * (HID // 8), axis=0).astype(BF16)

    mix_to = []
    mix_from = []
    for g in range(FIELDS):
        to_tile = jnp.zeros((8, LANES), F32)
        from_tile = jnp.zeros((8, LANES), F32)
        for f in range(FIELDS):
            to_tile = jnp.where(sub == f, mix_ref[f, g], to_tile)
            from_tile = jnp.where(sub == f, mix_ref[g, f], from_tile)
        mix_to.append(to_tile)
        mix_from.append(from_tile)

    pl.semaphore_wait(here_sem.at[0], told)
    told = tell(1, 2)

    def mixed(tiles, value):
        length = value.shape[1]
        total = None
        for g in range(FIELDS):
            term = spread_lanes(tiles[g], length) * jnp.broadcast_to(value[g : g + 1, :], (8, length))
            total = term if total is None else total + term
        return total

    pl.semaphore_wait(here_sem.at[1], told)
    told = tell(2, 4)
    all_halos = halo_copy(halo_in, halo_in, {"lon": east})
    all_halos.wait_recv()

    def top(value):
        return jnp.where(lat > 0, value, 0.0)

    def bottom(value):
        return jnp.where(lat < NLAT - 1, value, 0.0)

    blank = jnp.zeros((8, LANES), F32)
    sides = []
    for which in range(2):
        sides.append(
            {
                "left": (top(halo_in[12 + which]), halo_in[14 + which], bottom(halo_in[16 + which])),
                "right": (top(halo_in[18 + which]), halo_in[20 + which], bottom(halo_in[22 + which])),
            }
        )

    def source(which, j, part):
        if which == 1 and (j < 2 or j >= EXT - 2):
            return blank
        if part != "main":
            return sides[which][part][0 if j < HALO else 1 if j < HALO + ROWS else 2]
        if j < HALO:
            return top(halo_in[j if which == 0 else HALO + j - 2])
        if j < HALO + ROWS:
            return (own_a if which == 0 else own_b)[j - HALO]
        return bottom(halo_in[6 + (j - HALO - ROWS if which == 0 else j - ROWS)])

    for t in range(TILES):
        here = slice(t * LANES, (t + 1) * LANES)
        for which, target in ((0, flat_a), (1, flat_b)):
            value = blank
            for first, end, j, part in segments(t):
                piece = source(which, j, part)
                value = jnp.where((lane >= first) & (lane < end), piece, value)
            target[:, here] = value
            if which == 0:
                wide_mask[:, here] = jnp.broadcast_to(value[6:7, :], (8, LANES))
                wide_diff[:, here] = jnp.broadcast_to(value[7:8, :], (8, LANES))

    def shift(value, amount):
        return pltpu.roll(value, (-amount) % FLAT, 1)

    def make_patch(value, patch_ref):
        blocks = [value if (p, q) == (0, 0) else shift(value, p * PITCH + q) for p, q in offsets]
        for m in range(5):
            after = blocks[2 * m + 1] if m < 4 else jnp.zeros_like(value)
            patch_ref[16 * m : 16 * m + 16, :] = jnp.concatenate([blocks[2 * m], after], axis=0).astype(BF16)
        lap_ref[...] = blocks[1] + blocks[7] + blocks[3] + blocks[5] - 4.0 * value

    def forward(state_ref, patch_ref, one_ref, two_ref, next_ref, low, high, write_low, write_high):
        for start, size in chunks(low, high):
            here = slice(start, start + size)
            one = jnp.tanh(jnp.dot(w1, patch_ref[:, here], preferred_element_type=F32)).astype(BF16)
            one_ref[:, here] = one
            two = jnp.tanh(jnp.dot(w2, one, preferred_element_type=F32)).astype(BF16)
            two_ref[:, here] = two
            tendency = jnp.dot(w3, two, preferred_element_type=F32)[0:8]
            centre = state_ref[:, here]
            update = (
                centre
                + wide_diff[:, here] * lap_ref[:, here]
                + (mixed(mix_to, centre) + closure_dt * tendency)
            )
            next_ref[:, here] = wide_mask[:, here] * update

    make_patch(flat_a[...], patch_zero)
    low, high = tile_range(3)
    forward(flat_a, patch_zero, hid_one_zero, hid_two_zero, state_one, low, high, low, high)
    make_patch(state_one[...], patch_one)
    low, high = tile_range(2)
    forward(state_one, patch_one, hid_one_one, hid_two_one, state_two, low, high, low, high)

    def write_rows(source_ref, target_ref):
        for r in range(ROWS):
            start = (r + HALO) * PITCH + HALO
            t, turn = start // LANES, start % LANES
            before = source_ref[:, t * LANES : (t + 1) * LANES]
            after = source_ref[:, (t + 1) * LANES : (t + 2) * LANES]
            value = pltpu.roll(jnp.where(lane >= turn, before, after), (LANES - turn) % LANES, 1)
            target_ref[:, r, :] = value[0:FIELDS]

    grad_low, grad_high = tile_range(0)
    grad_here = slice(grad_low, grad_high)

    def backward(adj_ref, patch_ref, one_ref, two_ref, low, high):
        for start, size in chunks(low, high):
            here = slice(start, start + size)
            masked = wide_mask[:, here] * adj_ref[:, here]
            low_grad = jnp.concatenate([closure_dt * masked, jnp.zeros_like(masked)], axis=0).astype(BF16)
            out_grad[:, here] = low_grad
            two = two_ref[:, here].astype(F32)
            grad_two = (
                jnp.dot(w3_t, low_grad, preferred_element_type=F32) * (1.0 - two * two)
            ).astype(BF16)
            back_two[:, here] = grad_two
            one = one_ref[:, here].astype(F32)
            grad_one = (
                jnp.dot(w2_t, grad_two, preferred_element_type=F32) * (1.0 - one * one)
            ).astype(BF16)
            back_one[:, here] = grad_one
            grad_zero = jnp.dot(w1_t, grad_one, preferred_element_type=F32)
            spread = wide_diff[:, here] * masked
            direct = masked + mixed(mix_from, masked) - 4.0 * spread
            for k in range(9):
                block = grad_zero[8 * k : 8 * k + 8]
                if k == 4:
                    block = block + direct
                elif k % 2:
                    block = block + spread
                patch_grad[8 * k : 8 * k + 8, here] = block
        own = own_ref[:, grad_here]
        grad_second = nt(back_two[:, grad_here], one_ref[:, grad_here] * own)
        grad_output = nt(out_grad[:, grad_here] * own[0:16], two_ref[:, grad_here])
        grad_first = nt(back_one[:, grad_here], patch_ref[:, grad_here] * own[0:DEEP])
        return grad_first, grad_second, grad_output

    def scatter():
        total = None
        for k, (p, q) in enumerate(offsets):
            block = patch_grad[8 * k : 8 * k + 8, :]
            if (p, q) != (0, 0):
                block = shift(block, -(p * PITCH + q))
            total = block if total is None else total + block
        return total

    low, high = tile_range(2)
    late_first, late_second, late_output = backward(flat_b, patch_one, hid_one_one, hid_two_one, low, high)
    adj_one[...] = scatter()
    low, high = tile_range(1)
    first, second, output = backward(adj_one, patch_zero, hid_one_zero, hid_two_zero, low, high)
    first = first + late_first
    second = second + late_second
    output = output + late_output

    def copies_along(axis, here, steps, size, phase, source, target):
        made = []
        for place, d in enumerate(steps):
            peer = ring(here, d, size)
            made.append(
                pltpu.make_async_remote_copy(
                    src_ref=source(peer),
                    dst_ref=target(place),
                    send_sem=send_sem.at[phase],
                    recv_sem=recv_sem.at[phase],
                    device_id={axis: peer},
                    device_id_type=MESH,
                )
            )
        for copy in made:
            copy.start()

    def all_of(phase, buffer):
        return pltpu.make_async_remote_copy(
            src_ref=buffer,
            dst_ref=buffer,
            send_sem=send_sem.at[phase],
            recv_sem=recv_sem.at[phase],
            device_id={"lon": east},
            device_id_type=MESH,
        )

    core = lax.rem(lon, 2)
    chip = lax.div(lon, 2)
    twin = lon + 1 - 2 * core

    def twin_copy(phase, source, target):
        return pltpu.make_async_remote_copy(
            src_ref=source.at[1 - core],
            dst_ref=target,
            send_sem=send_sem.at[phase],
            recv_sem=recv_sem.at[phase],
            device_id={"lon": twin},
            device_id_type=MESH,
        )

    for c in range(CHUNKS):
        seconds[c % 2, c // 2] = second[16 * c : 16 * c + 16]
    twin_second = twin_copy(4, seconds, twin_seconds)
    twin_second.start()
    high_part, low_part = halves(first)
    narrow = jnp.dot(high_part, select, preferred_element_type=F32) + jnp.dot(
        low_part, select, preferred_element_type=F32
    )
    flat_first = flatten_rows(narrow, True)
    for c in range(CHUNKS):
        others[c % 2, c // 2] = flat_first[8 * c : 8 * c + 8] if c < CHUNKS - 1 else output[0:8]
    twin_other = twin_copy(5, others, twin_others)
    twin_other.start()
    twin_second.wait_recv()
    for m in range(CHUNKS // 2):
        grads[m, 0:16, :] = seconds[core, m] + twin_seconds[m]
    twin_other.wait_recv()
    for m in range(CHUNKS // 2):
        grads[m, 16:CHUNK, :] = others[core, m] + twin_others[m]
    pl.semaphore_wait(here_sem.at[2], told)
    copies_along(
        "lon", lon, CHIP_STEPS, NLON, 1,
        lambda peer: grads.at[lax.rem(lax.div(peer, 2), 4)], lambda place: recv_one.at[chip],
    )
    recv_one[chip] = grads[lax.rem(chip, 4)]

    write_rows(state_two, final_ref)
    adj_one[...] = scatter()
    write_rows(adj_one, adjoint_ref)

    scatters = all_of(1, recv_one.at[0 : NLON // 2 - 1])
    scatters.wait_recv()
    band = recv_one[0]
    for n in range(1, NLON // 2):
        band = band + recv_one[n]
    recv_two[lat] = band

    copies_along("lat", lat, LAT_STEPS, NLAT, 2, lambda peer: recv_two.at[lat], lambda place: recv_two.at[lat])
    exchanges = all_of(2, recv_two.at[0 : NLAT - 1])
    exchanges.wait_recv()
    total = recv_two[0]
    squares = total * total
    for b in range(1, NLAT):
        value = recv_two[b]
        total = total + value
        squares = squares + value * value
    mine = lax.rem(lon, CHUNKS)
    gathered[mine, 0:CHUNK, :] = total
    gathered[mine, CHUNK:SENT, :] = jnp.sum(squares, axis=0, keepdims=True)

    copies_along("lon", lon, NEAR_STEPS, NLON, 3, lambda peer: gathered.at[mine], lambda place: gathered.at[mine])
    loads[8].wait()
    collects = all_of(3, gathered.at[0 : CHUNKS - 1])
    collects.wait_recv()

    square_sum = jnp.zeros((CHUNK, LANES), F32)
    band_sum = jnp.zeros((1, LANES), F32)
    for c in range(CHUNKS):
        value = gathered[c, 0:CHUNK, :]
        square_sum = square_sum + value * value
        band_sum = band_sum + gathered[c, CHUNK:SENT, :]
        total_ref[54 + 16 * c : 70 + 16 * c, :] = value[0:16]
        if c < 6:
            total_ref[8 * c : 8 * c + 8, :] = value[16:24]
        elif c == 6:
            total_ref[48:54, :] = value[16:22]
        else:
            total_ref[182:188, :] = value[16:22]
    grad_square = jnp.sum(jnp.sum(square_sum, axis=0, keepdims=True), axis=1, keepdims=True)
    band_square = jnp.sum(band_sum, axis=1, keepdims=True)
    ratio_ref[...] = jnp.broadcast_to(band_square / (grad_square + epsilon), (1, LANES))
    scale = learn_rate / jnp.sqrt(jnp.broadcast_to(grad_square, (1, LANES)) / PARAMS + epsilon)
    params_ref[...] = base_params[0:188, :] - scale * total_ref[0:188, :] + noise_in[...]

    for copies in (all_halos, twin_second, twin_other, scatters, exchanges, collects):
        copies.wait_send()


def emit(final_in, adjoint_in, params_in, ratio_in, final_out, adjoint_out, params_out, ratio_out, held, sem):
    pairs = ((final_in, final_out), (adjoint_in, adjoint_out), (params_in, params_out))
    copies = [pltpu.make_async_copy(src, dst, sem.at[n]) for n, (src, dst) in enumerate(pairs)]
    for copy in copies:
        copy.start()
    held[0] = ratio_in[0, 0]
    copies.append(pltpu.make_async_copy(held, ratio_out, sem.at[3]))
    copies[3].start()
    for copy in copies:
        copy.wait()


def on_device(
    initial_state,
    diffusion,
    mixing,
    land_mask,
    first_layer,
    second_layer,
    output_layer,
    cotangent,
    update_noise,
):
    vmem = pltpu.VMEM
    flat8 = vmem((8, FLAT), F32)
    hidden = vmem((HID, FLAT), BF16)
    dma = pltpu.SemaphoreType.DMA
    scratch = [
        vmem((FIELDS, ROWS, COLS), F32),
        vmem((ROWS, COLS), F32),
        vmem((ROWS, COLS), jnp.int32),
        vmem((FIELDS, ROWS, COLS), F32),
        vmem((188, LANES), F32),
        pltpu.SMEM((FIELDS, FIELDS), F32),
        vmem((PATCH, HID), BF16),
        vmem((HID, HID), BF16),
        vmem((FIELDS, HID), BF16),
        dma((9,)),
        vmem((ROWS, 8, LANES), F32),
        vmem((ROWS, 8, LANES), F32),
        vmem((6, 8, LANES), F32),
        vmem((6, 8, LANES), F32),
        vmem((2, 8, LANES), F32),
        vmem((24, 8, LANES), F32),
        pltpu.SemaphoreType.REGULAR((3,)),
        dma((6,)),
        dma((6,)),
        flat8,
        flat8,
        hidden,
        flat8,
        flat8,
        flat8,
        flat8,
        flat8,
        vmem((DEEP, FLAT), BF16),
        vmem((DEEP, FLAT), BF16),
        hidden,
        hidden,
        hidden,
        hidden,
        hidden,
        hidden,
        vmem((16, FLAT), BF16),
        vmem((72, FLAT), F32),
        flat8,
        vmem((HID, LANES), F32),
        vmem((16, LANES), F32),
        vmem((192, LANES), F32),
        vmem((2, CHUNKS // 2, 16, LANES), F32),
        vmem((2, CHUNKS // 2, 8, LANES), F32),
        vmem((CHUNKS // 2, 16, LANES), F32),
        vmem((CHUNKS // 2, 8, LANES), F32),
        vmem((CHUNKS // 2, CHUNK, LANES), F32),
        vmem((NLON // 2, CHUNK, LANES), F32),
        vmem((NLAT, CHUNK, LANES), F32),
        vmem((CHUNKS, SENT, LANES), F32),
        vmem((192, LANES), F32),
    ]
    hbm = pl.BlockSpec(memory_space=pltpu.HBM)
    local = pl.BlockSpec(memory_space=pltpu.VMEM)
    final, adjoint, params, ratio = pl.pallas_call(
        kernel,
        out_shape=(
            jax.ShapeDtypeStruct((FIELDS, ROWS, COLS), F32),
            jax.ShapeDtypeStruct((FIELDS, ROWS, COLS), F32),
            jax.ShapeDtypeStruct((188, LANES), F32),
            jax.ShapeDtypeStruct((1, LANES), F32),
        ),
        in_specs=[hbm] * 9,
        out_specs=(local,) * 4,
        scratch_shapes=scratch,
        compiler_params=pltpu.CompilerParams(
            collective_id=0, has_side_effects=True, vmem_limit_bytes=40 * 1024 * 1024
        ),
        name="ocean",
    )(
        *(
            pltpu.with_memory_space_constraint(value, pltpu.HBM)
            for value in (
                initial_state,
                diffusion,
                mixing,
                land_mask,
                first_layer.T,
                second_layer,
                output_layer,
                cotangent,
                update_noise.reshape(188, LANES),
            )
        )
    )
    final, adjoint, params, ratio = pl.pallas_call(
        emit,
        out_shape=(
            jax.ShapeDtypeStruct((FIELDS, ROWS, COLS), F32),
            jax.ShapeDtypeStruct((FIELDS, ROWS, COLS), F32),
            jax.ShapeDtypeStruct((188, LANES), F32),
            jax.ShapeDtypeStruct((1,), F32),
        ),
        in_specs=[local] * 4,
        out_specs=(hbm,) * 4,
        scratch_shapes=[pltpu.SMEM((1,), F32), dma((4,))],
        name="emit",
    )(*(pltpu.with_memory_space_constraint(value, pltpu.VMEM) for value in (final, adjoint, params, ratio)))
    return final, adjoint, params.reshape(PARAMS), ratio


def solution(mesh):
    placed = (
        P("ens", "lat", "lon"),
        P("lat", "lon"),
        P(),
        P("lat", "lon"),
        P(),
        P(),
        P(),
        P("ens", "lat", "lon"),
        P("ens"),
    )
    return jax.shard_map(
        on_device,
        mesh=mesh,
        in_specs=placed,
        out_specs=(P("ens", "lat", "lon"), P("ens", "lat", "lon"), P("ens"), P("ens")),
        check_vma=False,
    )
```

```python
import functools
import math
from types import SimpleNamespace

import jax
import jax.numpy as jnp
from jax import lax
from jax.experimental import pallas as pl
from jax.experimental.pallas import tpu as pltpu
from jax.sharding import PartitionSpec as P

MESH = pl.DeviceIdType.MESH
F32 = jnp.float32
BF16 = jnp.bfloat16

closure_dt = 0.1
learn_rate = 0.1
epsilon = 1e-06
offsets = [(p, q) for p in (-1, 0, 1) for q in (-1, 0, 1)]

FIELDS, ROWS, COLS = 6, 16, 128
HALO = 4
PITCH = COLS + 2 * HALO
EXT = ROWS + 2 * HALO
LANES = 128
TILES = -(-EXT * PITCH // LANES)
FLAT = TILES * LANES
HID = 128
PATCH = 54
DEEP = 80
PARAMS = 24064
NLON, NLAT = 16, 8
CHUNKS = 8
CHUNK = 24
SENT = CHUNK + 1
CHIP_STEPS = (8, 6, 10, 4, 12, 2, 14)
NEAR_STEPS = (4, 13, 3, 14, 2, 15, 1)
LON_STEPS = (8, 6, 10, 4, 12, 3, 13, 2, 14, 1, 15)
LAT_STEPS = (2, 6, 1, 3, 5, 7, 4)


def ring(index, step, size):
    return lax.rem(index + step + size, size)


def tile_range(distance):
    low = (HALO - distance) * PITCH // LANES
    high = -(-(HALO + ROWS + distance) * PITCH // LANES)
    if (high - low) % 2:
        low, high = (low, high + 1) if high < TILES else (low - 1, high)
    return low * LANES, high * LANES


def chunks(low, high, size=4096):
    return [(start, min(size, high - start)) for start in range(low, high, size)]


def spread_lanes(tile, length):
    return jnp.concatenate([tile] * (length // LANES), axis=1)


def segments(tile):
    found = []
    base = tile * LANES
    for row in range(EXT):
        start = row * PITCH
        for part, low, high in (
            ("left", start, start + HALO),
            ("main", start + HALO, start + HALO + COLS),
            ("right", start + HALO + COLS, start + PITCH),
        ):
            first, end = max(low, base), min(high, base + LANES)
            if first < end:
                found.append((first - base, end - base, row, part))
    return found


def kernel(
    state_hbm,
    diff_hbm,
    mix_hbm,
    mask_hbm,
    first_hbm,
    second_hbm,
    output_hbm,
    cot_hbm,
    noise_hbm,
    final_ref,
    adjoint_ref,
    params_ref,
    ratio_ref,
    state_in,
    diff_in,
    mask_in,
    cot_in,
    noise_in,
    mix_ref,
    first_ref,
    second_ref,
    output_ref,
    load_sem,
    own_a,
    own_b,
    send_north,
    send_south,
    edge,
    halo_in,
    here_sem,
    send_sem,
    recv_sem,
    flat_a,
    flat_b,
    own_ref,
    wide_mask,
    wide_diff,
    state_one,
    state_two,
    lap_ref,
    patch_zero,
    patch_one,
    hid_one_zero,
    hid_two_zero,
    hid_one_one,
    hid_two_one,
    back_one,
    back_two,
    out_grad,
    late_one,
    late_two,
    late_out,
    patch_grad,
    adj_one,
    weights_one,
    weights_three,
    base_params,
    seconds,
    others,
    twin_seconds,
    twin_others,
    grads,
    recv_one,
    recv_two,
    gathered,
    total_ref,
):
    lat = lax.axis_index("lat")
    lon = lax.axis_index("lon")
    north, south = ring(lat, -1, NLAT), ring(lat, 1, NLAT)
    west, east = ring(lon, -1, NLON), ring(lon, 1, NLON)

    barrier = pltpu.get_barrier_semaphore()
    greet = [{"lat": a, "lon": b} for a in (north, south) for b in (west, east)]
    greet += [{"lat": north}, {"lat": south}, {"lon": west}, {"lon": east}]
    for device in greet:
        pl.semaphore_signal(barrier, inc=1, device_id=device, device_id_type=MESH)

    loads = [
        pltpu.make_async_copy(src, dst, load_sem.at[n])
        for n, (src, dst) in enumerate(
            (
                (state_hbm, state_in),
                (mask_hbm, mask_in),
                (diff_hbm, diff_in),
                (cot_hbm, cot_in),
                (mix_hbm, mix_ref),
                (first_hbm, first_ref),
                (second_hbm, second_ref),
                (output_hbm, output_ref),
                (noise_hbm, noise_in),
            )
        )
    ]
    for load in loads:
        load.start()

    lane = lax.broadcasted_iota(jnp.int32, (8, LANES), 1)
    sub = lax.broadcasted_iota(jnp.int32, (8, LANES), 0)
    for load in loads[:4]:
        load.wait()

    own_b[...] = jnp.zeros_like(own_b)
    for r in range(ROWS):
        own_a[r, 0:FIELDS, :] = state_in[:, r, :]
        own_a[r, 6:7, :] = mask_in[r : r + 1, :].astype(F32)
        own_a[r, 7:8, :] = diff_in[r : r + 1, :]
        own_b[r, 0:FIELDS, :] = cot_in[:, r, :]
    edge_a = jnp.zeros((8, LANES), F32)
    edge_b = jnp.zeros((8, LANES), F32)
    for r in range(ROWS):
        j = r + HALO
        turn = (j * PITCH + HALO) % LANES
        tile_a = pltpu.roll(own_a[r], turn, 1)
        tile_b = pltpu.roll(own_b[r], turn, 1)
        own_a[r] = tile_a
        own_b[r] = tile_b
        place = (j * PITCH) % LANES
        pick = (lane >= place) & (lane < place + 2 * HALO)
        edge_a = jnp.where(pick, tile_a, edge_a)
        edge_b = jnp.where(pick, tile_b, edge_b)
        if r < HALO:
            send_north[r] = tile_a
        if r < 2:
            send_north[HALO + r] = tile_b
        if r >= ROWS - HALO:
            send_south[r - (ROWS - HALO)] = tile_a
        if r >= ROWS - 2:
            send_south[HALO + r - (ROWS - 2)] = tile_b
    edge[0] = edge_a
    edge[1] = edge_b

    pl.semaphore_wait(barrier, len(greet))

    def halo_copy(source, target, device):
        return pltpu.make_async_remote_copy(
            src_ref=source,
            dst_ref=target,
            send_sem=send_sem.at[0],
            recv_sem=recv_sem.at[0],
            device_id=device,
            device_id_type=MESH,
        )

    from_north, from_south = halo_in.at[0:6], halo_in.at[6:12]
    edges_in = [halo_in.at[12 + 2 * n : 14 + 2 * n] for n in range(6)]
    halos = [
        halo_copy(edge, edges_in[0], {"lat": south, "lon": east}),
        halo_copy(edge, edges_in[2], {"lat": north, "lon": east}),
        halo_copy(edge, edges_in[3], {"lat": south, "lon": west}),
        halo_copy(edge, edges_in[5], {"lat": north, "lon": west}),
        halo_copy(send_north, from_south, {"lat": north}),
        halo_copy(send_south, from_north, {"lat": south}),
        halo_copy(edge, edges_in[1], {"lon": east}),
        halo_copy(edge, edges_in[4], {"lon": west}),
    ]
    for copy in halos:
        copy.start()

    def tell(stage, reach):
        devices = [{"lon": ring(lon, d, NLON)} for d in (reach, -reach)]
        if reach < NLAT // 2:
            devices += [{"lat": ring(lat, d, NLAT)} for d in (reach, -reach)]
        for device in devices:
            pl.semaphore_signal(here_sem.at[stage], inc=1, device_id=device, device_id_type=MESH)
        return len(devices)

    told = tell(0, 1)

    for load in loads[4:8]:
        load.wait()
    weights_one[...] = jnp.zeros_like(weights_one)
    weights_one[0:PATCH, :] = first_ref[...].astype(F32)
    weights_three[...] = jnp.zeros_like(weights_three)
    state_one[...] = jnp.zeros_like(state_one)
    patch_grad[...] = jnp.zeros_like(patch_grad)
    weights_three[0:FIELDS, :] = output_ref[...].astype(F32)

    def nt(left, right, precision=None):
        return lax.dot_general(
            left, right, (((1,), (1,)), ((), ())), preferred_element_type=F32, precision=precision
        )

    deep_i = lax.broadcasted_iota(jnp.int32, (DEEP, HID), 0)
    deep_j = lax.broadcasted_iota(jnp.int32, (DEEP, HID), 1)
    deep_f = lax.bitwise_and(deep_i, 7)
    picked = (deep_j == 6 * lax.shift_right_logical(deep_i, 3) + deep_f) & (deep_f < 6) & (deep_i < 72)
    select = jnp.where(picked, 1.0, 0.0).astype(BF16)
    row = lax.broadcasted_iota(jnp.int32, (HID, HID), 0)
    column = lax.broadcasted_iota(jnp.int32, (HID, HID), 1)
    eye = jnp.where(row == column, 1.0, 0.0).astype(BF16)
    turned_one = weights_one[...].astype(BF16)
    plain_one = nt(eye, turned_one).astype(BF16)
    w1 = nt(plain_one, select).astype(BF16)
    w1_t = jnp.dot(select, turned_one, preferred_element_type=F32).astype(BF16)
    w2 = second_ref[...]
    w2_t = nt(eye, w2).astype(BF16)
    w3 = weights_three[...].astype(BF16)
    w3_t = nt(eye, w3).astype(BF16)

    turn_of = lax.bitwise_and(row * PATCH, LANES - 1)
    deep_r = lax.broadcasted_iota(jnp.int32, (56, 2 * HID), 0)
    deep_h = lax.broadcasted_iota(jnp.int32, (56, 2 * HID), 1)
    hid_h = lax.bitwise_and(deep_h, HID - 1)
    lands = lax.shift_right_logical(hid_h * PATCH, 7) + lax.shift_right_logical(deep_h, 7)
    gather_rows = jnp.where(lands == deep_r, 1.0, 0.0).astype(BF16)

    def halves(value):
        high = value.astype(BF16)
        return high, (value - high.astype(F32)).astype(BF16)

    def flatten_rows(value, exact):
        turned = []
        for m in range(HID // 8):
            tile = value[8 * m : 8 * m + 8]
            if (8 * m * PATCH) % LANES:
                tile = pltpu.roll(tile, (8 * m * PATCH) % LANES, 1)
            for _ in range(3):
                tile = pltpu.roll(tile, 0, 1, stride=PATCH // 3, stride_axis=0)
            turned.append(tile)
        value = jnp.concatenate(turned, axis=0)
        ahead = jnp.where(column >= turn_of, value, 0.0)
        behind = jnp.where(column < turn_of, value, 0.0)
        both = jnp.concatenate([ahead, behind], axis=0)
        if not exact:
            return jnp.dot(gather_rows, both.astype(BF16), preferred_element_type=F32)
        high, low = halves(both)
        return jnp.dot(gather_rows, high, preferred_element_type=F32) + jnp.dot(
            gather_rows, low, preferred_element_type=F32
        )

    base_params[0:56, :] = flatten_rows(plain_one.astype(F32), False)
    base_params[54:182, :] = w2.astype(F32)
    base_params[182:188, :] = output_ref[...].astype(F32)

    for t in range(TILES):
        own = jnp.zeros((8, LANES), F32)
        for first, end, j, part in segments(t):
            if part == "main" and HALO <= j < HALO + ROWS:
                own = jnp.where((lane >= first) & (lane < end), 1.0, own)
        own_ref[:, t * LANES : (t + 1) * LANES] = jnp.concatenate([own] * (HID // 8), axis=0).astype(BF16)

    mix_to = []
    mix_from = []
    for g in range(FIELDS):
        to_tile = jnp.zeros((8, LANES), F32)
        from_tile = jnp.zeros((8, LANES), F32)
        for f in range(FIELDS):
            to_tile = jnp.where(sub == f, mix_ref[f, g], to_tile)
            from_tile = jnp.where(sub == f, mix_ref[g, f], from_tile)
        mix_to.append(to_tile)
        mix_from.append(from_tile)

    pl.semaphore_wait(here_sem.at[0], told)
    told = tell(1, 2)

    def mixed(tiles, value):
        length = value.shape[1]
        total = None
        for g in range(FIELDS):
            term = spread_lanes(tiles[g], length) * jnp.broadcast_to(value[g : g + 1, :], (8, length))
            total = term if total is None else total + term
        return total

    pl.semaphore_wait(here_sem.at[1], told)
    told = tell(2, 4)
    all_halos = halo_copy(halo_in, halo_in, {"lon": east})
    all_halos.wait_recv()

    def top(value):
        return jnp.where(lat > 0, value, 0.0)

    def bottom(value):
        return jnp.where(lat < NLAT - 1, value, 0.0)

    blank = jnp.zeros((8, LANES), F32)
    sides = []
    for which in range(2):
        sides.append(
            {
                "left": (top(halo_in[12 + which]), halo_in[14 + which], bottom(halo_in[16 + which])),
                "right": (top(halo_in[18 + which]), halo_in[20 + which], bottom(halo_in[22 + which])),
            }
        )

    def source(which, j, part):
        if which == 1 and (j < 2 or j >= EXT - 2):
            return blank
        if part != "main":
            return sides[which][part][0 if j < HALO else 1 if j < HALO + ROWS else 2]
        if j < HALO:
            return top(halo_in[j if which == 0 else HALO + j - 2])
        if j < HALO + ROWS:
            return (own_a if which == 0 else own_b)[j - HALO]
        return bottom(halo_in[6 + (j - HALO - ROWS if which == 0 else j - ROWS)])

    for t in range(TILES):
        here = slice(t * LANES, (t + 1) * LANES)
        for which, target in ((0, flat_a), (1, flat_b)):
            value = blank
            for first, end, j, part in segments(t):
                piece = source(which, j, part)
                value = jnp.where((lane >= first) & (lane < end), piece, value)
            target[:, here] = value
            if which == 0:
                wide_mask[:, here] = jnp.broadcast_to(value[6:7, :], (8, LANES))
                wide_diff[:, here] = jnp.broadcast_to(value[7:8, :], (8, LANES))

    def shift(value, amount):
        return pltpu.roll(value, (-amount) % FLAT, 1)

    def make_patch(value, patch_ref):
        blocks = [value if (p, q) == (0, 0) else shift(value, p * PITCH + q) for p, q in offsets]
        for m in range(5):
            after = blocks[2 * m + 1] if m < 4 else jnp.zeros_like(value)
            patch_ref[16 * m : 16 * m + 16, :] = jnp.concatenate([blocks[2 * m], after], axis=0).astype(BF16)
        lap_ref[...] = blocks[1] + blocks[7] + blocks[3] + blocks[5] - 4.0 * value

    def forward(state_ref, patch_ref, one_ref, two_ref, next_ref, low, high, write_low, write_high):
        for start, size in chunks(low, high):
            here = slice(start, start + size)
            one = jnp.tanh(jnp.dot(w1, patch_ref[:, here], preferred_element_type=F32)).astype(BF16)
            one_ref[:, here] = one
            two = jnp.tanh(jnp.dot(w2, one, preferred_element_type=F32)).astype(BF16)
            two_ref[:, here] = two
            tendency = jnp.dot(w3, two, preferred_element_type=F32)[0:8]
            centre = state_ref[:, here]
            update = (
                centre
                + wide_diff[:, here] * lap_ref[:, here]
                + (mixed(mix_to, centre) + closure_dt * tendency)
            )
            next_ref[:, here] = wide_mask[:, here] * update

    make_patch(flat_a[...], patch_zero)
    low, high = tile_range(3)
    forward(flat_a, patch_zero, hid_one_zero, hid_two_zero, state_one, low, high, low, high)
    make_patch(state_one[...], patch_one)
    low, high = tile_range(2)
    forward(state_one, patch_one, hid_one_one, hid_two_one, state_two, low, high, low, high)

    def write_rows(source_ref, target_ref):
        for r in range(ROWS):
            start = (r + HALO) * PITCH + HALO
            t, turn = start // LANES, start % LANES
            before = source_ref[:, t * LANES : (t + 1) * LANES]
            after = source_ref[:, (t + 1) * LANES : (t + 2) * LANES]
            value = pltpu.roll(jnp.where(lane >= turn, before, after), (LANES - turn) % LANES, 1)
            target_ref[:, r, :] = value[0:FIELDS]

    grad_low, grad_high = tile_range(0)
    grad_here = slice(grad_low, grad_high)

    def backward(adj_ref, patch_ref, one_ref, two_ref, back_one, back_two, out_grad, low, high):
        for start, size in chunks(low, high):
            here = slice(start, start + size)
            masked = wide_mask[:, here] * adj_ref[:, here]
            low_grad = jnp.concatenate([closure_dt * masked, jnp.zeros_like(masked)], axis=0).astype(BF16)
            out_grad[:, here] = low_grad
            two = two_ref[:, here].astype(F32)
            grad_two = (
                jnp.dot(w3_t, low_grad, preferred_element_type=F32) * (1.0 - two * two)
            ).astype(BF16)
            back_two[:, here] = grad_two
            one = one_ref[:, here].astype(F32)
            grad_one = (
                jnp.dot(w2_t, grad_two, preferred_element_type=F32) * (1.0 - one * one)
            ).astype(BF16)
            back_one[:, here] = grad_one
            grad_zero = jnp.dot(w1_t, grad_one, preferred_element_type=F32)
            spread = wide_diff[:, here] * masked
            direct = masked + mixed(mix_from, masked) - 4.0 * spread
            for k in range(9):
                block = grad_zero[8 * k : 8 * k + 8]
                if k == 4:
                    block = block + direct
                elif k % 2:
                    block = block + spread
                patch_grad[8 * k : 8 * k + 8, here] = block

    def gradients(patch_ref, one_ref, two_ref, back_one, back_two, out_grad):
        own = own_ref[:, grad_here]
        grad_second = nt(back_two[:, grad_here], one_ref[:, grad_here] * own)
        grad_output = nt(out_grad[:, grad_here] * own[0:16], two_ref[:, grad_here])
        grad_first = nt(back_one[:, grad_here], patch_ref[:, grad_here] * own[0:DEEP])
        return grad_first, grad_second, grad_output

    def scatter():
        total = None
        for k, (p, q) in enumerate(offsets):
            block = patch_grad[8 * k : 8 * k + 8, :]
            if (p, q) != (0, 0):
                block = shift(block, -(p * PITCH + q))
            total = block if total is None else total + block
        return total

    low, high = tile_range(2)
    backward(
        flat_b, patch_one, hid_one_one, hid_two_one, late_one, late_two, late_out, low, high
    )
    adj_one[...] = scatter()
    late_first, late_second, late_output = gradients(patch_one, hid_one_one, hid_two_one, late_one, late_two, late_out)
    low, high = tile_range(1)
    backward(
        adj_one, patch_zero, hid_one_zero, hid_two_zero, back_one, back_two, out_grad, low, high
    )
    first, second, output = gradients(patch_zero, hid_one_zero, hid_two_zero, back_one, back_two, out_grad)
    first = first + late_first
    second = second + late_second
    output = output + late_output

    def copies_along(axis, here, steps, size, phase, source, target):
        made = []
        for place, d in enumerate(steps):
            peer = ring(here, d, size)
            made.append(
                pltpu.make_async_remote_copy(
                    src_ref=source(peer),
                    dst_ref=target(place),
                    send_sem=send_sem.at[phase],
                    recv_sem=recv_sem.at[phase],
                    device_id={axis: peer},
                    device_id_type=MESH,
                )
            )
        for copy in made:
            copy.start()

    def all_of(phase, buffer):
        return pltpu.make_async_remote_copy(
            src_ref=buffer,
            dst_ref=buffer,
            send_sem=send_sem.at[phase],
            recv_sem=recv_sem.at[phase],
            device_id={"lon": east},
            device_id_type=MESH,
        )

    core = lax.rem(lon, 2)
    chip = lax.div(lon, 2)
    twin = lon + 1 - 2 * core

    def twin_copy(phase, source, target):
        return pltpu.make_async_remote_copy(
            src_ref=source.at[1 - core],
            dst_ref=target,
            send_sem=send_sem.at[phase],
            recv_sem=recv_sem.at[phase],
            device_id={"lon": twin},
            device_id_type=MESH,
        )

    for c in range(CHUNKS):
        seconds[c % 2, c // 2] = second[16 * c : 16 * c + 16]
    twin_second = twin_copy(4, seconds, twin_seconds)
    twin_second.start()
    high_part, low_part = halves(first)
    narrow = jnp.dot(high_part, select, preferred_element_type=F32) + jnp.dot(
        low_part, select, preferred_element_type=F32
    )
    flat_first = flatten_rows(narrow, True)
    for c in range(CHUNKS):
        others[c % 2, c // 2] = flat_first[8 * c : 8 * c + 8] if c < CHUNKS - 1 else output[0:8]
    twin_other = twin_copy(5, others, twin_others)
    twin_other.start()
    twin_second.wait_recv()
    for m in range(CHUNKS // 2):
        grads[m, 0:16, :] = seconds[core, m] + twin_seconds[m]
    twin_other.wait_recv()
    for m in range(CHUNKS // 2):
        grads[m, 16:CHUNK, :] = others[core, m] + twin_others[m]
    pl.semaphore_wait(here_sem.at[2], told)
    copies_along(
        "lon", lon, CHIP_STEPS, NLON, 1,
        lambda peer: grads.at[lax.rem(lax.div(peer, 2), 4)], lambda place: recv_one.at[chip],
    )
    recv_one[chip] = grads[lax.rem(chip, 4)]

    write_rows(state_two, final_ref)
    adj_one[...] = scatter()
    write_rows(adj_one, adjoint_ref)

    scatters = all_of(1, recv_one.at[0 : NLON // 2 - 1])
    scatters.wait_recv()
    band = recv_one[0]
    for n in range(1, NLON // 2):
        band = band + recv_one[n]
    recv_two[lat] = band

    copies_along("lat", lat, LAT_STEPS, NLAT, 2, lambda peer: recv_two.at[lat], lambda place: recv_two.at[lat])
    exchanges = all_of(2, recv_two.at[0 : NLAT - 1])
    exchanges.wait_recv()
    total = recv_two[0]
    squares = total * total
    for b in range(1, NLAT):
        value = recv_two[b]
        total = total + value
        squares = squares + value * value
    mine = lax.rem(lon, CHUNKS)
    gathered[mine, 0:CHUNK, :] = total
    gathered[mine, CHUNK:SENT, :] = jnp.sum(squares, axis=0, keepdims=True)

    copies_along("lon", lon, NEAR_STEPS, NLON, 3, lambda peer: gathered.at[mine], lambda place: gathered.at[mine])
    loads[8].wait()
    collects = all_of(3, gathered.at[0 : CHUNKS - 1])
    collects.wait_recv()

    square_sum = jnp.zeros((CHUNK, LANES), F32)
    band_sum = jnp.zeros((1, LANES), F32)
    for c in range(CHUNKS):
        value = gathered[c, 0:CHUNK, :]
        square_sum = square_sum + value * value
        band_sum = band_sum + gathered[c, CHUNK:SENT, :]
        total_ref[54 + 16 * c : 70 + 16 * c, :] = value[0:16]
        if c < 6:
            total_ref[8 * c : 8 * c + 8, :] = value[16:24]
        elif c == 6:
            total_ref[48:54, :] = value[16:22]
        else:
            total_ref[182:188, :] = value[16:22]
    grad_square = jnp.sum(jnp.sum(square_sum, axis=0, keepdims=True), axis=1, keepdims=True)
    band_square = jnp.sum(band_sum, axis=1, keepdims=True)
    ratio_ref[...] = jnp.broadcast_to(band_square / (grad_square + epsilon), (1, LANES))
    scale = learn_rate / jnp.sqrt(jnp.broadcast_to(grad_square, (1, LANES)) / PARAMS + epsilon)
    params_ref[...] = base_params[0:188, :] - scale * total_ref[0:188, :] + noise_in[...]

    for copies in (all_halos, twin_second, twin_other, scatters, exchanges, collects):
        copies.wait_send()


def emit(final_in, adjoint_in, params_in, ratio_in, final_out, adjoint_out, params_out, ratio_out, held, sem):
    pairs = ((final_in, final_out), (adjoint_in, adjoint_out), (params_in, params_out))
    copies = [pltpu.make_async_copy(src, dst, sem.at[n]) for n, (src, dst) in enumerate(pairs)]
    for copy in copies:
        copy.start()
    held[0] = ratio_in[0, 0]
    copies.append(pltpu.make_async_copy(held, ratio_out, sem.at[3]))
    copies[3].start()
    for copy in copies:
        copy.wait()


def on_device(
    initial_state,
    diffusion,
    mixing,
    land_mask,
    first_layer,
    second_layer,
    output_layer,
    cotangent,
    update_noise,
):
    vmem = pltpu.VMEM
    flat8 = vmem((8, FLAT), F32)
    hidden = vmem((HID, FLAT), BF16)
    dma = pltpu.SemaphoreType.DMA
    scratch = [
        vmem((FIELDS, ROWS, COLS), F32),
        vmem((ROWS, COLS), F32),
        vmem((ROWS, COLS), jnp.int32),
        vmem((FIELDS, ROWS, COLS), F32),
        vmem((188, LANES), F32),
        pltpu.SMEM((FIELDS, FIELDS), F32),
        vmem((PATCH, HID), BF16),
        vmem((HID, HID), BF16),
        vmem((FIELDS, HID), BF16),
        dma((9,)),
        vmem((ROWS, 8, LANES), F32),
        vmem((ROWS, 8, LANES), F32),
        vmem((6, 8, LANES), F32),
        vmem((6, 8, LANES), F32),
        vmem((2, 8, LANES), F32),
        vmem((24, 8, LANES), F32),
        pltpu.SemaphoreType.REGULAR((3,)),
        dma((6,)),
        dma((6,)),
        flat8,
        flat8,
        hidden,
        flat8,
        flat8,
        flat8,
        flat8,
        flat8,
        vmem((DEEP, FLAT), BF16),
        vmem((DEEP, FLAT), BF16),
        hidden,
        hidden,
        hidden,
        hidden,
        hidden,
        hidden,
        vmem((16, FLAT), BF16),
        hidden,
        hidden,
        vmem((16, FLAT), BF16),
        vmem((72, FLAT), F32),
        flat8,
        vmem((HID, LANES), F32),
        vmem((16, LANES), F32),
        vmem((192, LANES), F32),
        vmem((2, CHUNKS // 2, 16, LANES), F32),
        vmem((2, CHUNKS // 2, 8, LANES), F32),
        vmem((CHUNKS // 2, 16, LANES), F32),
        vmem((CHUNKS // 2, 8, LANES), F32),
        vmem((CHUNKS // 2, CHUNK, LANES), F32),
        vmem((NLON // 2, CHUNK, LANES), F32),
        vmem((NLAT, CHUNK, LANES), F32),
        vmem((CHUNKS, SENT, LANES), F32),
        vmem((192, LANES), F32),
    ]
    hbm = pl.BlockSpec(memory_space=pltpu.HBM)
    local = pl.BlockSpec(memory_space=pltpu.VMEM)
    final, adjoint, params, ratio = pl.pallas_call(
        kernel,
        out_shape=(
            jax.ShapeDtypeStruct((FIELDS, ROWS, COLS), F32),
            jax.ShapeDtypeStruct((FIELDS, ROWS, COLS), F32),
            jax.ShapeDtypeStruct((188, LANES), F32),
            jax.ShapeDtypeStruct((1, LANES), F32),
        ),
        in_specs=[hbm] * 9,
        out_specs=(local,) * 4,
        scratch_shapes=scratch,
        compiler_params=pltpu.CompilerParams(
            collective_id=0, has_side_effects=True, vmem_limit_bytes=40 * 1024 * 1024
        ),
        name="ocean",
    )(
        *(
            pltpu.with_memory_space_constraint(value, pltpu.HBM)
            for value in (
                initial_state,
                diffusion,
                mixing,
                land_mask,
                first_layer.T,
                second_layer,
                output_layer,
                cotangent,
                update_noise.reshape(188, LANES),
            )
        )
    )
    final, adjoint, params, ratio = pl.pallas_call(
        emit,
        out_shape=(
            jax.ShapeDtypeStruct((FIELDS, ROWS, COLS), F32),
            jax.ShapeDtypeStruct((FIELDS, ROWS, COLS), F32),
            jax.ShapeDtypeStruct((188, LANES), F32),
            jax.ShapeDtypeStruct((1,), F32),
        ),
        in_specs=[local] * 4,
        out_specs=(hbm,) * 4,
        scratch_shapes=[pltpu.SMEM((1,), F32), dma((4,))],
        name="emit",
    )(*(pltpu.with_memory_space_constraint(value, pltpu.VMEM) for value in (final, adjoint, params, ratio)))
    return final, adjoint, params.reshape(PARAMS), ratio


def solution(mesh):
    placed = (
        P("ens", "lat", "lon"),
        P("lat", "lon"),
        P(),
        P("lat", "lon"),
        P(),
        P(),
        P(),
        P("ens", "lat", "lon"),
        P("ens"),
    )
    return jax.shard_map(
        on_device,
        mesh=mesh,
        in_specs=placed,
        out_specs=(P("ens", "lat", "lon"), P("ens", "lat", "lon"), P("ens"), P("ens")),
        check_vma=False,
    )
```
